128 devices in a mesh: seq: 8 (over y, core), tp: 16 (over x, z).
Axes of the slice: x: 4, y: 4, z: 4, core: 2. Of those that a mesh axis runs over, the one named last changes fastest.
Arguments:
- queries: bfloat16 [64, 8, 16, 128], P('tp'), may hold values from -10 to 10
- cache_kv: bfloat16 [64, 8, 2048, 256], P('tp', None, 'seq'), may hold values from -5 to 5
- new_kv: bfloat16 [64, 8, 256, 256], P('tp', None, 'seq'), may hold values from -5 to 5
- ctx_len: int32 [64], replicated, may hold values from 2 to 2048, as said below
- new_len: int32 [64], replicated, may hold values from 1 to 256, as said below
- owner: int32 [64], replicated, may hold values from 0 to 7, as said below
- wo: bfloat16 [16384, 16384], P(('seq', 'tp')), may hold values from -1 to 1
- hidden_in: bfloat16 [64, 16384], P(None, ('seq', 'tp')), may hold values from -3 to 3
- norm_gain: float32 [16384], P(('seq', 'tp')), may hold values from 0.5 to 1.5
Outputs:
- residual_out: bfloat16 [64, 16384], P(None, ('seq', 'tp'))
- normed: bfloat16 [64, 16384], P(None, ('seq', 'tp'))
- appended: bfloat16 [64, 8, 2048, 256], P('tp', None, 'seq')
The draws below stay inside these ranges and needn't reach their ends.
Inputs may be any that keep to these rules, and one draw needn't show every extreme that they name: `ctx_len`: some request reaches 2048. `new_len`: some request reaches 256. `owner`: every shard owns some request.
All inputs are finite; a program needn't handle non-finite values.
Results may differ from the reference program's by a relative error of at most 0.014.
Values may be sent and summed in bfloat16 or wider, within the bound.
A program may use at most 64 MiB of HBM per device.

```python
import jax
import jax.numpy as jnp
from jax import lax

D = 16384
KVH = 8
GROUP = 16
HD = 128
B = 64
CTX = 2048
BLOCK = 256
HQ = 128
N_SEQ = 8
N_TP = 16


def draw_queries(key, part):
    key = jax.random.fold_in(key, 1)
    first = jax.random.fold_in(key, 0)
    values = jnp.clip(jax.random.normal(first, (B, KVH, GROUP, HD), jnp.float32), -4.0, 4.0)
    return values.astype(jnp.bfloat16)


def draw_cache_kv(key, part):
    key = jax.random.fold_in(key, 2)
    first, second, third = jax.random.split(key, 3)
    offset = jax.random.uniform(third, (B, KVH, 1, HD), jnp.float32, -0.5, 0.5)
    keys = jnp.clip(jax.random.normal(first, (B, KVH, CTX, HD), jnp.float32), -4.0, 4.0)
    values = jnp.clip(jax.random.normal(second, (B, KVH, CTX, HD), jnp.float32), -4.0, 4.0)
    values = values + offset
    return jnp.concatenate([keys, values], axis=3).astype(jnp.bfloat16)


def draw_ctx_len(key, part):
    key = jax.random.fold_in(key, 3)
    first, second = jax.random.split(key)
    lengths = jax.random.randint(first, (B,), 2, CTX + 1)
    where_full = jax.random.randint(second, (), 0, B)
    return jnp.where(jnp.arange(B) == where_full, CTX, lengths).astype(jnp.int32)


def draw_new_len(key, part):
    key = jax.random.fold_in(key, 4)
    first, second = jax.random.split(key)
    lengths = jax.random.randint(first, (B,), 1, BLOCK + 1)
    where_full = jax.random.randint(second, (), 0, B)
    return jnp.where(jnp.arange(B) == where_full, BLOCK, lengths).astype(jnp.int32)


def draw_owner(key, part):
    key = jax.random.fold_in(key, 5)
    first, second, third = jax.random.split(key, 3)
    shards = jnp.minimum(jax.random.randint(first, (B,), 0, N_SEQ), jax.random.randint(second, (B,), 0, N_SEQ))
    order = jax.random.permutation(third, B)
    shards = shards.at[order[:N_SEQ]].set(jnp.arange(N_SEQ, dtype=jnp.int32))
    return shards.astype(jnp.int32)


def draw_wo(key, part):
    key = jax.random.fold_in(key, 7)
    first = jax.random.fold_in(key, 0)
    third = jax.random.fold_in(key, 2)
    total_rows = HQ * HD
    blocks = N_SEQ * N_TP
    factor = total_rows ** (-0.5)
    pairing = jax.random.permutation(third, blocks)
    row_block = jnp.arange(total_rows, dtype=jnp.int32) // (total_rows // blocks)
    col_block = jnp.arange(D, dtype=jnp.int32) // (D // blocks)
    boost = jnp.where(pairing[row_block][:, None] == col_block[None, :], 4.0, 1.0)
    values = jnp.clip(jax.random.normal(first, (total_rows, D), jnp.float32), -6.0, 6.0)
    return (values * boost * factor).astype(jnp.bfloat16)


def draw_hidden_in(key, part):
    key = jax.random.fold_in(key, 6)
    first = jax.random.fold_in(key, 0)
    ramp = 0.15 * (1.0 + 2.0 * jnp.arange(D, dtype=jnp.float32) / (D - 1))
    values = jnp.clip(jax.random.normal(first, (B, D), jnp.float32), -4.0, 4.0)
    return jnp.clip(values * ramp[None, :], -3.0, 3.0).astype(jnp.bfloat16)


def levels(rng, shape, pieces, low, high):
    level = 1.0
    for dim, blocks in pieces:
        steps = jax.random.uniform(jax.random.fold_in(jax.random.fold_in(rng, 6), dim), (blocks,), jnp.float32, low / len(pieces), high / len(pieces))
        level = level * jnp.repeat(jnp.exp(steps), shape[dim] // blocks).reshape((-1,) + (1,) * (len(shape) - 1 - dim))
    return level


def gaussian(own_key, shape, deviation, limit, cuts=(), held_as=jnp.bfloat16):
    loudness = levels(own_key, shape, cuts, -0.22, 0.18) if cuts else 1.0
    result = jax.random.normal(own_key, shape, jnp.float32) * deviation * loudness
    return jnp.minimum(jnp.maximum(result, -limit), limit).astype(held_as)


def setup_inputs(seed: int = 0) -> dict:
    splits = jax.random.split(jax.random.key(seed), 10)
    queries = draw_queries(jax.random.fold_in(splits[9], 71), 0)
    cache_kv = draw_cache_kv(jax.random.fold_in(splits[9], 71), 0)
    new_kv = gaussian(splits[2], (B, KVH, BLOCK, 2 * HD), 1.0, 5.0, ((0, 16), (2, 8)))
    ctx_len = draw_ctx_len(jax.random.fold_in(splits[9], 71), 0)
    new_len = draw_new_len(jax.random.fold_in(splits[9], 71), 0)
    owner = draw_owner(jax.random.fold_in(splits[9], 71), 0)
    wo = draw_wo(jax.random.fold_in(splits[9], 71), 0)
    hidden_in = draw_hidden_in(jax.random.fold_in(splits[9], 71), 0)
    norm_gain = jnp.clip(1.0 + 0.1 * jax.random.normal(splits[8], (D,), jnp.float32), 0.5, 1.5)
    return dict(queries=queries, cache_kv=cache_kv, new_kv=new_kv, ctx_len=ctx_len, new_len=new_len, owner=owner, wo=wo, hidden_in=hidden_in, norm_gain=norm_gain)


def one_request(args):
    query, cache_row, new_row, live_ctx, live_new = args
    keys = jnp.concatenate([cache_row[:, :, :HD], new_row[:, :, :HD]], axis=1).astype(jnp.float32)
    values = jnp.concatenate([cache_row[:, :, HD:], new_row[:, :, HD:]], axis=1).astype(jnp.float32)
    positions = jnp.arange(CTX + BLOCK, dtype=jnp.int32)
    valid = jnp.where(positions < CTX, positions < live_ctx, positions - CTX < live_new)
    scores = jnp.einsum('hgd,hpd->hgp', query.astype(jnp.float32), keys) * HD ** (-0.5)
    scores = jnp.where(valid[None, None, :], scores, -jnp.inf)
    weights = jax.nn.softmax(scores, axis=-1)
    context = jnp.einsum('hgp,hpd->hgd', weights, values)
    return context.astype(jnp.bfloat16)

def reference(queries, cache_kv, new_kv, ctx_len, new_len, owner, wo, hidden_in, norm_gain):
    context = lax.map(one_request, (queries, cache_kv, new_kv, ctx_len, new_len))
    flat = context.reshape(B, HQ * HD)
    attn = jnp.dot(flat, wo, preferred_element_type=jnp.float32)
    stream = hidden_in.astype(jnp.float32) + attn
    residual_out = stream.astype(jnp.bfloat16)
    mean_square = lax.optimization_barrier(jnp.mean(stream * stream, axis=1, keepdims=True))
    normed = (stream * lax.rsqrt(mean_square + 1e-05) * norm_gain[None, :]).astype(jnp.bfloat16)
    shard_ids = jnp.arange(N_SEQ, dtype=jnp.int32)
    slots = jnp.arange(BLOCK, dtype=jnp.int32)
    keep = (owner[:, None, None] == shard_ids[None, :, None]) & (slots[None, None, :] < new_len[:, None, None])
    stored = jnp.where(keep[:, None, :, :, None], new_kv[:, :, None, :, :], jnp.zeros((), jnp.bfloat16))
    appended = stored.reshape(B, KVH, N_SEQ * BLOCK, 2 * HD)
    return (residual_out, normed, appended)
```

```python
import functools

import jax
import jax.numpy as jnp
from jax import lax
from jax.experimental import pallas as pl
from jax.experimental.pallas import tpu as pltpu
from jax.sharding import PartitionSpec as P

D = 16384
HD = 128
KVH = 8
GROUP = 16
REQ = 4
WIDTH = 256
SHARE = 32
KEYS = WIDTH + SHARE
NEG = -1e30
MESH = pl.DeviceIdType.MESH


def remote(src, dst, send, recv, device):
    return pltpu.make_async_remote_copy(
        src_ref=src, dst_ref=dst, send_sem=send, recv_sem=recv, device_id=device, device_id_type=MESH
    )


def kernel(
    ctx_ref, new_ref, q_hbm, cache_hbm, newkv_hbm, wo_hbm, hidden_hbm, gain_hbm,
    res_ref, norm_ref, deliv_hbm,
    q_v, kv, w_v, hid_v, gain_v,
    osend, orecv, lsend, lrecv, csend, crecv,
    a_send, b_send, a_recv, b_recv, a2_send, b2_send, a2_recv, b2_recv,
    y_send, y_recv, n_send, n_recv, m_send, m_recv, rows_v,
    loc_sem, kv_sem, wl_sem, ws_sem, wr_sem,
    os_sem, or_sem, ls_sem, lr_sem, cs_sem, cr_sem,
    r1s_sem, r1r_sem, r2s_sem, r2r_sem, ys_sem, yr_sem,
    ns_sem, nr_sem, ms_sem, mr_sem,
    gs_sem, gr_sem, ps_sem, pr_sem, gl_sem,
):
    s = lax.axis_index("seq")
    t = lax.axis_index("tp")
    y, c = s // 2, s % 2
    x, z = t // 4, t % 4
    sp = y * 2 + (1 - c)

    def seq_peer(i):
        return lax.rem(s + 1 + i, 8)

    def tp_peer(i):
        return lax.rem(t + 1 + i, 16)

    def y_at(d):
        return lax.rem(y + d, 4) * 2 + c

    def x_at(d):
        return lax.rem(x + d, 4) * 4 + z

    def z_at(d):
        return x * 4 + lax.rem(z + d, 4)

    barrier = pltpu.get_barrier_semaphore()

    def greet_seq(i, _):
        pl.semaphore_signal(barrier, inc=1, device_id=(seq_peer(i), t), device_id_type=MESH)
        return 0

    def greet_tp(i, _):
        pl.semaphore_signal(barrier, inc=1, device_id=(s, tp_peer(i)), device_id_type=MESH)
        pl.semaphore_signal(barrier, inc=1, device_id=(sp, tp_peer(i)), device_id_type=MESH)
        return 0

    lax.fori_loop(0, 7, greet_seq, 0)
    lax.fori_loop(0, 15, greet_tp, 0)

    q_copy = pltpu.make_async_copy(q_hbm, q_v, loc_sem.at[0])
    h_copy = pltpu.make_async_copy(hidden_hbm, hid_v, loc_sem.at[1])
    g_copy = pltpu.make_async_copy(gain_hbm, gain_v, loc_sem.at[2])
    q_copy.start()

    def kv_copies(r):
        return (
            pltpu.make_async_copy(cache_hbm.at[r], kv.at[r, :, pl.ds(0, WIDTH), :], kv_sem.at[r, 0]),
            pltpu.make_async_copy(newkv_hbm.at[r], kv.at[r, :, pl.ds(WIDTH, SHARE), :], kv_sem.at[r, 1]),
        )

    for r in range(REQ):
        for copy in kv_copies(r):
            copy.start()
    h_copy.start()
    g_copy.start()

    def w_local(j):
        return pltpu.make_async_copy(
            wo_hbm.at[:, pl.ds(pl.multiple_of(j * 4096 + c * 2048, 2048), 2048)],
            w_v.at[j, pl.ds(pl.multiple_of(c * 128, 128), 128), :],
            wl_sem.at[j],
        )

    def w_remote(j):
        return remote(
            wo_hbm.at[:, pl.ds(pl.multiple_of(j * 4096 + (1 - c) * 2048, 2048), 2048)],
            w_v.at[j, pl.ds(pl.multiple_of(c * 128, 128), 128), :],
            ws_sem.at[j], wr_sem.at[j], (sp, t),
        )

    for j in range(4):
        w_local(j).start()

    def block(half, who):
        return deliv_hbm.at[pl.ds(half * 2, 2), :, pl.ds(pl.multiple_of(who * SHARE, SHARE), SHARE), :]

    own = [
        pltpu.make_async_copy(newkv_hbm.at[pl.ds(half * 2, 2)], block(half, s), gl_sem.at[half])
        for half in range(2)
    ]

    def ring(way, slot, src, dst):
        return remote(src, dst, gs_sem.at[way, slot], gr_sem.at[way, slot], (y_at(1 if way == 0 else 3), t))

    def first(way, order):
        half = order if way == 0 else 1 - order
        return ring(way, order, newkv_hbm.at[pl.ds(half * 2, 2)], block(half, s))

    def second(way):
        who = y_at(3) if way == 0 else y_at(1)
        return ring(way, 2, block(way, who), block(way, who))

    def pair(slot, src, half, who):
        return remote(src, block(half, who), ps_sem.at[slot], pr_sem.at[slot], (sp, t))

    def pair_own(half):
        return pair(half, newkv_hbm.at[pl.ds(half * 2, 2)], half, s)

    def pair_near(way, order):
        half = order if way == 0 else 1 - order
        who = y_at(3) if way == 0 else y_at(1)
        return pair(2 + way * 2 + order, block(half, who), half, who)

    def pair_far(way):
        return pair(6 + way, block(way, y_at(2)), way, y_at(2))

    pl.semaphore_wait(barrier, 37)

    for order in range(2):
        for way in range(2):
            first(way, order).start()
    for j in range(4):
        w_remote(j).start()
    for half in range(2):
        own[half].start()
        pair_own(half).start()

    q_copy.wait()
    col = lax.broadcasted_iota(jnp.int32, (GROUP, KEYS), 1)
    lane = lax.broadcasted_iota(jnp.int32, (GROUP, 128), 1)

    def attend(r, ls):
        for copy in kv_copies(r):
            copy.wait()
        live_ctx = jnp.minimum(ctx_ref[t * REQ + r] - s * WIDTH, WIDTH)
        live_new = new_ref[t * REQ + r] - s * SHARE + WIDTH
        mask = (col < live_ctx) | ((col >= WIDTH) & (col < live_new))
        for h in range(KVH):
            scores = lax.dot_general(
                q_v[r, h], kv[r, h, :, :HD], (((1,), (1,)), ((), ())), preferred_element_type=jnp.float32
            ) * HD ** (-0.5)
            scores = jnp.where(mask, scores, NEG)
            top = jnp.max(scores, axis=1, keepdims=True)
            weights = jnp.where(mask, jnp.exp(scores - top), 0.0)
            total = jnp.maximum(jnp.sum(weights, axis=1, keepdims=True), 1e-30)
            out = jnp.dot(weights.astype(jnp.bfloat16), kv[r, h, :, HD:], preferred_element_type=jnp.float32)
            osend[h, pl.ds(pl.multiple_of(r * GROUP, GROUP), GROUP), :] = (out / total).astype(jnp.bfloat16)
            ls = jnp.where(lane == h * REQ + r, top + jnp.log(total), ls)
        return ls

    lsend[...] = lax.fori_loop(0, REQ, attend, jnp.zeros((GROUP, 128), jnp.float32))

    def o_copy(k, slot):
        return remote(osend.at[k], orecv.at[slot], os_sem.at[k], or_sem.at[slot], (k, t))

    def l_copy(k, slot):
        return remote(lsend, lrecv.at[slot], ls_sem.at[k], lr_sem.at[slot], (k, t))

    def send_o(i, _):
        k = seq_peer(i)
        l_copy(k, s).start()
        o_copy(k, s).start()
        return 0

    lax.fori_loop(0, 7, send_o, 0)
    orecv[s] = osend[s]
    lrecv[s] = lsend[...]

    def wait_o(i, _):
        k = seq_peer(i)
        l_copy(k, k).wait_recv()
        o_copy(k, k).wait_recv()
        return 0

    lax.fori_loop(0, 7, wait_o, 0)
    shift = lax.rem(128 - s * REQ, 128)
    tops = [lrecv[k] for k in range(8)]
    top = functools.reduce(jnp.maximum, tops)
    exps = [jnp.exp(v - top) for v in tops]
    total = functools.reduce(jnp.add, exps)
    shares = [pltpu.roll(e / total, shift, 1) for e in exps]
    for r in range(REQ):
        context = jnp.zeros((GROUP, HD), jnp.float32)
        for k in range(8):
            part = orecv[k, r * GROUP:(r + 1) * GROUP, :].astype(jnp.float32)
            context = context + part * shares[k][:, r:r + 1]
        csend[pl.ds(r, GROUP, stride=8), :] = context
        csend[pl.ds(r + REQ, GROUP, stride=8), :] = context

    def c_copy(core, g, slot_core, slot_t):
        return remote(
            csend.at[pl.ds(pl.multiple_of(g * 8, 8), 8), :],
            crecv.at[slot_core, pl.ds(pl.multiple_of(slot_t * 8, 8), 8), :],
            cs_sem.at[core, g], cr_sem.at[slot_core, slot_t],
            (y * 2 + core, g),
        )

    def send_c(i, _):
        g = tp_peer(i)
        c_copy(c, g, c, t).start()
        c_copy(1 - c, g, c, t).start()
        return 0

    c_copy(1 - c, t, c, t).start()
    lax.fori_loop(0, 15, send_c, 0)
    crecv[c, pl.ds(pl.multiple_of(t * 8, 8), 8), :] = csend[pl.ds(pl.multiple_of(t * 8, 8), 8), :]

    for way in range(2):
        first(way, 0).wait_recv()
        second(way).start()
        pair_near(way, 0).start()

    def wait_c(i, _):
        g = tp_peer(i)
        c_copy(c, g, c, g).wait_recv()
        c_copy(1 - c, g, 1 - c, g).wait_recv()
        return 0

    for j in range(4):
        w_local(j).wait()
        w_remote(j).wait_recv()
    c_copy(1 - c, t, 1 - c, t).wait_recv()
    lax.fori_loop(0, 15, wait_c, 0)

    flat = jnp.concatenate(
        [
            jnp.concatenate([crecv[core, pl.ds(r, 16, stride=8), :] for r in range(REQ)], axis=0)
            for core in range(2)
        ],
        axis=1,
    ).astype(jnp.bfloat16)

    def r1_copy(way, d, part):
        dst = lax.rem((x if way == 0 else z) + d, 4)
        src = (a_send if way == 0 else b_send).at[dst, pl.ds(part * 2, 2)]
        to = (a_recv if way == 0 else b_recv).at[d - 1, pl.ds(part * 2, 2)]
        return remote(
            src, to, r1s_sem.at[way, d - 1, part], r1r_sem.at[way, d - 1, part],
            (s, x_at(d) if way == 0 else z_at(d)),
        )

    def project(j, _):
        for i in range(4):
            piece = jnp.dot(flat, w_v[j, :, i * 512:(i + 1) * 512], preferred_element_type=jnp.float32)
            piece = piece.astype(jnp.bfloat16)
            a_send[i, j] = piece[:32]
            for k in range(4):
                b_send[k, j, :, i * 128:(i + 1) * 128] = piece[32:, k * 128:(k + 1) * 128]
        return 0

    for part in range(2):
        lax.fori_loop(part * 2, part * 2 + 2, project, 0)
        for d in (2, 1, 3):
            for way in range(2):
                r1_copy(way, d, part).start()

    for way in range(2):
        first(way, 1).wait_recv()
        pair_near(way, 1).start()

    def r2_copy(way, d, part):
        dst = lax.rem((z if way == 0 else x) + d, 4)
        src = (a2_send if way == 0 else b2_send).at[dst, pl.ds(part * 2, 2)]
        to = (a2_recv if way == 0 else b2_recv).at[d - 1, pl.ds(part * 2, 2)]
        return remote(
            src, to, r2s_sem.at[way, d - 1, part], r2r_sem.at[way, d - 1, part],
            (s, z_at(d) if way == 0 else x_at(d)),
        )

    for part in range(2):
        for way in range(2):
            for d in (1, 3, 2):
                r1_copy(way, d, part).wait_recv()
            send, recv, nxt = ((a_send, a_recv, a2_send), (b_send, b_recv, b2_send))[way]
            mine = x if way == 0 else z

            def add(j, _):
                out = send[mine, j].astype(jnp.float32)
                for d in range(3):
                    out = out + recv[d, j].astype(jnp.float32)
                out = out.astype(jnp.bfloat16)
                for k in range(4):
                    nxt[k, j] = out[:, k * 128:(k + 1) * 128]
                return 0

            lax.fori_loop(part * 2, part * 2 + 2, add, 0)
            for d in (2, 1, 3):
                r2_copy(way, d, part).start()

    h_copy.wait()
    g_copy.wait()
    for part in range(2):
        for way in range(2):
            for d in (1, 3, 2):
                r2_copy(way, d, part).wait_recv()
            send, recv = ((a2_send, a2_recv), (b2_send, b2_recv))[way]
            mine = z if way == 0 else x
            for j in range(part * 2, part * 2 + 2):
                out = send[mine, j].astype(jnp.float32)
                for d in range(3):
                    out = out + recv[d, j].astype(jnp.float32)
                y_send[j, way * 32:(way + 1) * 32, :] = out.astype(jnp.bfloat16)

    def y_copy(d):
        dst = lax.rem(y + d, 4)
        return remote(y_send.at[dst], y_recv.at[d - 1], ys_sem.at[d - 1], yr_sem.at[d - 1], (y_at(d), t))

    for d in (2, 1, 3):
        y_copy(d).start()

    for way in range(2):
        second(way).wait_recv()
        pair_far(way).start()

    rows_v[...] = hid_v[...].astype(jnp.float32)
    stream = jnp.concatenate([rows_v[pl.ds(r, 16, stride=REQ), :] for r in range(REQ)], axis=0)
    stream = stream + y_send[y].astype(jnp.float32)
    for d in (1, 3, 2):
        y_copy(d).wait_recv()
    for d in range(3):
        stream = stream + y_recv[d].astype(jnp.float32)

    squares = stream * stream
    squares = jnp.sum(jnp.concatenate([squares, squares], axis=0).T, axis=0, keepdims=True)
    n_send[...] = jnp.broadcast_to(squares, (8, 128))

    def n_copy(k, slot):
        return remote(n_send, n_recv.at[slot], ns_sem.at[k], nr_sem.at[slot], (k, t))

    def m_copy(k, slot):
        return remote(m_send, m_recv.at[slot], ms_sem.at[k], mr_sem.at[slot], (s, k))

    def send_n(i, _):
        n_copy(seq_peer(i), s).start()
        return 0

    def wait_n(i, so_far):
        k = seq_peer(i)
        n_copy(k, k).wait_recv()
        return so_far + n_recv[k]

    lax.fori_loop(0, 7, send_n, 0)
    for r in range(REQ):
        rows_v[pl.ds(r, 16, stride=REQ), :] = stream[r * 16:(r + 1) * 16]
    res_ref[...] = rows_v[...].astype(jnp.bfloat16)
    m_send[...] = lax.fori_loop(0, 7, wait_n, n_send[...])

    def send_m(i, _):
        m_copy(tp_peer(i), t).start()
        return 0

    def wait_m(i, so_far):
        k = tp_peer(i)
        m_copy(k, k).wait_recv()
        return so_far + m_recv[k]

    lax.fori_loop(0, 15, send_m, 0)
    squares = lax.fori_loop(0, 15, wait_m, m_send[...])
    scale = lax.rsqrt(squares[:1] / D + 1e-05)
    scale = jnp.broadcast_to(scale, (128, 128)).T[:64]
    normed = stream * scale * gain_v[...]
    for r in range(REQ):
        rows_v[pl.ds(r, 16, stride=REQ), :] = normed[r * 16:(r + 1) * 16]
    norm_ref[...] = rows_v[...].astype(jnp.bfloat16)

    for half in range(2):
        own[half].wait()
        pair_own(half).wait()
        for way in range(2):
            first(way, half).wait_send()
            pair_near(way, half).wait()
    for way in range(2):
        second(way).wait_send()
        pair_far(way).wait()
    for j in range(4):
        w_remote(j).wait_send()

    def drain_seq(i, _):
        k = seq_peer(i)
        l_copy(k, s).wait_send()
        o_copy(k, s).wait_send()
        n_copy(k, s).wait_send()
        return 0

    def drain_tp(i, _):
        k = tp_peer(i)
        c_copy(c, k, c, t).wait_send()
        c_copy(1 - c, k, c, t).wait_send()
        m_copy(k, t).wait_send()
        return 0

    lax.fori_loop(0, 7, drain_seq, 0)
    lax.fori_loop(0, 15, drain_tp, 0)
    c_copy(1 - c, t, c, t).wait_send()
    for way in range(2):
        for d in range(1, 4):
            for part in range(2):
                r1_copy(way, d, part).wait_send()
                r2_copy(way, d, part).wait_send()
    for d in range(1, 4):
        y_copy(d).wait_send()


def step(queries, cache_kv, new_kv, ctx_len, new_len, wo, hidden_in, norm_gain):
    bf, f32 = jnp.bfloat16, jnp.float32
    dma = pltpu.SemaphoreType.DMA
    anywhere = pl.BlockSpec(memory_space=pl.ANY)
    vmem = pl.BlockSpec(memory_space=pltpu.VMEM)
    smem = pl.BlockSpec(memory_space=pltpu.SMEM)
    V = pltpu.VMEM
    return pl.pallas_call(
        kernel,
        out_shape=(
            jax.ShapeDtypeStruct((64, 128), bf),
            jax.ShapeDtypeStruct((64, 128), bf),
            jax.ShapeDtypeStruct((REQ, KVH, WIDTH, 256), bf),
        ),
        in_specs=[smem, smem] + [anywhere] * 6,
        out_specs=(vmem, vmem, anywhere),
        scratch_shapes=[
            V((REQ, KVH, GROUP, HD), bf),
            V((REQ, KVH, KEYS, 256), bf),
            V((4, 256, 2048), bf),
            V((64, 128), bf),
            V((1, 128), f32),
            V((8, 64, HD), bf), V((8, 64, HD), bf),
            V((GROUP, 128), f32), V((8, GROUP, 128), f32),
            V((128, HD), f32), V((2, 128, HD), f32),
            V((4, 4, 32, 512), bf), V((4, 4, 32, 512), bf),
            V((3, 4, 32, 512), bf), V((3, 4, 32, 512), bf),
            V((4, 4, 32, 128), bf), V((4, 4, 32, 128), bf),
            V((3, 4, 32, 128), bf), V((3, 4, 32, 128), bf),
            V((4, 64, 128), bf), V((3, 64, 128), bf),
            V((8, 128), f32), V((8, 8, 128), f32),
            V((8, 128), f32), V((16, 8, 128), f32),
            V((64, 128), f32),
            dma((3,)), dma((REQ, 2)), dma((4,)), dma((4,)), dma((4,)),
            dma((8,)), dma((8,)), dma((8,)), dma((8,)), dma((2, 16)), dma((2, 16)),
            dma((2, 3, 2)), dma((2, 3, 2)), dma((2, 3, 2)), dma((2, 3, 2)), dma((3,)), dma((3,)),
            dma((8,)), dma((8,)), dma((16,)), dma((16,)),
            dma((2, 3)), dma((2, 3)), dma((8,)), dma((8,)), dma((2,)),
        ],
        compiler_params=pltpu.CompilerParams(
            collective_id=0, has_side_effects=True, vmem_limit_bytes=40 * 1024 * 1024
        ),
        cost_estimate=pl.CostEstimate(flops=600_000_000, bytes_accessed=14_000_000, transcendentals=1_000_000),
    )(ctx_len, new_len, queries, cache_kv, new_kv, wo, hidden_in, norm_gain.reshape(1, 128))


def per_device(queries, cache_kv, new_kv, ctx_len, new_len, owner, wo, hidden_in, norm_gain):
    seq_index = lax.axis_index("seq")
    tp_index = lax.axis_index("tp")
    residual_out, normed, delivered = step(
        queries, cache_kv, new_kv, ctx_len, new_len, wo, hidden_in, norm_gain
    )
    my_new = lax.dynamic_slice_in_dim(new_len, tp_index * REQ, REQ)
    my_owner = lax.dynamic_slice_in_dim(owner, tp_index * REQ, REQ)
    slots = jnp.arange(WIDTH, dtype=jnp.int32)
    kept = (my_owner == seq_index)[:, None] & (slots[None, :] < my_new[:, None])
    appended = jnp.where(kept[:, None, :, None], delivered, jnp.zeros((), jnp.bfloat16))
    return (residual_out, normed, appended)


def solution(mesh):
    in_specs = (
        P("tp", None, None, None),
        P("tp", None, "seq", None),
        P("tp", None, "seq", None),
        P(),
        P(),
        P(),
        P(("seq", "tp"), None),
        P(None, ("seq", "tp")),
        P(("seq", "tp")),
    )
    out_specs = (P(None, ("seq", "tp")), P(None, ("seq", "tp")), P("tp", None, "seq", None))
    return jax.shard_map(
        per_device, mesh=mesh, in_specs=in_specs, out_specs=out_specs, check_vma=False
    )
```

```python
import functools

import jax
import jax.numpy as jnp
from jax import lax
from jax.experimental import pallas as pl
from jax.experimental.pallas import tpu as pltpu
from jax.sharding import PartitionSpec as P

D = 16384
HD = 128
KVH = 8
GROUP = 16
REQ = 4
WIDTH = 256
SHARE = 32
KEYS = WIDTH + SHARE
NEG = -1e30
MESH = pl.DeviceIdType.MESH


def remote(src, dst, send, recv, device):
    return pltpu.make_async_remote_copy(
        src_ref=src, dst_ref=dst, send_sem=send, recv_sem=recv, device_id=device, device_id_type=MESH
    )


def kernel(
    ctx_ref, new_ref, q_hbm, cache_hbm, newkv_hbm, wo_hbm, hidden_hbm, gain_hbm,
    res_ref, norm_ref, deliv_hbm,
    q_v, kv, w_v, hid_v, gain_v,
    osend, orecv, lsend, lrecv, csend, crecv,
    a_send, b_send, a_recv, b_recv, a2_send, b2_send, a2_recv, b2_recv,
    y_send, y_recv, n_send, n_recv, m_send, m_recv, rows_v,
    loc_sem, kv_sem, wl_sem, ws_sem, wr_sem,
    os_sem, or_sem, ls_sem, lr_sem, cs_sem, cr_sem,
    r1s_sem, r1r_sem, r2s_sem, r2r_sem, ys_sem, yr_sem,
    ns_sem, nr_sem, ms_sem, mr_sem,
    gs_sem, gr_sem, ps_sem, pr_sem, gl_sem,
):
    s = lax.axis_index("seq")
    t = lax.axis_index("tp")
    y, c = s // 2, s % 2
    x, z = t // 4, t % 4
    sp = y * 2 + (1 - c)

    def seq_peer(i):
        return lax.rem(s + 1 + i, 8)

    def tp_peer(i):
        return lax.rem(t + 1 + i, 16)

    def y_at(d):
        return lax.rem(y + d, 4) * 2 + c

    def x_at(d):
        return lax.rem(x + d, 4) * 4 + z

    def z_at(d):
        return x * 4 + lax.rem(z + d, 4)

    barrier = pltpu.get_barrier_semaphore()

    def greet_seq(i, _):
        pl.semaphore_signal(barrier, inc=1, device_id=(seq_peer(i), t), device_id_type=MESH)
        return 0

    def greet_tp(i, _):
        pl.semaphore_signal(barrier, inc=1, device_id=(s, tp_peer(i)), device_id_type=MESH)
        pl.semaphore_signal(barrier, inc=1, device_id=(sp, tp_peer(i)), device_id_type=MESH)
        return 0

    lax.fori_loop(0, 7, greet_seq, 0)
    lax.fori_loop(0, 15, greet_tp, 0)

    q_copy = pltpu.make_async_copy(q_hbm, q_v, loc_sem.at[0])
    h_copy = pltpu.make_async_copy(hidden_hbm, hid_v, loc_sem.at[1])
    g_copy = pltpu.make_async_copy(gain_hbm, gain_v, loc_sem.at[2])
    q_copy.start()

    def kv_copies(r):
        return (
            pltpu.make_async_copy(cache_hbm.at[r], kv.at[r, :, pl.ds(0, WIDTH), :], kv_sem.at[r, 0]),
            pltpu.make_async_copy(newkv_hbm.at[r], kv.at[r, :, pl.ds(WIDTH, SHARE), :], kv_sem.at[r, 1]),
        )

    for r in range(REQ):
        for copy in kv_copies(r):
            copy.start()
    h_copy.start()
    g_copy.start()

    def w_local(j):
        return pltpu.make_async_copy(
            wo_hbm.at[:, pl.ds(pl.multiple_of(j * 4096 + c * 2048, 2048), 2048)],
            w_v.at[j, pl.ds(pl.multiple_of(c * 128, 128), 128), :],
            wl_sem.at[j],
        )

    def w_remote(j):
        return remote(
            wo_hbm.at[:, pl.ds(pl.multiple_of(j * 4096 + (1 - c) * 2048, 2048), 2048)],
            w_v.at[j, pl.ds(pl.multiple_of(c * 128, 128), 128), :],
            ws_sem.at[j], wr_sem.at[j], (sp, t),
        )

    for j in range(4):
        w_local(j).start()

    def block(half, who):
        return deliv_hbm.at[pl.ds(half * 2, 2), :, pl.ds(pl.multiple_of(who * SHARE, SHARE), SHARE), :]

    own = [
        pltpu.make_async_copy(newkv_hbm.at[pl.ds(half * 2, 2)], block(half, s), gl_sem.at[half])
        for half in range(2)
    ]

    def ring(way, slot, src, dst):
        return remote(src, dst, gs_sem.at[way, slot], gr_sem.at[way, slot], (y_at(1 if way == 0 else 3), t))

    def first(way, order):
        half = order if way == 0 else 1 - order
        return ring(way, order, newkv_hbm.at[pl.ds(half * 2, 2)], block(half, s))

    def second(way):
        who = y_at(3) if way == 0 else y_at(1)
        return ring(way, 2, block(way, who), block(way, who))

    def pair(slot, src, half, who):
        return remote(src, block(half, who), ps_sem.at[slot], pr_sem.at[slot], (sp, t))

    def pair_own(half):
        return pair(half, newkv_hbm.at[pl.ds(half * 2, 2)], half, s)

    def pair_near(way, order):
        half = order if way == 0 else 1 - order
        who = y_at(3) if way == 0 else y_at(1)
        return pair(2 + way * 2 + order, block(half, who), half, who)

    def pair_far(way):
        return pair(6 + way, block(way, y_at(2)), way, y_at(2))

    pl.semaphore_wait(barrier, 37)

    for order in range(2):
        for way in range(2):
            first(way, order).start()
    for j in range(4):
        w_remote(j).start()
    for half in range(2):
        own[half].start()
        pair_own(half).start()

    q_copy.wait()
    col = lax.broadcasted_iota(jnp.int32, (GROUP, KEYS), 1)
    lane = lax.broadcasted_iota(jnp.int32, (GROUP, 128), 1)

    def attend(r, ls):
        for copy in kv_copies(r):
            copy.wait()
        live_ctx = jnp.minimum(ctx_ref[t * REQ + r] - s * WIDTH, WIDTH)
        live_new = new_ref[t * REQ + r] - s * SHARE + WIDTH
        mask = (col < live_ctx) | ((col >= WIDTH) & (col < live_new))
        for h in range(KVH):
            scores = lax.dot_general(
                q_v[r, h], kv[r, h, :, :HD], (((1,), (1,)), ((), ())), preferred_element_type=jnp.float32
            ) * HD ** (-0.5)
            scores = jnp.where(mask, scores, NEG)
            top = jnp.max(scores, axis=1, keepdims=True)
            weights = jnp.where(mask, jnp.exp(scores - top), 0.0)
            total = jnp.maximum(jnp.sum(weights, axis=1, keepdims=True), 1e-30)
            out = jnp.dot(weights.astype(jnp.bfloat16), kv[r, h, :, HD:], preferred_element_type=jnp.float32)
            osend[h, pl.ds(pl.multiple_of(r * GROUP, GROUP), GROUP), :] = (out / total).astype(jnp.bfloat16)
            ls = jnp.where(lane == h * REQ + r, top + jnp.log(total), ls)
        return ls

    lsend[...] = lax.fori_loop(0, REQ, attend, jnp.zeros((GROUP, 128), jnp.float32))

    def o_copy(k, slot):
        return remote(osend.at[k], orecv.at[slot], os_sem.at[k], or_sem.at[slot], (k, t))

    def l_copy(k, slot):
        return remote(lsend, lrecv.at[slot], ls_sem.at[k], lr_sem.at[slot], (k, t))

    def send_o(i, _):
        k = seq_peer(i)
        l_copy(k, s).start()
        o_copy(k, s).start()
        return 0

    lax.fori_loop(0, 7, send_o, 0)
    orecv[s] = osend[s]
    lrecv[s] = lsend[...]

    def wait_o(i, _):
        k = seq_peer(i)
        l_copy(k, k).wait_recv()
        o_copy(k, k).wait_recv()
        return 0

    lax.fori_loop(0, 7, wait_o, 0)
    shift = lax.rem(128 - s * REQ, 128)
    tops = [lrecv[k] for k in range(8)]
    top = functools.reduce(jnp.maximum, tops)
    exps = [jnp.exp(v - top) for v in tops]
    total = functools.reduce(jnp.add, exps)
    shares = [pltpu.roll(e / total, shift, 1) for e in exps]
    for r in range(REQ):
        context = jnp.zeros((GROUP, HD), jnp.float32)
        for k in range(8):
            part = orecv[k, r * GROUP:(r + 1) * GROUP, :].astype(jnp.float32)
            context = context + part * shares[k][:, r:r + 1]
        csend[pl.ds(r, GROUP, stride=8), :] = context
        csend[pl.ds(r + REQ, GROUP, stride=8), :] = context

    def c_copy(core, g, slot_core, slot_t):
        return remote(
            csend.at[pl.ds(pl.multiple_of(g * 8, 8), 8), :],
            crecv.at[slot_core, pl.ds(pl.multiple_of(slot_t * 8, 8), 8), :],
            cs_sem.at[core, g], cr_sem.at[slot_core, slot_t],
            (y * 2 + core, g),
        )

    def send_c(i, _):
        g = tp_peer(i)
        c_copy(c, g, c, t).start()
        c_copy(1 - c, g, c, t).start()
        return 0

    c_copy(1 - c, t, c, t).start()
    lax.fori_loop(0, 15, send_c, 0)
    crecv[c, pl.ds(pl.multiple_of(t * 8, 8), 8), :] = csend[pl.ds(pl.multiple_of(t * 8, 8), 8), :]

    for way in range(2):
        first(way, 0).wait_recv()
        second(way).start()
        pair_near(way, 0).start()

    def wait_c(i, _):
        g = tp_peer(i)
        c_copy(c, g, c, g).wait_recv()
        c_copy(1 - c, g, 1 - c, g).wait_recv()
        return 0

    for j in range(4):
        w_local(j).wait()
        w_remote(j).wait_recv()
    c_copy(1 - c, t, 1 - c, t).wait_recv()
    lax.fori_loop(0, 15, wait_c, 0)

    flat = jnp.concatenate(
        [
            jnp.concatenate([crecv[core, pl.ds(r, 16, stride=8), :] for r in range(REQ)], axis=0)
            for core in range(2)
        ],
        axis=1,
    ).astype(jnp.bfloat16)

    def r1_copy(way, d, part):
        dst = lax.rem((x if way == 0 else z) + d, 4)
        src = (a_send if way == 0 else b_send).at[dst, pl.ds(part * 2, 2)]
        to = (a_recv if way == 0 else b_recv).at[d - 1, pl.ds(part * 2, 2)]
        return remote(
            src, to, r1s_sem.at[way, d - 1, part], r1r_sem.at[way, d - 1, part],
            (s, x_at(d) if way == 0 else z_at(d)),
        )

    def project(j, _):
        for i in range(4):
            piece = jnp.dot(flat, w_v[j, :, i * 512:(i + 1) * 512], preferred_element_type=jnp.float32)
            piece = piece.astype(jnp.bfloat16)
            a_send[i, j] = piece[:32]
            for k in range(4):
                b_send[k, j, :, i * 128:(i + 1) * 128] = piece[32:, k * 128:(k + 1) * 128]
        return 0

    for part in range(2):
        lax.fori_loop(part * 2, part * 2 + 2, project, 0)
        for d in (2, 1, 3):
            for way in range(2):
                r1_copy(way, d, part).start()

    for way in range(2):
        first(way, 1).wait_recv()
        pair_near(way, 1).start()

    def r2_copy(way, d, part):
        dst = lax.rem((z if way == 0 else x) + d, 4)
        src = (a2_send if way == 0 else b2_send).at[dst, pl.ds(part * 2, 2)]
        to = (a2_recv if way == 0 else b2_recv).at[d - 1, pl.ds(part * 2, 2)]
        return remote(
            src, to, r2s_sem.at[way, d - 1, part], r2r_sem.at[way, d - 1, part],
            (s, z_at(d) if way == 0 else x_at(d)),
        )

    for part in range(2):
        for way in range(2):
            for d in (1, 3, 2):
                r1_copy(way, d, part).wait_recv()
            send, recv, nxt = ((a_send, a_recv, a2_send), (b_send, b_recv, b2_send))[way]
            mine = x if way == 0 else z

            def add(j, _):
                out = send[mine, j].astype(jnp.float32)
                for d in range(3):
                    out = out + recv[d, j].astype(jnp.float32)
                out = out.astype(jnp.bfloat16)
                for k in range(4):
                    nxt[k, j] = out[:, k * 128:(k + 1) * 128]
                return 0

            lax.fori_loop(part * 2, part * 2 + 2, add, 0)
            for d in (2, 1, 3):
                r2_copy(way, d, part).start()

    h_copy.wait()
    g_copy.wait()
    for part in range(2):
        for way in range(2):
            for d in (1, 3, 2):
                r2_copy(way, d, part).wait_recv()
            send, recv = ((a2_send, a2_recv), (b2_send, b2_recv))[way]
            mine = z if way == 0 else x
            for j in range(part * 2, part * 2 + 2):
                out = send[mine, j].astype(jnp.float32)
                for d in range(3):
                    out = out + recv[d, j].astype(jnp.float32)
                y_send[j, way * 32:(way + 1) * 32, :] = out.astype(jnp.bfloat16)

    def y_copy(d):
        dst = lax.rem(y + d, 4)
        return remote(y_send.at[dst], y_recv.at[d - 1], ys_sem.at[d - 1], yr_sem.at[d - 1], (y_at(d), t))

    for d in (2, 1, 3):
        y_copy(d).start()

    for way in range(2):
        second(way).wait_recv()
        pair_far(way).start()

    rows_v[...] = hid_v[...].astype(jnp.float32)
    stream = jnp.concatenate([rows_v[pl.ds(r, 16, stride=REQ), :] for r in range(REQ)], axis=0)
    stream = stream + y_send[y].astype(jnp.float32)
    for d in (1, 3, 2):
        y_copy(d).wait_recv()
    for d in range(3):
        stream = stream + y_recv[d].astype(jnp.float32)

    squares = stream * stream
    squares = jnp.sum(jnp.concatenate([squares, squares], axis=0).T, axis=0, keepdims=True)
    n_send[...] = jnp.broadcast_to(squares, (8, 128))

    def n_copy(k, slot):
        return remote(n_send, n_recv.at[slot], ns_sem.at[k], nr_sem.at[slot], (k, t))

    def m_copy(k, slot):
        return remote(m_send, m_recv.at[slot], ms_sem.at[k], mr_sem.at[slot], (s, k))

    def send_n(i, _):
        n_copy(seq_peer(i), s).start()
        return 0

    def wait_n(i, so_far):
        k = seq_peer(i)
        n_copy(k, k).wait_recv()
        return so_far + n_recv[k]

    lax.fori_loop(0, 7, send_n, 0)
    for r in range(REQ):
        rows_v[pl.ds(r, 16, stride=REQ), :] = stream[r * 16:(r + 1) * 16]
    res_ref[...] = rows_v[...].astype(jnp.bfloat16)
    m_send[...] = lax.fori_loop(0, 7, wait_n, n_send[...])

    def send_m(i, _):
        m_copy(tp_peer(i), t).start()
        return 0

    def wait_m(i, so_far):
        k = tp_peer(i)
        m_copy(k, k).wait_recv()
        return so_far + m_recv[k]

    lax.fori_loop(0, 15, send_m, 0)
    squares = lax.fori_loop(0, 15, wait_m, m_send[...])
    scale = lax.rsqrt(squares[:1] / D + 1e-05)
    scale = jnp.broadcast_to(scale, (128, 128)).T[:64]
    normed = stream * scale * gain_v[...]
    for r in range(REQ):
        rows_v[pl.ds(r, 16, stride=REQ), :] = normed[r * 16:(r + 1) * 16]
    norm_ref[...] = rows_v[...].astype(jnp.bfloat16)

    for half in range(2):
        own[half].wait()
        pair_own(half).wait()
        for way in range(2):
            first(way, half).wait_send()
            pair_near(way, half).wait()
    for way in range(2):
        second(way).wait_send()
        pair_far(way).wait()
    for j in range(4):
        w_remote(j).wait_send()

    def drain_seq(i, _):
        k = seq_peer(i)
        l_copy(k, s).wait_send()
        o_copy(k, s).wait_send()
        n_copy(k, s).wait_send()
        return 0

    def drain_tp(i, _):
        k = tp_peer(i)
        c_copy(c, k, c, t).wait_send()
        c_copy(1 - c, k, c, t).wait_send()
        m_copy(k, t).wait_send()
        return 0

    lax.fori_loop(0, 7, drain_seq, 0)
    lax.fori_loop(0, 15, drain_tp, 0)
    c_copy(1 - c, t, c, t).wait_send()
    for way in range(2):
        for d in range(1, 4):
            for part in range(2):
                r1_copy(way, d, part).wait_send()
                r2_copy(way, d, part).wait_send()
    for d in range(1, 4):
        y_copy(d).wait_send()


def step(queries, cache_kv, new_kv, ctx_len, new_len, wo, hidden_in, norm_gain):
    bf, f32 = jnp.bfloat16, jnp.float32
    dma = pltpu.SemaphoreType.DMA
    anywhere = pl.BlockSpec(memory_space=pl.ANY)
    vmem = pl.BlockSpec(memory_space=pltpu.VMEM)
    smem = pl.BlockSpec(memory_space=pltpu.SMEM)
    V = pltpu.VMEM
    return pl.pallas_call(
        kernel,
        out_shape=(
            jax.ShapeDtypeStruct((64, 128), bf),
            jax.ShapeDtypeStruct((64, 128), bf),
            jax.ShapeDtypeStruct((REQ, KVH, WIDTH, 256), bf),
        ),
        in_specs=[smem, smem] + [anywhere] * 6,
        out_specs=(vmem, vmem, anywhere),
        scratch_shapes=[
            V((REQ, KVH, GROUP, HD), bf),
            V((REQ, KVH, KEYS, 256), bf),
            V((4, 256, 2048), bf),
            V((64, 128), bf),
            V((1, 128), f32),
            V((8, 64, HD), bf), V((8, 64, HD), bf),
            V((GROUP, 128), f32), V((8, GROUP, 128), f32),
            V((128, HD), f32), V((2, 128, HD), f32),
            V((4, 4, 32, 512), bf), V((4, 4, 32, 512), bf),
            V((3, 4, 32, 512), bf), V((3, 4, 32, 512), bf),
            V((4, 4, 32, 128), bf), V((4, 4, 32, 128), bf),
            V((3, 4, 32, 128), bf), V((3, 4, 32, 128), bf),
            V((4, 64, 128), bf), V((3, 64, 128), bf),
            V((8, 128), f32), V((8, 8, 128), f32),
            V((8, 128), f32), V((16, 8, 128), f32),
            V((64, 128), f32),
            dma((3,)), dma((REQ, 2)), dma((4,)), dma((4,)), dma((4,)),
            dma((8,)), dma((8,)), dma((8,)), dma((8,)), dma((2, 16)), dma((2, 16)),
            dma((2, 3, 2)), dma((2, 3, 2)), dma((2, 3, 2)), dma((2, 3, 2)), dma((3,)), dma((3,)),
            dma((8,)), dma((8,)), dma((16,)), dma((16,)),
            dma((2, 3)), dma((2, 3)), dma((8,)), dma((8,)), dma((2,)),
        ],
        compiler_params=pltpu.CompilerParams(
            collective_id=0, has_side_effects=True, vmem_limit_bytes=62 * 1024 * 1024
        ),
        cost_estimate=pl.CostEstimate(flops=600_000_000, bytes_accessed=14_000_000, transcendentals=1_000_000),
    )(ctx_len, new_len, queries, cache_kv, new_kv, wo, hidden_in, norm_gain.reshape(1, 128))


def store_kernel(owner_ref, new_ref, res_in, norm_in, deliv_hbm, res_ref, norm_ref, app_hbm, zeros, held, out_sem, in_sem):
    s = lax.axis_index("seq")
    t = lax.axis_index("tp")

    def blank(r, i):
        return pltpu.make_async_copy(zeros, app_hbm.at[r, pl.ds(i * 2, 2)], out_sem.at[r, i])

    def fetch(r):
        return pltpu.make_async_copy(deliv_hbm.at[r], held.at[r], in_sem.at[r])

    def put(r):
        return pltpu.make_async_copy(held.at[r], app_hbm.at[r], in_sem.at[r])

    zeros[...] = jnp.zeros_like(zeros)
    for r in range(REQ):
        mine = owner_ref[t * REQ + r] == s

        @pl.when(mine)
        def _():
            fetch(r).start()

        @pl.when(jnp.logical_not(mine))
        def _():
            for i in range(4):
                blank(r, i).start()

    res_ref[...] = res_in[...]
    norm_ref[...] = norm_in[...]
    slot = lax.broadcasted_iota(jnp.int32, (WIDTH, 256), 0)
    for r in range(REQ):
        @pl.when(owner_ref[t * REQ + r] == s)
        def _():
            fetch(r).wait()
            live = slot < new_ref[t * REQ + r]
            for h in range(KVH):
                held[r, h] = jnp.where(live, held[r, h], jnp.zeros((), jnp.bfloat16))
            put(r).start()

    for r in range(REQ):
        mine = owner_ref[t * REQ + r] == s

        @pl.when(mine)
        def _():
            put(r).wait()

        @pl.when(jnp.logical_not(mine))
        def _():
            for i in range(4):
                blank(r, i).wait()


def store(owner, new_len, residual_out, normed, delivered):
    anywhere = pl.BlockSpec(memory_space=pl.ANY)
    vmem = pl.BlockSpec(memory_space=pltpu.VMEM)
    smem = pl.BlockSpec(memory_space=pltpu.SMEM)
    return pl.pallas_call(
        store_kernel,
        out_shape=tuple(jax.ShapeDtypeStruct(v.shape, v.dtype) for v in (residual_out, normed, delivered)),
        in_specs=[smem, smem, vmem, vmem, anywhere],
        out_specs=(vmem, vmem, anywhere),
        scratch_shapes=[
            pltpu.VMEM((2, WIDTH, 256), jnp.bfloat16),
            pltpu.VMEM((REQ, KVH, WIDTH, 256), jnp.bfloat16),
            pltpu.SemaphoreType.DMA((REQ, 4)),
            pltpu.SemaphoreType.DMA((REQ,)),
        ],
        compiler_params=pltpu.CompilerParams(vmem_limit_bytes=62 * 1024 * 1024),
        cost_estimate=pl.CostEstimate(flops=0, bytes_accessed=6_000_000, transcendentals=0),
    )(owner, new_len, residual_out, normed, delivered)


def per_device(queries, cache_kv, new_kv, ctx_len, new_len, owner, wo, hidden_in, norm_gain):
    residual_out, normed, delivered = step(
        queries, cache_kv, new_kv, ctx_len, new_len, wo, hidden_in, norm_gain
    )
    return store(owner, new_len, residual_out, normed, delivered)


def solution(mesh):
    in_specs = (
        P("tp", None, None, None),
        P("tp", None, "seq", None),
        P("tp", None, "seq", None),
        P(),
        P(),
        P(),
        P(("seq", "tp"), None),
        P(None, ("seq", "tp")),
        P(("seq", "tp")),
    )
    out_specs = (P(None, ("seq", "tp")), P(None, ("seq", "tp")), P("tp", None, "seq", None))
    return jax.shard_map(
        per_device, mesh=mesh, in_specs=in_specs, out_specs=out_specs, check_vma=False
    )
```

```python
import functools

import jax
import jax.numpy as jnp
from jax import lax
from jax.experimental import pallas as pl
from jax.experimental.pallas import tpu as pltpu
from jax.sharding import PartitionSpec as P

D = 16384
HD = 128
KVH = 8
GROUP = 16
REQ = 4
WIDTH = 256
SHARE = 32
KEYS = WIDTH + SHARE
NEG = -1e30
MESH = pl.DeviceIdType.MESH


def remote(src, dst, send, recv, device):
    return pltpu.make_async_remote_copy(
        src_ref=src, dst_ref=dst, send_sem=send, recv_sem=recv, device_id=device, device_id_type=MESH
    )


def kernel(
    ctx_hbm, new_hbm, q_hbm, cache_hbm, newkv_hbm, wo_hbm, hidden_hbm, gain_hbm,
    res_hbm, norm_hbm, deliv_hbm,
    ctx_s, new_s, q_v, kv, fresh, w_v, hid_v, gain_v,
    osend, orecv, csend, crecv,
    a_send, b_send, a_recv, b_recv, a2_send, b2_send, a2_recv, b2_recv,
    n_send, n_recv, rows_v, res_v, norm_v,
    loc_sem, out_sem, kv_sem, wl_sem, ws_sem, wr_sem,
    os_sem, or_sem, cs_sem, cr_sem,
    r1s_sem, r1r_sem, r2s_sem, r2r_sem, ns_sem, nr_sem,
    gs_sem, gr_sem, ps_sem, pr_sem, gl_sem,
):
    s = lax.axis_index("seq")
    t = lax.axis_index("tp")
    y, c = s // 2, s % 2
    x, z = t // 4, t % 4
    me = s * 16 + t
    sp = y * 2 + (1 - c)

    def seq_peer(i):
        return lax.rem(s + 1 + i, 8)

    def tp_peer(i):
        return lax.rem(t + 1 + i, 16)

    def any_peer(i):
        k = lax.rem(me + 1 + i, 128)
        return k // 16, lax.rem(k, 16)

    def y_at(d):
        return lax.rem(y + d, 4) * 2 + c

    def x_at(d):
        return lax.rem(x + d, 4) * 4 + z

    def z_at(d):
        return x * 4 + lax.rem(z + d, 4)

    drains = []

    loads = [
        pltpu.make_async_copy(src, dst, loc_sem.at[i])
        for i, (src, dst) in enumerate(
            [(ctx_hbm, ctx_s), (new_hbm, new_s), (q_hbm, q_v), (hidden_hbm, hid_v), (gain_hbm, gain_v)]
        )
    ]

    def kv_copies(r):
        return (
            pltpu.make_async_copy(cache_hbm.at[r], kv.at[r, :, pl.ds(0, WIDTH), :], kv_sem.at[r, 0]),
            pltpu.make_async_copy(newkv_hbm.at[r], kv.at[r, :, pl.ds(WIDTH, SHARE), :], kv_sem.at[r, 1]),
        )

    for load in loads[:3]:
        load.start()
    for r in range(REQ):
        for copy in kv_copies(r):
            copy.start()
    for load in loads[3:]:
        load.start()

    barrier = pltpu.get_barrier_semaphore()

    def greet(i, _):
        pl.semaphore_signal(barrier, inc=1, device_id=any_peer(i), device_id_type=MESH)
        return 0

    lax.fori_loop(0, 127, greet, 0)

    def w_local(j):
        return pltpu.make_async_copy(
            wo_hbm.at[:, pl.ds(pl.multiple_of(j * 4096 + c * 2048, 2048), 2048)],
            w_v.at[j, pl.ds(pl.multiple_of(c * 128, 128), 128), :],
            wl_sem.at[j],
        )

    def w_remote(j):
        return remote(
            wo_hbm.at[:, pl.ds(pl.multiple_of(j * 4096 + (1 - c) * 2048, 2048), 2048)],
            w_v.at[j, pl.ds(pl.multiple_of(c * 128, 128), 128), :],
            ws_sem.at[j], wr_sem.at[j], (sp, t),
        )

    for j in range(4):
        w_local(j).start()

    def block(half, who):
        return deliv_hbm.at[pl.ds(half * 2, 2), :, pl.ds(pl.multiple_of(who * SHARE, SHARE), SHARE), :]

    own = [
        pltpu.make_async_copy(fresh.at[pl.ds(half * 2, 2)], block(half, s), gl_sem.at[half])
        for half in range(2)
    ]

    def ring(way, slot, src, dst):
        return remote(src, dst, gs_sem.at[way, slot], gr_sem.at[way, slot], (y_at(1 if way == 0 else 3), t))

    def first(way, order):
        half = order if way == 0 else 1 - order
        return ring(way, order, fresh.at[pl.ds(half * 2, 2)], block(half, s))

    def second(way):
        who = y_at(3) if way == 0 else y_at(1)
        return ring(way, 2, block(way, who), block(way, who))

    def pair(slot, src, half, who):
        return remote(src, block(half, who), ps_sem.at[slot], pr_sem.at[slot], (sp, t))

    def pair_own(half):
        return pair(half, fresh.at[pl.ds(half * 2, 2)], half, s)

    def pair_near(way, order):
        half = order if way == 0 else 1 - order
        who = y_at(3) if way == 0 else y_at(1)
        return pair(2 + way * 2 + order, block(half, who), half, who)

    def pair_far(way):
        return pair(6 + way, block(way, y_at(2)), way, y_at(2))

    col = lax.broadcasted_iota(jnp.int32, (KVH * GROUP, KEYS), 1)
    lane = lax.broadcasted_iota(jnp.int32, (KVH * GROUP, 128), 1)

    def attend(r, stats):
        for copy in kv_copies(r):
            copy.wait()
        live_ctx = jnp.minimum(ctx_s[t * REQ + r] - s * WIDTH, WIDTH)
        live_new = new_s[t * REQ + r] - s * SHARE + WIDTH
        mask = (col < live_ctx) | ((col >= WIDTH) & (col < live_new))
        scores = jnp.concatenate(
            [
                lax.dot_general(
                    q_v[r, h], kv[r, h, :, :HD], (((1,), (1,)), ((), ())), preferred_element_type=jnp.float32
                )
                for h in range(KVH)
            ],
            axis=0,
        ) * HD ** (-0.5)
        scores = jnp.where(mask, scores, NEG)
        top = jnp.max(scores, axis=1, keepdims=True)
        weights = jnp.where(mask, jnp.exp(scores - top), 0.0)
        total = jnp.maximum(jnp.sum(weights, axis=1, keepdims=True), 1e-30)
        weights = weights.astype(jnp.bfloat16)
        inverse = 1.0 / total
        for h in range(KVH):
            rows = slice(h * GROUP, (h + 1) * GROUP)
            out = jnp.dot(weights[rows], kv[r, h, :, HD:], preferred_element_type=jnp.float32)
            osend[h, r * GROUP:(r + 1) * GROUP, :] = (out * inverse[rows]).astype(jnp.bfloat16)
        return jnp.where(lane == r, top + jnp.log(total), stats)

    def rows_of(part):
        return pl.ds(0, 32) if part == 0 else pl.ds(32, 48)

    def o_copy(k, part):
        return remote(
            osend.at[k, rows_of(part)], orecv.at[s, rows_of(part)], os_sem.at[part], or_sem.at[part], (k, t)
        )

    def o_own(part):
        return pltpu.make_async_copy(
            osend.at[s, rows_of(part)], orecv.at[s, rows_of(part)], or_sem.at[part]
        )

    def send_o(part):
        o_own(part).start()

        def one(i, _):
            o_copy(seq_peer(i), part).start()
            return 0

        lax.fori_loop(0, 7, one, 0)

    def wait_o(part):
        everything = orecv.at[:, rows_of(part)]
        pltpu.make_async_copy(everything, everything, or_sem.at[part]).wait()

    def drain_o():
        for part in range(2):
            sent = osend.at[pl.ds(0, 7), rows_of(part)]
            pltpu.make_async_copy(sent, sent, os_sem.at[part]).wait()

    for load in loads[:3]:
        load.wait()
    stats = jnp.zeros((KVH * GROUP, 128), jnp.float32)
    stats = attend(0, stats)
    stats = attend(1, stats)
    pl.semaphore_wait(barrier, 127)
    drains.append(drain_o)
    send_o(0)
    for j in range(4):
        w_remote(j).start()
    stats = attend(2, stats)
    stats = attend(3, stats)
    high = stats.astype(jnp.bfloat16).astype(jnp.float32)
    middle = (stats - high).astype(jnp.bfloat16).astype(jnp.float32)
    low = stats - high - middle
    pieces = (high + pltpu.roll(middle, 4, 1) + pltpu.roll(low, 8, 1)).astype(jnp.bfloat16)
    for h in range(KVH):
        osend[h, 64:80, :] = pieces[h * GROUP:(h + 1) * GROUP]
    send_o(1)

    slot = lax.broadcasted_iota(jnp.int32, (SHARE, 256), 0)
    for r in range(REQ):
        live = slot < new_s[t * REQ + r] - s * SHARE
        for h in range(KVH):
            fresh[r, h] = jnp.where(live, kv[r, h, WIDTH:, :], jnp.zeros((), jnp.bfloat16))

    def drain_gather():
        for half in range(2):
            own[half].wait()
            pair_own(half).wait()
            for way in range(2):
                first(way, half).wait_send()
                pair_near(way, half).wait()
        for way in range(2):
            second(way).wait_send()
            pair_far(way).wait()

    def drain_w():
        for j in range(4):
            w_remote(j).wait_send()

    drains.append(drain_gather)
    drains.append(drain_w)

    wait_o(0)
    wait_o(1)
    for order in range(2):
        for way in range(2):
            first(way, order).start()
    for half in range(2):
        own[half].start()
        pair_own(half).start()

    tops = []
    for k in range(8):
        piece = orecv[k, 64:80, :].astype(jnp.float32)
        tops.append(piece + pltpu.roll(piece, 124, 1) + pltpu.roll(piece, 120, 1))
    top = functools.reduce(jnp.maximum, tops)
    exps = [jnp.exp(v - top) for v in tops]
    total = functools.reduce(jnp.add, exps)
    shares = [e / total for e in exps]
    for r in range(REQ):
        context = jnp.zeros((GROUP, HD), jnp.float32)
        for k in range(8):
            part = orecv[k, r * GROUP:(r + 1) * GROUP, :].astype(jnp.float32)
            context = context + part * shares[k][:, r:r + 1]
        csend[:, r, :] = context

    def c_copy(core, g):
        return remote(
            csend.at[g], crecv.at[c, t], cs_sem.at[0], cr_sem.at[0], (y * 2 + core, g)
        )

    def send_c(i, _):
        g = tp_peer(i)
        c_copy(c, g).start()
        c_copy(1 - c, g).start()
        return 0

    def drain_c():
        for sent in (csend, csend.at[pl.ds(0, 15)]):
            pltpu.make_async_copy(sent, sent, cs_sem.at[0]).wait()

    drains.append(drain_c)
    lax.fori_loop(0, 15, send_c, 0)
    c_copy(1 - c, t).start()
    pltpu.make_async_copy(csend.at[t], crecv.at[c, t], cr_sem.at[0]).start()
    for j in range(4):
        w_local(j).wait()
        w_remote(j).wait_recv()
    pltpu.make_async_copy(crecv, crecv, cr_sem.at[0]).wait()

    flat = jnp.concatenate(
        [
            jnp.concatenate([crecv[core, :, r, :] for r in range(REQ)], axis=0)
            for core in range(2)
        ],
        axis=1,
    ).astype(jnp.bfloat16)

    def r1_copy(way, d, part):
        dst = lax.rem((x if way == 0 else z) + d, 4)
        src = (a_send if way == 0 else b_send).at[dst, pl.ds(part * 2, 2)]
        to = (a_recv if way == 0 else b_recv).at[d - 1, pl.ds(part * 2, 2)]
        return remote(
            src, to, r1s_sem.at[way, d - 1, part], r1r_sem.at[way, d - 1, part],
            (s, x_at(d) if way == 0 else z_at(d)),
        )

    def project(j, _):
        for i in range(4):
            piece = jnp.dot(flat, w_v[j, :, i * 512:(i + 1) * 512], preferred_element_type=jnp.float32)
            piece = piece.astype(jnp.bfloat16)
            a_send[i, j] = piece[:32]
            for k in range(4):
                b_send[k, j, :, i * 128:(i + 1) * 128] = piece[32:, k * 128:(k + 1) * 128]
        return 0

    def drain_r1():
        for way in range(2):
            for d in range(1, 4):
                for part in range(2):
                    r1_copy(way, d, part).wait_send()

    drains.append(drain_r1)
    for part in range(2):
        lax.fori_loop(part * 2, part * 2 + 2, project, 0)
        for d in (2, 1, 3):
            for way in range(2):
                r1_copy(way, d, part).start()

    def r2_copy(way, j, k):
        there = z if way == 0 else x
        send, recv = ((a2_send, a2_recv), (b2_send, b2_recv))[way]
        return remote(
            send.at[j, k], recv.at[y, there], r2s_sem.at[way], r2r_sem.at[way],
            (j * 2 + c, x * 4 + k if way == 0 else k * 4 + z),
        )

    def drain_r2():
        for way in range(2):
            send = (a2_send, b2_send)[way]
            for sent in (send.at[pl.ds(0, 3)], send.at[0, pl.ds(0, 3)]):
                pltpu.make_async_copy(sent, sent, r2s_sem.at[way]).wait()

    drains.append(drain_r2)
    for part in range(2):
        for way in range(2):
            for d in (1, 3, 2):
                r1_copy(way, d, part).wait_recv()
            send, recv, nxt = ((a_send, a_recv, a2_send), (b_send, b_recv, b2_send))[way]
            last = ((a2_send, a2_recv), (b2_send, b2_recv))[way]
            mine = x if way == 0 else z
            there = z if way == 0 else x

            def add(j, _):
                out = send[mine, j].astype(jnp.float32)
                for d in range(3):
                    out = out + recv[d, j].astype(jnp.float32)
                out = out.astype(jnp.bfloat16)
                for k in range(4):
                    nxt[j, k] = out[:, k * 128:(k + 1) * 128]
                for k in range(4):
                    away = (j != y) | (k != there)

                    @pl.when(away)
                    def _():
                        r2_copy(way, j, k).start()

                    @pl.when(jnp.logical_not(away))
                    def _():
                        pltpu.make_async_copy(nxt.at[j, k], last[1].at[j, k], r2r_sem.at[way]).start()
                return 0

            lax.fori_loop(part * 2, part * 2 + 2, add, 0)
        if part == 0:
            for way in range(2):
                first(way, 0).wait_recv()
                second(way).start()
                pair_near(way, 0).start()

    for load in loads[3:]:
        load.wait()
    rows_v[...] = hid_v[...].astype(jnp.float32)
    stream = jnp.concatenate([rows_v[pl.ds(r, 16, stride=REQ), :] for r in range(REQ)], axis=0)
    for way in range(2):
        first(way, 1).wait_recv()
        pair_near(way, 1).start()
    sums = []
    for way in range(2):
        recv = (a2_recv, b2_recv)[way]
        pltpu.make_async_copy(recv, recv, r2r_sem.at[way]).wait()
        out = recv[0, 0].astype(jnp.float32)
        for i in range(1, 16):
            out = out + recv[i // 4, i % 4].astype(jnp.float32)
        sums.append(out)
    stream = stream + jnp.concatenate(sums, axis=0)

    squares = stream * stream
    n_send[...] = jnp.sum(jnp.concatenate([squares, squares], axis=0).T, axis=0, keepdims=True)

    def send_n(i, _):
        pltpu.make_async_remote_copy(
            src_ref=n_send, dst_ref=n_recv.at[me], send_sem=ns_sem.at[0], recv_sem=nr_sem.at[0],
            device_id=any_peer(i), device_id_type=MESH,
        ).start()
        return 0

    def drain_n():
        sent = n_recv.at[pl.ds(0, 127)]
        pltpu.make_async_copy(sent, sent, ns_sem.at[0]).wait()

    drains.append(drain_n)
    lax.fori_loop(0, 127, send_n, 0)
    pltpu.make_async_copy(n_send, n_recv.at[me], nr_sem.at[0]).start()
    for r in range(REQ):
        rows_v[pl.ds(r, 16, stride=REQ), :] = stream[r * 16:(r + 1) * 16]
    res_v[...] = rows_v[...].astype(jnp.bfloat16)
    res_out = pltpu.make_async_copy(res_v, res_hbm, out_sem.at[0])
    res_out.start()
    for way in range(2):
        second(way).wait_recv()
        pair_far(way).start()
    scaled = stream * gain_v[...]
    pltpu.make_async_copy(n_recv, n_recv, nr_sem.at[0]).wait()
    scale = lax.rsqrt(jnp.sum(n_recv[...], axis=0) / D + 1e-05)
    scale = jnp.broadcast_to(scale, (128, 128)).T[:64]
    normed = scaled * scale
    for r in range(REQ):
        rows_v[pl.ds(r, 16, stride=REQ), :] = normed[r * 16:(r + 1) * 16]
    norm_v[...] = rows_v[...].astype(jnp.bfloat16)
    norm_out = pltpu.make_async_copy(norm_v, norm_hbm, out_sem.at[1])
    norm_out.start()
    res_out.wait()
    norm_out.wait()
    for drain in drains:
        drain()


def step(queries, cache_kv, new_kv, ctx_len, new_len, wo, hidden_in, norm_gain):
    bf, f32 = jnp.bfloat16, jnp.float32
    dma = pltpu.SemaphoreType.DMA
    anywhere = pl.BlockSpec(memory_space=pl.ANY)
    V = pltpu.VMEM
    return pl.pallas_call(
        kernel,
        out_shape=(
            jax.ShapeDtypeStruct((64, 128), bf),
            jax.ShapeDtypeStruct((64, 128), bf),
            jax.ShapeDtypeStruct((REQ, KVH, WIDTH, 256), bf),
        ),
        in_specs=[anywhere] * 8,
        out_specs=(anywhere, anywhere, anywhere),
        scratch_shapes=[
            pltpu.SMEM((64,), jnp.int32), pltpu.SMEM((64,), jnp.int32),
            V((REQ, KVH, GROUP, HD), bf),
            V((REQ, KVH, KEYS, 256), bf),
            V((REQ, KVH, SHARE, 256), bf),
            V((4, 256, 2048), bf),
            V((64, 128), bf),
            V((1, 128), f32),
            V((8, 80, HD), bf), V((8, 80, HD), bf),
            V((16, REQ, HD), f32), V((2, 16, REQ, HD), f32),
            V((4, 4, 32, 512), bf), V((4, 4, 32, 512), bf),
            V((3, 4, 32, 512), bf), V((3, 4, 32, 512), bf),
            V((4, 4, 32, 128), bf), V((4, 4, 32, 128), bf),
            V((4, 4, 32, 128), bf), V((4, 4, 32, 128), bf),
            V((1, 128), f32), V((128, 1, 128), f32),
            V((64, 128), f32), V((64, 128), bf), V((64, 128), bf),
            dma((5,)), dma((2,)), dma((REQ, 2)), dma((4,)), dma((4,)), dma((4,)),
            dma((2,)), dma((2,)), dma((1,)), dma((1,)),
            dma((2, 3, 2)), dma((2, 3, 2)), dma((2,)), dma((2,)), dma((1,)), dma((1,)),
            dma((2, 3)), dma((2, 3)), dma((8,)), dma((8,)), dma((2,)),
        ],
        compiler_params=pltpu.CompilerParams(
            collective_id=0, has_side_effects=True, vmem_limit_bytes=62 * 1024 * 1024
        ),
        cost_estimate=pl.CostEstimate(flops=600_000_000, bytes_accessed=14_000_000, transcendentals=1_000_000),
    )(ctx_len, new_len, queries, cache_kv, new_kv, wo, hidden_in, norm_gain.reshape(1, 128))


def store_kernel(owner_ref, res_in, norm_in, deliv_hbm, res_hbm, norm_hbm, app_hbm, zeros, out_sem, sem):
    s = lax.axis_index("seq")
    t = lax.axis_index("tp")
    small = (
        pltpu.make_async_copy(res_in, res_hbm, sem.at[0]),
        pltpu.make_async_copy(norm_in, norm_hbm, sem.at[1]),
    )
    for copy in small:
        copy.start()

    def blank(r, i):
        return pltpu.make_async_copy(zeros, app_hbm.at[r, pl.ds(i * 2, 2)], out_sem.at[r, i])

    def put(r, i):
        part = pl.ds(i * 2, 2)
        return pltpu.make_async_copy(deliv_hbm.at[r, part], app_hbm.at[r, part], out_sem.at[r, i])

    zeros[...] = jnp.zeros_like(zeros)
    for r in range(REQ):
        mine = owner_ref[t * REQ + r] == s

        @pl.when(mine)
        def _():
            for i in range(4):
                put(r, i).start()

        @pl.when(jnp.logical_not(mine))
        def _():
            for i in range(4):
                blank(r, i).start()

    for copy in small:
        copy.wait()
    for r in range(REQ):
        for i in range(4):
            put(r, i).wait()


def store(owner, residual_out, normed, delivered):
    anywhere = pl.BlockSpec(memory_space=pl.ANY)
    smem = pl.BlockSpec(memory_space=pltpu.SMEM)
    return pl.pallas_call(
        store_kernel,
        out_shape=tuple(jax.ShapeDtypeStruct(v.shape, v.dtype) for v in (residual_out, normed, delivered)),
        in_specs=[smem] + [anywhere] * 3,
        out_specs=(anywhere,) * 3,
        scratch_shapes=[
            pltpu.VMEM((2, WIDTH, 256), jnp.bfloat16),
            pltpu.SemaphoreType.DMA((REQ, 4)),
            pltpu.SemaphoreType.DMA((2,)),
        ],
        compiler_params=pltpu.CompilerParams(vmem_limit_bytes=62 * 1024 * 1024),
        cost_estimate=pl.CostEstimate(flops=0, bytes_accessed=6_000_000, transcendentals=0),
    )(owner, residual_out, normed, delivered)


def per_device(queries, cache_kv, new_kv, ctx_len, new_len, owner, wo, hidden_in, norm_gain):
    residual_out, normed, delivered = step(
        queries, cache_kv, new_kv, ctx_len, new_len, wo, hidden_in, norm_gain
    )
    return store(owner, residual_out, normed, delivered)


def solution(mesh):
    in_specs = (
        P("tp", None, None, None),
        P("tp", None, "seq", None),
        P("tp", None, "seq", None),
        P(),
        P(),
        P(),
        P(("seq", "tp"), None),
        P(None, ("seq", "tp")),
        P(("seq", "tp")),
    )
    out_specs = (P(None, ("seq", "tp")), P(None, ("seq", "tp")), P("tp", None, "seq", None))
    return jax.shard_map(
        per_device, mesh=mesh, in_specs=in_specs, out_specs=out_specs, check_vma=False
    )
```

```python
import functools

import jax
import jax.numpy as jnp
from jax import lax
from jax.experimental import pallas as pl
from jax.experimental.pallas import tpu as pltpu
from jax.sharding import PartitionSpec as P

D = 16384
HD = 128
KVH = 8
GROUP = 16
REQ = 4
WIDTH = 256
SHARE = 32
KEYS = WIDTH + SHARE
NEG = -1e30
MESH = pl.DeviceIdType.MESH


def remote(src, dst, send, recv, device):
    return pltpu.make_async_remote_copy(
        src_ref=src, dst_ref=dst, send_sem=send, recv_sem=recv, device_id=device, device_id_type=MESH
    )


def kernel(
    ctx_hbm, new_hbm, q_hbm, cache_hbm, newkv_hbm, wo_hbm, hidden_hbm, gain_hbm,
    res_hbm, norm_hbm, deliv_hbm,
    ctx_s, new_s, q_v, kv, got, w_v, hid_v, gain_v,
    osend, orecv, csend, crecv,
    a_send, b_send, a_recv, b_recv, a2_send, b2_send, a2_recv, b2_recv,
    n_send, n_recv, rows_v, res_v, norm_v,
    loc_sem, out_sem, kv_sem, wl_sem, ws_sem, wr_sem,
    os_sem, or_sem, cs_sem, cr_sem,
    r1s_sem, r1r_sem, r2s_sem, r2r_sem, ns_sem, nr_sem,
    gs_sem, gr_sem, ps_sem, pr_sem, gl_sem,
):
    s = lax.axis_index("seq")
    t = lax.axis_index("tp")
    y, c = s // 2, s % 2
    x, z = t // 4, t % 4
    me = s * 16 + t
    sp = y * 2 + (1 - c)

    def seq_peer(i):
        return (s + 1 + i) & 7

    def tp_peer(i):
        return (t + 1 + i) & 15

    def any_peer(i):
        k = (me + 1 + i) & 127
        return k >> 4, k & 15

    def y_at(d):
        return lax.rem(y + d, 4) * 2 + c

    def x_at(d):
        return lax.rem(x + d, 4) * 4 + z

    def z_at(d):
        return x * 4 + lax.rem(z + d, 4)

    drains = []

    loads = [
        pltpu.make_async_copy(src, dst, loc_sem.at[i])
        for i, (src, dst) in enumerate(
            [(ctx_hbm, ctx_s), (new_hbm, new_s), (q_hbm, q_v), (hidden_hbm, hid_v), (gain_hbm, gain_v)]
        )
    ]

    def kv_copies(r):
        return (
            pltpu.make_async_copy(cache_hbm.at[r], kv.at[r, :, pl.ds(0, WIDTH), :], kv_sem.at[r, 0]),
            pltpu.make_async_copy(newkv_hbm.at[r], kv.at[r, :, pl.ds(WIDTH, SHARE), :], kv_sem.at[r, 1]),
        )

    for load in loads[:3]:
        load.start()
    for r in range(REQ):
        for copy in kv_copies(r):
            copy.start()
    for load in loads[3:]:
        load.start()

    barrier = pltpu.get_barrier_semaphore()

    def greet(i, _):
        pl.semaphore_signal(barrier, inc=1, device_id=any_peer(i), device_id_type=MESH)
        return 0

    lax.fori_loop(0, 127, greet, 0)

    def w_local(j):
        return pltpu.make_async_copy(
            wo_hbm.at[:, pl.ds(pl.multiple_of(j * 4096 + c * 2048, 2048), 2048)],
            w_v.at[j, pl.ds(pl.multiple_of(c * 128, 128), 128), :],
            wl_sem.at[j],
        )

    def w_remote(j):
        return remote(
            wo_hbm.at[:, pl.ds(pl.multiple_of(j * 4096 + (1 - c) * 2048, 2048), 2048)],
            w_v.at[j, pl.ds(pl.multiple_of(c * 128, 128), 128), :],
            ws_sem.at[j], wr_sem.at[j], (sp, t),
        )

    for j in range(4):
        w_local(j).start()

    def block(half, who):
        return got.at[pl.ds(half * 2, 2), :, pl.ds(pl.multiple_of(who * SHARE, SHARE), SHARE), :]

    def ring(way, slot, src, dst):
        return remote(src, dst, gs_sem.at[way, slot], gr_sem.at[way, slot], (y_at(1 if way == 0 else 3), t))

    def first(way, order):
        half = order if way == 0 else 1 - order
        return ring(way, order, block(half, s), block(half, s))

    def second(way):
        who = y_at(3) if way == 0 else y_at(1)
        return ring(way, 2, block(way, who), block(way, who))

    def pair(slot, src, half, who):
        return remote(src, block(half, who), ps_sem.at[slot], pr_sem.at[slot], (sp, t))

    def pair_own(half):
        return pair(half, block(half, s), half, s)

    def pair_near(way, order):
        half = order if way == 0 else 1 - order
        who = y_at(3) if way == 0 else y_at(1)
        return pair(2 + way * 2 + order, block(half, who), half, who)

    def pair_far(way):
        return pair(6 + way, block(way, y_at(2)), way, y_at(2))

    col = lax.broadcasted_iota(jnp.int32, (KVH * GROUP, KEYS), 1)
    lane = lax.broadcasted_iota(jnp.int32, (KVH * GROUP, 128), 1)

    def attend(r, stats):
        for copy in kv_copies(r):
            copy.wait()
        live_ctx = jnp.minimum(ctx_s[t * REQ + r] - s * WIDTH, WIDTH)
        live_new = new_s[t * REQ + r] - s * SHARE + WIDTH
        mask = (col < live_ctx) | ((col >= WIDTH) & (col < live_new))
        scores = jnp.concatenate(
            [
                lax.dot_general(
                    q_v[r, h], kv[r, h, :, :HD], (((1,), (1,)), ((), ())), preferred_element_type=jnp.float32
                )
                for h in range(KVH)
            ],
            axis=0,
        ) * HD ** (-0.5)
        scores = jnp.where(mask, scores, NEG)
        top = jnp.max(scores, axis=1, keepdims=True)
        weights = jnp.where(mask, jnp.exp(scores - top), 0.0)
        total = jnp.maximum(jnp.sum(weights, axis=1, keepdims=True), 1e-30)
        weights = weights.astype(jnp.bfloat16)
        inverse = 1.0 / total
        for h in range(KVH):
            rows = slice(h * GROUP, (h + 1) * GROUP)
            out = jnp.dot(weights[rows], kv[r, h, :, HD:], preferred_element_type=jnp.float32)
            osend[h, r * GROUP:(r + 1) * GROUP, :] = (out * inverse[rows]).astype(jnp.bfloat16)
        return jnp.where(lane == r, top + jnp.log(total), stats)

    def rows_of(part):
        return pl.ds(0, 32) if part == 0 else pl.ds(32, 48)

    def o_copy(k, part):
        return remote(
            osend.at[k, rows_of(part)], orecv.at[s, rows_of(part)], os_sem.at[part], or_sem.at[part], (k, t)
        )

    def o_own(part):
        return pltpu.make_async_copy(
            osend.at[s, rows_of(part)], orecv.at[s, rows_of(part)], or_sem.at[part]
        )

    def send_o(part):
        o_own(part).start()

        def one(i, _):
            o_copy(seq_peer(i), part).start()
            return 0

        lax.fori_loop(0, 7, one, 0)

    def wait_o(part):
        everything = orecv.at[:, rows_of(part)]
        pltpu.make_async_copy(everything, everything, or_sem.at[part]).wait()

    def drain_o():
        for part in range(2):
            sent = osend.at[pl.ds(0, 7), rows_of(part)]
            pltpu.make_async_copy(sent, sent, os_sem.at[part]).wait()

    for load in loads[:3]:
        load.wait()
    stats = jnp.zeros((KVH * GROUP, 128), jnp.float32)
    stats = attend(0, stats)
    stats = attend(1, stats)
    pl.semaphore_wait(barrier, 127)
    drains.append(drain_o)
    send_o(0)
    for j in range(4):
        w_remote(j).start()
    stats = attend(2, stats)
    stats = attend(3, stats)
    high = stats.astype(jnp.bfloat16).astype(jnp.float32)
    middle = (stats - high).astype(jnp.bfloat16).astype(jnp.float32)
    low = stats - high - middle
    pieces = (high + pltpu.roll(middle, 4, 1) + pltpu.roll(low, 8, 1)).astype(jnp.bfloat16)
    for h in range(KVH):
        osend[h, 64:80, :] = pieces[h * GROUP:(h + 1) * GROUP]
    send_o(1)

    slot = lax.broadcasted_iota(jnp.int32, (SHARE, 256), 0)
    for r in range(REQ):
        live = slot < new_s[t * REQ + r] - s * SHARE
        for h in range(KVH):
            got[r, h, pl.ds(pl.multiple_of(s * SHARE, SHARE), SHARE), :] = jnp.where(
                live, kv[r, h, WIDTH:, :], jnp.zeros((), jnp.bfloat16)
            )

    for order in range(2):
        for way in range(2):
            first(way, order).start()
    for half in range(2):
        pair_own(half).start()

    def drain_gather():
        for half in range(2):
            pair_own(half).wait()
            for way in range(2):
                first(way, half).wait_send()
                pair_near(way, half).wait()
        for way in range(2):
            second(way).wait_send()
            pair_far(way).wait()
        pltpu.make_async_copy(got, deliv_hbm, gl_sem.at[0]).start()

    def drain_w():
        for j in range(4):
            w_remote(j).wait_send()

    drains.append(drain_gather)
    drains.append(drain_w)

    wait_o(0)
    wait_o(1)

    tops = []
    for k in range(8):
        piece = orecv[k, 64:80, :].astype(jnp.float32)
        tops.append(piece + pltpu.roll(piece, 124, 1) + pltpu.roll(piece, 120, 1))
    top = functools.reduce(jnp.maximum, tops)
    exps = [jnp.exp(v - top) for v in tops]
    total = functools.reduce(jnp.add, exps)
    shares = [e / total for e in exps]
    for r in range(REQ):
        context = jnp.zeros((GROUP, HD), jnp.float32)
        for k in range(8):
            part = orecv[k, r * GROUP:(r + 1) * GROUP, :].astype(jnp.float32)
            context = context + part * shares[k][:, r:r + 1]
        csend[:, r, :] = context

    def c_copy(core, g):
        return remote(
            csend.at[g], crecv.at[c, t], cs_sem.at[0], cr_sem.at[0], (y * 2 + core, g)
        )

    def send_c(i, _):
        g = tp_peer(i)
        c_copy(c, g).start()
        c_copy(1 - c, g).start()
        return 0

    def drain_c():
        for sent in (csend, csend.at[pl.ds(0, 15)]):
            pltpu.make_async_copy(sent, sent, cs_sem.at[0]).wait()

    drains.append(drain_c)
    lax.fori_loop(0, 15, send_c, 0)
    c_copy(1 - c, t).start()
    pltpu.make_async_copy(csend.at[t], crecv.at[c, t], cr_sem.at[0]).start()
    for j in range(4):
        w_local(j).wait()
        w_remote(j).wait_recv()
    pltpu.make_async_copy(crecv, crecv, cr_sem.at[0]).wait()

    for way in range(2):
        first(way, 0).wait_recv()
        second(way).start()
        pair_near(way, 0).start()
    flat = jnp.concatenate(
        [
            jnp.concatenate([crecv[core, :, r, :] for r in range(REQ)], axis=0)
            for core in range(2)
        ],
        axis=1,
    ).astype(jnp.bfloat16)

    def r1_copy(way, d, part):
        dst = lax.rem((x if way == 0 else z) + d, 4)
        src = (a_send if way == 0 else b_send).at[dst, part]
        to = (a_recv if way == 0 else b_recv).at[d - 1, part]
        return remote(
            src, to, r1s_sem.at[way, d - 1, part], r1r_sem.at[way, d - 1, part],
            (s, x_at(d) if way == 0 else z_at(d)),
        )

    def project(j, _):
        for i in range(4):
            piece = jnp.dot(flat, w_v[j, :, i * 512:(i + 1) * 512], preferred_element_type=jnp.float32)
            piece = piece.astype(jnp.bfloat16)
            a_send[i, j] = piece[:32]
            for k in range(4):
                b_send[k, j, :, i * 128:(i + 1) * 128] = piece[32:, k * 128:(k + 1) * 128]
        return 0

    def drain_r1():
        for way in range(2):
            for d in range(1, 4):
                for part in range(4):
                    r1_copy(way, d, part).wait_send()

    drains.append(drain_r1)
    for part in range(4):
        project(part, 0)
        for d in (2, 1, 3):
            for way in range(2):
                r1_copy(way, d, part).start()

    for way in range(2):
        first(way, 1).wait_recv()
        pair_near(way, 1).start()

    def r2_copy(way, j, k):
        there = z if way == 0 else x
        send, recv = ((a2_send, a2_recv), (b2_send, b2_recv))[way]
        return remote(
            send.at[j, k], recv.at[y, there], r2s_sem.at[way], r2r_sem.at[way],
            (j * 2 + c, x * 4 + k if way == 0 else k * 4 + z),
        )

    def drain_r2():
        for way in range(2):
            send = (a2_send, b2_send)[way]
            for sent in (send.at[pl.ds(0, 3)], send.at[0, pl.ds(0, 3)]):
                pltpu.make_async_copy(sent, sent, r2s_sem.at[way]).wait()

    drains.append(drain_r2)
    for part in range(4):
        for way in range(2):
            for d in (1, 3, 2):
                r1_copy(way, d, part).wait_recv()
            send, recv, nxt = ((a_send, a_recv, a2_send), (b_send, b_recv, b2_send))[way]
            last = ((a2_send, a2_recv), (b2_send, b2_recv))[way]
            mine = x if way == 0 else z
            there = z if way == 0 else x

            def add(j, _):
                out = send[mine, j].astype(jnp.float32)
                for d in range(3):
                    out = out + recv[d, j].astype(jnp.float32)
                out = out.astype(jnp.bfloat16)
                for k in range(4):
                    nxt[j, k] = out[:, k * 128:(k + 1) * 128]
                for k in range(4):
                    away = (j != y) | (k != there)

                    @pl.when(away)
                    def _():
                        r2_copy(way, j, k).start()

                    @pl.when(jnp.logical_not(away))
                    def _():
                        pltpu.make_async_copy(nxt.at[j, k], last[1].at[j, k], r2r_sem.at[way]).start()
                return 0

            add(part, 0)

    for load in loads[3:]:
        load.wait()
    rows_v[...] = hid_v[...].astype(jnp.float32)
    stream = jnp.concatenate([rows_v[pl.ds(r, 16, stride=REQ), :] for r in range(REQ)], axis=0)
    sums = []
    for way in range(2):
        recv = (a2_recv, b2_recv)[way]
        pltpu.make_async_copy(recv, recv, r2r_sem.at[way]).wait()
        out = recv[0, 0].astype(jnp.float32)
        for i in range(1, 16):
            out = out + recv[i // 4, i % 4].astype(jnp.float32)
        sums.append(out)
    stream = stream + jnp.concatenate(sums, axis=0)

    squares = stream * stream
    n_send[...] = jnp.sum(jnp.concatenate([squares, squares], axis=0).T, axis=0, keepdims=True)

    def send_n(i, _):
        pltpu.make_async_remote_copy(
            src_ref=n_send, dst_ref=n_recv.at[me], send_sem=ns_sem.at[0], recv_sem=nr_sem.at[0],
            device_id=any_peer(i), device_id_type=MESH,
        ).start()
        return 0

    def drain_n():
        sent = n_recv.at[pl.ds(0, 127)]
        pltpu.make_async_copy(sent, sent, ns_sem.at[0]).wait()

    lax.fori_loop(0, 127, send_n, 0)
    pltpu.make_async_copy(n_send, n_recv.at[me], nr_sem.at[0]).start()
    for r in range(REQ):
        rows_v[pl.ds(r, 16, stride=REQ), :] = stream[r * 16:(r + 1) * 16]
    res_v[...] = rows_v[...].astype(jnp.bfloat16)
    res_out = pltpu.make_async_copy(res_v, res_hbm, out_sem.at[0])
    res_out.start()
    for way in range(2):
        second(way).wait_recv()
        pair_far(way).start()
    scaled = stream * gain_v[...]
    for drain in drains:
        drain()
    pltpu.make_async_copy(n_recv, n_recv, nr_sem.at[0]).wait()
    scale = lax.rsqrt(jnp.sum(n_recv[...], axis=0) / D + 1e-05)
    scale = jnp.broadcast_to(scale, (128, 128)).T[:64]
    normed = scaled * scale
    for r in range(REQ):
        rows_v[pl.ds(r, 16, stride=REQ), :] = normed[r * 16:(r + 1) * 16]
    norm_v[...] = rows_v[...].astype(jnp.bfloat16)
    norm_out = pltpu.make_async_copy(norm_v, norm_hbm, out_sem.at[1])
    norm_out.start()
    res_out.wait()
    drain_n()
    pltpu.make_async_copy(got, deliv_hbm, gl_sem.at[0]).wait()
    norm_out.wait()


def step(queries, cache_kv, new_kv, ctx_len, new_len, wo, hidden_in, norm_gain):
    bf, f32 = jnp.bfloat16, jnp.float32
    dma = pltpu.SemaphoreType.DMA
    anywhere = pl.BlockSpec(memory_space=pl.ANY)
    V = pltpu.VMEM
    return pl.pallas_call(
        kernel,
        out_shape=(
            jax.ShapeDtypeStruct((64, 128), bf),
            jax.ShapeDtypeStruct((64, 128), bf),
            jax.ShapeDtypeStruct((REQ, KVH, WIDTH, 256), bf),
        ),
        in_specs=[anywhere] * 8,
        out_specs=(anywhere, anywhere, anywhere),
        scratch_shapes=[
            pltpu.SMEM((64,), jnp.int32), pltpu.SMEM((64,), jnp.int32),
            V((REQ, KVH, GROUP, HD), bf),
            V((REQ, KVH, KEYS, 256), bf),
            V((REQ, KVH, WIDTH, 256), bf),
            V((4, 256, 2048), bf),
            V((64, 128), bf),
            V((1, 128), f32),
            V((8, 80, HD), bf), V((8, 80, HD), bf),
            V((16, REQ, HD), f32), V((2, 16, REQ, HD), f32),
            V((4, 4, 32, 512), bf), V((4, 4, 32, 512), bf),
            V((3, 4, 32, 512), bf), V((3, 4, 32, 512), bf),
            V((4, 4, 32, 128), bf), V((4, 4, 32, 128), bf),
            V((4, 4, 32, 128), bf), V((4, 4, 32, 128), bf),
            V((1, 128), f32), V((128, 1, 128), f32),
            V((64, 128), f32), V((64, 128), bf), V((64, 128), bf),
            dma((5,)), dma((2,)), dma((REQ, 2)), dma((4,)), dma((4,)), dma((4,)),
            dma((2,)), dma((2,)), dma((1,)), dma((1,)),
            dma((2, 3, 4)), dma((2, 3, 4)), dma((2,)), dma((2,)), dma((1,)), dma((1,)),
            dma((2, 3)), dma((2, 3)), dma((8,)), dma((8,)), dma((1,)),
        ],
        compiler_params=pltpu.CompilerParams(
            collective_id=0, has_side_effects=True, vmem_limit_bytes=62 * 1024 * 1024
        ),
        cost_estimate=pl.CostEstimate(flops=600_000_000, bytes_accessed=14_000_000, transcendentals=1_000_000),
    )(ctx_len, new_len, queries, cache_kv, new_kv, wo, hidden_in, norm_gain.reshape(1, 128))


def store_kernel(
    owner_hbm, res_in, norm_in, deliv_hbm, res_hbm, norm_hbm, app_hbm,
    owner_ref, zeros, held, out_sem, in_sem, sem,
):
    s = lax.axis_index("seq")
    t = lax.axis_index("tp")

    def blank(r, i):
        return pltpu.make_async_copy(zeros, app_hbm.at[r, pl.ds(i * 2, 2)], out_sem.at[r, i])

    def fetch(r, i):
        part = pl.ds(i * 2, 2)
        return pltpu.make_async_copy(deliv_hbm.at[r, part], held.at[r, part], in_sem.at[r, i])

    def put(r, i):
        part = pl.ds(i * 2, 2)
        return pltpu.make_async_copy(held.at[r, part], app_hbm.at[r, part], out_sem.at[r, i])

    def mine(r):
        return owner_ref[t * REQ + r] == s

    who = pltpu.make_async_copy(owner_hbm, owner_ref, sem.at[2])
    who.start()
    small = (
        pltpu.make_async_copy(res_in, res_hbm, sem.at[0]),
        pltpu.make_async_copy(norm_in, norm_hbm, sem.at[1]),
    )
    for copy in small:
        copy.start()
    zeros[...] = jnp.zeros_like(zeros)
    who.wait()
    for r in range(REQ):
        @pl.when(mine(r))
        def _():
            for i in range(4):
                fetch(r, i).start()

    for r in range(REQ):
        @pl.when(jnp.logical_not(mine(r)))
        def _():
            for i in range(4):
                blank(r, i).start()

    for r in range(REQ):
        @pl.when(mine(r))
        def _():
            for i in range(4):
                fetch(r, i).wait()
                put(r, i).start()

    for copy in small:
        copy.wait()
    for r in range(REQ):
        for i in range(4):
            put(r, i).wait()


def store(owner, residual_out, normed, delivered):
    anywhere = pl.BlockSpec(memory_space=pl.ANY)
    return pl.pallas_call(
        store_kernel,
        out_shape=tuple(jax.ShapeDtypeStruct(v.shape, v.dtype) for v in (residual_out, normed, delivered)),
        in_specs=[anywhere] * 4,
        out_specs=(anywhere,) * 3,
        scratch_shapes=[
            pltpu.SMEM((64,), jnp.int32),
            pltpu.VMEM((2, WIDTH, 256), jnp.bfloat16),
            pltpu.VMEM((REQ, KVH, WIDTH, 256), jnp.bfloat16),
            pltpu.SemaphoreType.DMA((REQ, 4)),
            pltpu.SemaphoreType.DMA((REQ, 4)),
            pltpu.SemaphoreType.DMA((3,)),
        ],
        compiler_params=pltpu.CompilerParams(vmem_limit_bytes=62 * 1024 * 1024),
        cost_estimate=pl.CostEstimate(flops=0, bytes_accessed=6_000_000, transcendentals=0),
    )(owner, residual_out, normed, delivered)


def per_device(queries, cache_kv, new_kv, ctx_len, new_len, owner, wo, hidden_in, norm_gain):
    residual_out, normed, delivered = step(
        queries, cache_kv, new_kv, ctx_len, new_len, wo, hidden_in, norm_gain
    )
    return store(owner, residual_out, normed, delivered)


def solution(mesh):
    in_specs = (
        P("tp", None, None, None),
        P("tp", None, "seq", None),
        P("tp", None, "seq", None),
        P(),
        P(),
        P(),
        P(("seq", "tp"), None),
        P(None, ("seq", "tp")),
        P(("seq", "tp")),
    )
    out_specs = (P(None, ("seq", "tp")), P(None, ("seq", "tp")), P("tp", None, "seq", None))
    return jax.shard_map(
        per_device, mesh=mesh, in_specs=in_specs, out_specs=out_specs, check_vma=False
    )
```

```python
import functools

import jax
import jax.numpy as jnp
from jax import lax
from jax.experimental import pallas as pl
from jax.experimental.pallas import tpu as pltpu
from jax.sharding import PartitionSpec as P

D = 16384
HD = 128
KVH = 8
GROUP = 16
REQ = 4
WIDTH = 256
SHARE = 32
KEYS = WIDTH + SHARE
NEG = -1e30
MESH = pl.DeviceIdType.MESH


def remote(src, dst, send, recv, device):
    return pltpu.make_async_remote_copy(
        src_ref=src, dst_ref=dst, send_sem=send, recv_sem=recv, device_id=device, device_id_type=MESH
    )


def kernel(
    ctx_hbm, new_hbm, q_hbm, cache_hbm, newkv_hbm, wo_hbm, hidden_hbm, gain_hbm,
    res_ref, norm_ref, got,
    ctx_s, new_s, q_v, kv, w_v, hid_v, gain_v,
    osend, orecv, csend, crecv,
    a_send, b_send, a_recv, b_recv, a2_send, b2_send, a2_recv, b2_recv,
    n_send, n_recv, rows_v,
    loc_sem, kv_sem, wl_sem, ws_sem, wr_sem,
    os_sem, or_sem, cs_sem, cr_sem,
    r1s_sem, r1r_sem, r2s_sem, r2r_sem, ns_sem, nr_sem,
    gs_sem, gr_sem, ps_sem, pr_sem,
):
    s = lax.axis_index("seq")
    t = lax.axis_index("tp")
    y, c = s // 2, s % 2
    x, z = t // 4, t % 4
    me = s * 16 + t
    sp = y * 2 + (1 - c)

    def seq_peer(i):
        return (s + 1 + i) & 7

    def tp_peer(i):
        return ((x + 2 - (i & 3)) & 3) * 4 + ((z + 2 - (i >> 2)) & 3)

    def any_peer(i):
        far = (y + 2 - ((i >> 5) & 3)) & 3
        core = c ^ (1 - (i & 1))
        return far * 2 + core, ((x + 2 - ((i >> 1) & 3)) & 3) * 4 + ((z + 2 - ((i >> 3) & 3)) & 3)

    def y_at(d):
        return lax.rem(y + d, 4) * 2 + c

    def x_at(d):
        return lax.rem(x + d, 4) * 4 + z

    def z_at(d):
        return x * 4 + lax.rem(z + d, 4)

    drains = []

    def others(count, own, send):
        lax.fori_loop(0, own, send, 0)
        lax.fori_loop(own + 1, count, send, 0)

    loads = [
        pltpu.make_async_copy(src, dst, loc_sem.at[i])
        for i, (src, dst) in enumerate(
            [(ctx_hbm, ctx_s), (new_hbm, new_s), (q_hbm, q_v), (hidden_hbm, hid_v), (gain_hbm, gain_v)]
        )
    ]

    def kv_copies(r):
        return (
            pltpu.make_async_copy(cache_hbm.at[r], kv.at[r, :, pl.ds(0, WIDTH), :], kv_sem.at[r, 0]),
            pltpu.make_async_copy(newkv_hbm.at[r], kv.at[r, :, pl.ds(WIDTH, SHARE), :], kv_sem.at[r, 1]),
        )

    for load in loads[:3]:
        load.start()
    for r in range(REQ):
        for copy in kv_copies(r):
            copy.start()
    for load in loads[3:]:
        load.start()

    barrier = pltpu.get_barrier_semaphore()

    def greet(i, _):
        pl.semaphore_signal(barrier, inc=1, device_id=any_peer(i), device_id_type=MESH)
        return 0

    others(128, 85, greet)

    def w_local(j):
        return pltpu.make_async_copy(
            wo_hbm.at[:, pl.ds(pl.multiple_of(j * 4096 + c * 2048, 2048), 2048)],
            w_v.at[j, pl.ds(pl.multiple_of(c * 128, 128), 128), :],
            wl_sem.at[j],
        )

    def w_remote(j):
        return remote(
            wo_hbm.at[:, pl.ds(pl.multiple_of(j * 4096 + (1 - c) * 2048, 2048), 2048)],
            w_v.at[j, pl.ds(pl.multiple_of(c * 128, 128), 128), :],
            ws_sem.at[j], wr_sem.at[j], (sp, t),
        )

    for j in range(4):
        w_local(j).start()

    def block(half, who):
        return got.at[pl.ds(half * 2, 2), :, pl.ds(pl.multiple_of(who * SHARE, SHARE), SHARE), :]

    def ring(way, slot, src, dst):
        return remote(src, dst, gs_sem.at[way, slot], gr_sem.at[way, slot], (y_at(1 if way == 0 else 3), t))

    def first(way, order):
        half = order if way == 0 else 1 - order
        return ring(way, order, block(half, s), block(half, s))

    def second(way):
        who = y_at(3) if way == 0 else y_at(1)
        return ring(way, 2, block(way, who), block(way, who))

    def pair(slot, src, half, who):
        return remote(src, block(half, who), ps_sem.at[slot], pr_sem.at[slot], (sp, t))

    def pair_own(half):
        return pair(half, block(half, s), half, s)

    def pair_near(way, order):
        half = order if way == 0 else 1 - order
        who = y_at(3) if way == 0 else y_at(1)
        return pair(2 + way * 2 + order, block(half, who), half, who)

    def pair_far(way):
        return pair(6 + way, block(way, y_at(2)), way, y_at(2))

    col = lax.broadcasted_iota(jnp.int32, (KVH * GROUP, KEYS), 1)
    lane = lax.broadcasted_iota(jnp.int32, (KVH * GROUP, 128), 1)

    def attend(r, stats):
        for copy in kv_copies(r):
            copy.wait()
        live_ctx = jnp.minimum(ctx_s[t * REQ + r] - s * WIDTH, WIDTH)
        live_new = new_s[t * REQ + r] - s * SHARE + WIDTH
        mask = (col < live_ctx) | ((col >= WIDTH) & (col < live_new))
        scores = jnp.concatenate(
            [
                lax.dot_general(
                    q_v[r, h], kv[r, h, :, :HD], (((1,), (1,)), ((), ())), preferred_element_type=jnp.float32
                )
                for h in range(KVH)
            ],
            axis=0,
        ) * HD ** (-0.5)
        scores = jnp.where(mask, scores, NEG)
        top = jnp.max(scores, axis=1, keepdims=True)
        weights = jnp.where(mask, jnp.exp(scores - top), 0.0)
        total = jnp.maximum(jnp.sum(weights, axis=1, keepdims=True), 1e-30)
        weights = weights.astype(jnp.bfloat16)
        inverse = 1.0 / total
        for h in range(KVH):
            rows = slice(h * GROUP, (h + 1) * GROUP)
            out = jnp.dot(weights[rows], kv[r, h, :, HD:], preferred_element_type=jnp.float32)
            osend[h, r * GROUP:(r + 1) * GROUP, :] = (out * inverse[rows]).astype(jnp.bfloat16)
        return jnp.where(lane == r, top + jnp.log(total), stats)

    def rows_of(part):
        return pl.ds(0, 32) if part == 0 else pl.ds(32, 48)

    def o_copy(k, part):
        return remote(
            osend.at[k, rows_of(part)], orecv.at[s, rows_of(part)], os_sem.at[part], or_sem.at[part], (k, t)
        )

    def o_own(part):
        return pltpu.make_async_copy(
            osend.at[s, rows_of(part)], orecv.at[s, rows_of(part)], or_sem.at[part]
        )

    def send_o(part):
        o_own(part).start()

        def one(i, _):
            o_copy(seq_peer(i), part).start()
            return 0

        lax.fori_loop(0, 7, one, 0)

    def wait_o(part):
        everything = orecv.at[:, rows_of(part)]
        pltpu.make_async_copy(everything, everything, or_sem.at[part]).wait()

    def drain_o():
        for part in range(2):
            sent = osend.at[pl.ds(0, 7), rows_of(part)]
            pltpu.make_async_copy(sent, sent, os_sem.at[part]).wait()

    for load in loads[:3]:
        load.wait()
    stats = jnp.zeros((KVH * GROUP, 128), jnp.float32)
    stats = attend(0, stats)
    stats = attend(1, stats)
    pl.semaphore_wait(barrier, 127)
    drains.append(drain_o)
    send_o(0)
    for j in range(4):
        w_remote(j).start()
    stats = attend(2, stats)
    stats = attend(3, stats)
    high = stats.astype(jnp.bfloat16).astype(jnp.float32)
    middle = (stats - high).astype(jnp.bfloat16).astype(jnp.float32)
    low = stats - high - middle
    pieces = (high + pltpu.roll(middle, 4, 1) + pltpu.roll(low, 8, 1)).astype(jnp.bfloat16)
    for h in range(KVH):
        osend[h, 64:80, :] = pieces[h * GROUP:(h + 1) * GROUP]
    send_o(1)

    slot = lax.broadcasted_iota(jnp.int32, (SHARE, 256), 0)
    for r in range(REQ):
        live = slot < new_s[t * REQ + r] - s * SHARE
        for h in range(KVH):
            got[r, h, pl.ds(pl.multiple_of(s * SHARE, SHARE), SHARE), :] = jnp.where(
                live, kv[r, h, WIDTH:, :], jnp.zeros((), jnp.bfloat16)
            )

    for order in range(2):
        for way in range(2):
            first(way, order).start()
    for half in range(2):
        pair_own(half).start()

    def drain_gather():
        for half in range(2):
            pair_own(half).wait()
            for way in range(2):
                first(way, half).wait_send()
                pair_near(way, half).wait()
        for way in range(2):
            second(way).wait_send()
            pair_far(way).wait()

    def drain_w():
        for j in range(4):
            w_remote(j).wait_send()

    drains.append(drain_gather)
    drains.append(drain_w)

    wait_o(0)
    wait_o(1)

    tops = []
    for k in range(8):
        piece = orecv[k, 64:80, :].astype(jnp.float32)
        tops.append(piece + pltpu.roll(piece, 124, 1) + pltpu.roll(piece, 120, 1))
    top = functools.reduce(jnp.maximum, tops)
    exps = [jnp.exp(v - top) for v in tops]
    total = functools.reduce(jnp.add, exps)
    shares = [e / total for e in exps]
    for r in range(REQ):
        context = jnp.zeros((GROUP, HD), jnp.float32)
        for k in range(8):
            part = orecv[k, r * GROUP:(r + 1) * GROUP, :].astype(jnp.float32)
            context = context + part * shares[k][:, r:r + 1]
        csend[:, r, :] = context

    def c_copy(core, g):
        return remote(
            csend.at[g], crecv.at[c, t], cs_sem.at[0], cr_sem.at[0], (y * 2 + core, g)
        )

    def send_c(i, _):
        g = tp_peer(i)
        c_copy(c, g).start()
        c_copy(1 - c, g).start()
        return 0

    def drain_c():
        for sent in (csend, csend.at[pl.ds(0, 15)]):
            pltpu.make_async_copy(sent, sent, cs_sem.at[0]).wait()

    drains.append(drain_c)
    others(16, 10, send_c)
    c_copy(1 - c, t).start()
    pltpu.make_async_copy(csend.at[t], crecv.at[c, t], cr_sem.at[0]).start()
    for j in range(4):
        w_local(j).wait()
        w_remote(j).wait_recv()
    pltpu.make_async_copy(crecv, crecv, cr_sem.at[0]).wait()

    for way in range(2):
        first(way, 0).wait_recv()
        second(way).start()
        pair_near(way, 0).start()
    flat = jnp.concatenate(
        [
            jnp.concatenate([crecv[core, :, r, :] for r in range(REQ)], axis=0)
            for core in range(2)
        ],
        axis=1,
    ).astype(jnp.bfloat16)

    def r1_copy(way, d, part):
        dst = lax.rem((x if way == 0 else z) + d, 4)
        src = (a_send if way == 0 else b_send).at[dst, part]
        to = (a_recv if way == 0 else b_recv).at[d - 1, part]
        return remote(
            src, to, r1s_sem.at[way, d - 1, part], r1r_sem.at[way, d - 1, part],
            (s, x_at(d) if way == 0 else z_at(d)),
        )

    def project(j, _):
        for i in range(4):
            piece = jnp.dot(flat, w_v[j, :, i * 512:(i + 1) * 512], preferred_element_type=jnp.float32)
            piece = piece.astype(jnp.bfloat16)
            a_send[i, j] = piece[:32]
            for k in range(4):
                b_send[k, j, :, i * 128:(i + 1) * 128] = piece[32:, k * 128:(k + 1) * 128]
        return 0

    def drain_r1():
        for way in range(2):
            for d in range(1, 4):
                for part in range(4):
                    r1_copy(way, d, part).wait_send()

    drains.append(drain_r1)
    for part in range(4):
        project(part, 0)
        for d in (2, 1, 3):
            for way in range(2):
                r1_copy(way, d, part).start()

    for way in range(2):
        first(way, 1).wait_recv()
        pair_near(way, 1).start()

    def r2_copy(way, j, k):
        there = z if way == 0 else x
        send, recv = ((a2_send, a2_recv), (b2_send, b2_recv))[way]
        return remote(
            send.at[j, k], recv.at[y, there], r2s_sem.at[way], r2r_sem.at[way],
            (j * 2 + c, x * 4 + k if way == 0 else k * 4 + z),
        )

    def drain_r2():
        for way in range(2):
            send = (a2_send, b2_send)[way]
            for sent in (send.at[pl.ds(0, 3)], send.at[0, pl.ds(0, 3)]):
                pltpu.make_async_copy(sent, sent, r2s_sem.at[way]).wait()

    drains.append(drain_r2)
    for part in range(4):
        for way in range(2):
            for d in (1, 3, 2):
                r1_copy(way, d, part).wait_recv()
            send, recv, nxt = ((a_send, a_recv, a2_send), (b_send, b_recv, b2_send))[way]
            last = ((a2_send, a2_recv), (b2_send, b2_recv))[way]
            mine = x if way == 0 else z
            there = z if way == 0 else x

            def add(j, _):
                out = send[mine, j].astype(jnp.float32)
                for d in range(3):
                    out = out + recv[d, j].astype(jnp.float32)
                out = out.astype(jnp.bfloat16)
                for k in range(4):
                    nxt[j, k] = out[:, k * 128:(k + 1) * 128]
                for k in range(4):
                    away = (j != y) | (k != there)

                    @pl.when(away)
                    def _():
                        r2_copy(way, j, k).start()

                    @pl.when(jnp.logical_not(away))
                    def _():
                        pltpu.make_async_copy(nxt.at[j, k], last[1].at[j, k], r2r_sem.at[way]).start()
                return 0

            add(part, 0)

    for load in loads[3:]:
        load.wait()
    rows_v[...] = hid_v[...].astype(jnp.float32)
    stream = jnp.concatenate([rows_v[pl.ds(r, 16, stride=REQ), :] for r in range(REQ)], axis=0)
    sums = []
    for way in range(2):
        recv = (a2_recv, b2_recv)[way]
        pltpu.make_async_copy(recv, recv, r2r_sem.at[way]).wait()
        out = recv[0, 0].astype(jnp.float32)
        for i in range(1, 16):
            out = out + recv[i // 4, i % 4].astype(jnp.float32)
        sums.append(out)
    stream = stream + jnp.concatenate(sums, axis=0)

    squares = stream * stream
    n_send[...] = jnp.sum(jnp.concatenate([squares, squares], axis=0).T, axis=0, keepdims=True)

    def send_n(i, _):
        pltpu.make_async_remote_copy(
            src_ref=n_send, dst_ref=n_recv.at[me], send_sem=ns_sem.at[0], recv_sem=nr_sem.at[0],
            device_id=any_peer(i), device_id_type=MESH,
        ).start()
        return 0

    def drain_n():
        sent = n_recv.at[pl.ds(0, 127)]
        pltpu.make_async_copy(sent, sent, ns_sem.at[0]).wait()

    others(128, 85, send_n)
    pltpu.make_async_copy(n_send, n_recv.at[me], nr_sem.at[0]).start()
    for r in range(REQ):
        rows_v[pl.ds(r, 16, stride=REQ), :] = stream[r * 16:(r + 1) * 16]
    res_ref[...] = rows_v[...].astype(jnp.bfloat16)
    for way in range(2):
        second(way).wait_recv()
        pair_far(way).start()
    scaled = stream * gain_v[...]
    for drain in drains:
        drain()
    pltpu.make_async_copy(n_recv, n_recv, nr_sem.at[0]).wait()
    scale = lax.rsqrt(jnp.sum(n_recv[...], axis=0) / D + 1e-05)
    scale = jnp.broadcast_to(scale, (128, 128)).T[:64]
    normed = scaled * scale
    for r in range(REQ):
        rows_v[pl.ds(r, 16, stride=REQ), :] = normed[r * 16:(r + 1) * 16]
    norm_ref[...] = rows_v[...].astype(jnp.bfloat16)
    drain_n()


def step(queries, cache_kv, new_kv, ctx_len, new_len, wo, hidden_in, norm_gain):
    bf, f32 = jnp.bfloat16, jnp.float32
    dma = pltpu.SemaphoreType.DMA
    anywhere = pl.BlockSpec(memory_space=pl.ANY)
    vmem = pl.BlockSpec(memory_space=pltpu.VMEM)
    V = pltpu.VMEM
    return pl.pallas_call(
        kernel,
        out_shape=(
            V((64, 128), bf),
            V((64, 128), bf),
            V((REQ, KVH, WIDTH, 256), bf),
        ),
        in_specs=[anywhere] * 8,
        out_specs=(vmem, vmem, vmem),
        scratch_shapes=[
            pltpu.SMEM((64,), jnp.int32), pltpu.SMEM((64,), jnp.int32),
            V((REQ, KVH, GROUP, HD), bf),
            V((REQ, KVH, KEYS, 256), bf),
            V((4, 256, 2048), bf),
            V((64, 128), bf),
            V((1, 128), f32),
            V((8, 80, HD), bf), V((8, 80, HD), bf),
            V((16, REQ, HD), f32), V((2, 16, REQ, HD), f32),
            V((4, 4, 32, 512), bf), V((4, 4, 32, 512), bf),
            V((3, 4, 32, 512), bf), V((3, 4, 32, 512), bf),
            V((4, 4, 32, 128), bf), V((4, 4, 32, 128), bf),
            V((4, 4, 32, 128), bf), V((4, 4, 32, 128), bf),
            V((1, 128), f32), V((128, 1, 128), f32),
            V((64, 128), f32),
            dma((5,)), dma((REQ, 2)), dma((4,)), dma((4,)), dma((4,)),
            dma((2,)), dma((2,)), dma((1,)), dma((1,)),
            dma((2, 3, 4)), dma((2, 3, 4)), dma((2,)), dma((2,)), dma((1,)), dma((1,)),
            dma((2, 3)), dma((2, 3)), dma((8,)), dma((8,)),
        ],
        compiler_params=pltpu.CompilerParams(
            collective_id=0, has_side_effects=True, vmem_limit_bytes=40 * 1024 * 1024
        ),
        cost_estimate=pl.CostEstimate(flops=600_000_000, bytes_accessed=14_000_000, transcendentals=1_000_000),
    )(
        *(
            pltpu.with_memory_space_constraint(v, pltpu.HBM)
            for v in (ctx_len, new_len, queries, cache_kv, new_kv, wo, hidden_in, norm_gain.reshape(1, 128))
        )
    )


def store_kernel(
    owner_hbm, res_in, norm_in, deliv_ref, res_hbm, norm_hbm, app_hbm,
    owner_ref, zeros, out_sem, sem,
):
    s = lax.axis_index("seq")
    t = lax.axis_index("tp")

    def blank(r, i):
        return pltpu.make_async_copy(zeros, app_hbm.at[r, pl.ds(i * 2, 2)], out_sem.at[r, i])

    def put(r, i):
        part = pl.ds(i * 2, 2)
        return pltpu.make_async_copy(deliv_ref.at[r, part], app_hbm.at[r, part], out_sem.at[r, i])

    def mine(r):
        return owner_ref[t * REQ + r] == s

    who = pltpu.make_async_copy(owner_hbm, owner_ref, sem.at[2])
    who.start()
    small = (
        pltpu.make_async_copy(res_in, res_hbm, sem.at[0]),
        pltpu.make_async_copy(norm_in, norm_hbm, sem.at[1]),
    )
    for copy in small:
        copy.start()
    zeros[...] = jnp.zeros_like(zeros)
    who.wait()
    for r in range(REQ):
        @pl.when(mine(r))
        def _():
            for i in range(4):
                put(r, i).start()

    for r in range(REQ):
        @pl.when(jnp.logical_not(mine(r)))
        def _():
            for i in range(4):
                blank(r, i).start()

    for copy in small:
        copy.wait()
    for r in range(REQ):
        for i in range(4):
            put(r, i).wait()


def store(owner, residual_out, normed, delivered):
    anywhere = pl.BlockSpec(memory_space=pl.ANY)
    vmem = pl.BlockSpec(memory_space=pltpu.VMEM)
    return pl.pallas_call(
        store_kernel,
        out_shape=tuple(jax.ShapeDtypeStruct(v.shape, v.dtype) for v in (residual_out, normed, delivered)),
        in_specs=[anywhere] + [vmem] * 3,
        out_specs=(anywhere,) * 3,
        scratch_shapes=[
            pltpu.SMEM((64,), jnp.int32),
            pltpu.VMEM((2, WIDTH, 256), jnp.bfloat16),
            pltpu.SemaphoreType.DMA((REQ, 4)),
            pltpu.SemaphoreType.DMA((3,)),
        ],
        compiler_params=pltpu.CompilerParams(vmem_limit_bytes=20 * 1024 * 1024),
        cost_estimate=pl.CostEstimate(flops=0, bytes_accessed=6_000_000, transcendentals=0),
    )(
        pltpu.with_memory_space_constraint(owner, pltpu.HBM),
        *(pltpu.with_memory_space_constraint(v, pltpu.VMEM) for v in (residual_out, normed, delivered)),
    )


def per_device(queries, cache_kv, new_kv, ctx_len, new_len, owner, wo, hidden_in, norm_gain):
    residual_out, normed, delivered = step(
        queries, cache_kv, new_kv, ctx_len, new_len, wo, hidden_in, norm_gain
    )
    return store(owner, residual_out, normed, delivered)


def solution(mesh):
    in_specs = (
        P("tp", None, None, None),
        P("tp", None, "seq", None),
        P("tp", None, "seq", None),
        P(),
        P(),
        P(),
        P(("seq", "tp"), None),
        P(None, ("seq", "tp")),
        P(("seq", "tp")),
    )
    out_specs = (P(None, ("seq", "tp")), P(None, ("seq", "tp")), P("tp", None, "seq", None))
    return jax.shard_map(
        per_device, mesh=mesh, in_specs=in_specs, out_specs=out_specs, check_vma=False
    )
```

```python
import functools

import jax
import jax.numpy as jnp
from jax import lax
from jax.experimental import pallas as pl
from jax.experimental.pallas import tpu as pltpu
from jax.sharding import PartitionSpec as P

D = 16384
HD = 128
KVH = 8
GROUP = 16
REQ = 4
WIDTH = 256
SHARE = 32
KEYS = WIDTH + SHARE
NEG = -1e30
MESH = pl.DeviceIdType.MESH


def remote(src, dst, send, recv, device):
    return pltpu.make_async_remote_copy(
        src_ref=src, dst_ref=dst, send_sem=send, recv_sem=recv, device_id=device, device_id_type=MESH
    )


def kernel(
    ctx_hbm, new_hbm, q_hbm, cache_hbm, newkv_hbm, wo_hbm, hidden_hbm, gain_hbm,
    res_ref, norm_ref, got,
    ctx_s, new_s, q_v, kv, w_v, hid_v, gain_v,
    osend, orecv, csend, crecv,
    a_send, b_send, e_send, a_recv, b_recv, e_recv, a2_send, b2_send, e2_send, a2_recv, b2_recv, e2_recv,
    n_send, n_recv, rows_v,
    loc_sem, kv_sem, wl_sem, ws_sem, wr_sem,
    os_sem, or_sem, cs_sem, cr_sem,
    r1s_sem, r1r_sem, e1s_sem, e1r_sem, r2s_sem, r2r_sem, ns_sem, nr_sem,
    gs_sem, gr_sem, ps_sem, pr_sem,
):
    s = lax.axis_index("seq")
    t = lax.axis_index("tp")
    y, c = s // 2, s % 2
    x, z = t // 4, t % 4
    me = s * 16 + t
    sp = y * 2 + (1 - c)

    def seq_peer(i):
        return (s + 1 + i) & 7

    def tp_peer(i):
        return ((x + 2 - (i & 3)) & 3) * 4 + ((z + 2 - (i >> 2)) & 3)

    def any_peer(i):
        far = (y + 2 - ((i >> 5) & 3)) & 3
        core = c ^ (1 - (i & 1))
        return far * 2 + core, ((x + 2 - ((i >> 1) & 3)) & 3) * 4 + ((z + 2 - ((i >> 3) & 3)) & 3)

    def y_at(d):
        return lax.rem(y + d, 4) * 2 + c

    def x_at(d):
        return lax.rem(x + d, 4) * 4 + z

    def z_at(d):
        return x * 4 + lax.rem(z + d, 4)

    drains = []

    def others(count, own, send):
        lax.fori_loop(0, own, send, 0)
        lax.fori_loop(own + 1, count, send, 0)

    loads = [
        pltpu.make_async_copy(src, dst, loc_sem.at[i])
        for i, (src, dst) in enumerate(
            [(ctx_hbm, ctx_s), (new_hbm, new_s), (q_hbm, q_v), (hidden_hbm, hid_v), (gain_hbm, gain_v)]
        )
    ]

    def kv_copies(r):
        return (
            pltpu.make_async_copy(cache_hbm.at[r], kv.at[r, :, pl.ds(0, WIDTH), :], kv_sem.at[r, 0]),
            pltpu.make_async_copy(newkv_hbm.at[r], kv.at[r, :, pl.ds(WIDTH, SHARE), :], kv_sem.at[r, 1]),
        )

    for load in loads[:3]:
        load.start()
    for r in range(REQ):
        for copy in kv_copies(r):
            copy.start()
    for load in loads[3:]:
        load.start()

    barrier = pltpu.get_barrier_semaphore()

    def greet(i, _):
        pl.semaphore_signal(barrier, inc=1, device_id=any_peer(i), device_id_type=MESH)
        return 0

    others(128, 85, greet)

    def w_local(j):
        return pltpu.make_async_copy(
            wo_hbm.at[:, pl.ds(pl.multiple_of(j * 4096 + c * 2048, 2048), 2048)],
            w_v.at[j, pl.ds(pl.multiple_of(c * 128, 128), 128), :],
            wl_sem.at[j],
        )

    def w_remote(j):
        return remote(
            wo_hbm.at[:, pl.ds(pl.multiple_of(j * 4096 + (1 - c) * 2048, 2048), 2048)],
            w_v.at[j, pl.ds(pl.multiple_of(c * 128, 128), 128), :],
            ws_sem.at[j], wr_sem.at[j], (sp, t),
        )

    for j in range(4):
        w_local(j).start()

    def block(r, who):
        return got.at[r, :, pl.ds(pl.multiple_of(who * SHARE, SHARE), SHARE), :]

    def request(way, n):
        return n if way == 0 else REQ - 1 - n

    def source(way):
        return y_at(3 if way == 0 else 1)

    def ring(way, n, slot, who):
        here = block(request(way, n), who)
        return remote(
            here, here, gs_sem.at[way, slot], gr_sem.at[way, slot], (y_at(1 if way == 0 else 3), t)
        )

    def first(way, n):
        return ring(way, n, n, s)

    def second(way, n):
        return ring(way, n, REQ + n, source(way))

    def pair(way, n, slot, who):
        here = block(request(way, n), who)
        return remote(here, here, ps_sem.at[way, slot], pr_sem.at[way, slot], (sp, t))

    def pair_own(n):
        return pair(0, n, n, s)

    def pair_near(way, n):
        return pair(way, n, REQ + n, source(way))

    def pair_far(way, n):
        return pair(way, n, 2 * REQ + n, y_at(2))

    def start_first(*steps):
        for n in steps:
            for way in range(2):
                first(way, n).start()

    def start_second(*steps):
        for n in steps:
            for way in range(2):
                first(way, n).wait_recv()
                second(way, n).start()
                pair_near(way, n).start()

    def start_near(*steps):
        for n in steps:
            for way in range(2):
                first(way, n).wait_recv()
                pair_near(way, n).start()

    def start_far():
        for n in range(2):
            for way in range(2):
                second(way, n).wait_recv()
                pair_far(way, n).start()

    col = lax.broadcasted_iota(jnp.int32, (KVH * GROUP, KEYS), 1)
    lane = lax.broadcasted_iota(jnp.int32, (KVH * GROUP, 128), 1)

    def attend(r, stats):
        for copy in kv_copies(r):
            copy.wait()
        live_ctx = jnp.minimum(ctx_s[t * REQ + r] - s * WIDTH, WIDTH)
        live_new = new_s[t * REQ + r] - s * SHARE + WIDTH
        mask = (col < live_ctx) | ((col >= WIDTH) & (col < live_new))
        scores = jnp.concatenate(
            [
                lax.dot_general(
                    q_v[r, h], kv[r, h, :, :HD], (((1,), (1,)), ((), ())), preferred_element_type=jnp.float32
                )
                for h in range(KVH)
            ],
            axis=0,
        ) * HD ** (-0.5)
        scores = jnp.where(mask, scores, NEG)
        top = jnp.max(scores, axis=1, keepdims=True)
        weights = jnp.where(mask, jnp.exp(scores - top), 0.0)
        total = jnp.maximum(jnp.sum(weights, axis=1, keepdims=True), 1e-30)
        weights = weights.astype(jnp.bfloat16)
        inverse = 1.0 / total
        for h in range(KVH):
            rows = slice(h * GROUP, (h + 1) * GROUP)
            out = jnp.dot(weights[rows], kv[r, h, :, HD:], preferred_element_type=jnp.float32)
            osend[h, r * GROUP:(r + 1) * GROUP, :] = (out * inverse[rows]).astype(jnp.bfloat16)
        return jnp.where(lane == r, top + jnp.log(total), stats)

    def rows_of(part):
        return pl.ds(0, 32) if part == 0 else pl.ds(32, 48)

    def o_copy(k, part):
        return remote(
            osend.at[k, rows_of(part)], orecv.at[s, rows_of(part)], os_sem.at[part], or_sem.at[part], (k, t)
        )

    def o_own(part):
        return pltpu.make_async_copy(
            osend.at[s, rows_of(part)], orecv.at[s, rows_of(part)], or_sem.at[part]
        )

    def send_o(part):
        o_own(part).start()

        def one(i, _):
            o_copy(seq_peer(i), part).start()
            return 0

        lax.fori_loop(0, 7, one, 0)

    def wait_o(part):
        everything = orecv.at[:, rows_of(part)]
        pltpu.make_async_copy(everything, everything, or_sem.at[part]).wait()

    def drain_o():
        for part in range(2):
            sent = osend.at[pl.ds(0, 7), rows_of(part)]
            pltpu.make_async_copy(sent, sent, os_sem.at[part]).wait()

    for load in loads[:3]:
        load.wait()
    stats = jnp.zeros((KVH * GROUP, 128), jnp.float32)
    stats = attend(0, stats)
    stats = attend(1, stats)
    pl.semaphore_wait(barrier, 127)
    drains.append(drain_o)
    send_o(0)
    for j in range(4):
        w_remote(j).start()
    stats = attend(2, stats)
    stats = attend(3, stats)
    high = stats.astype(jnp.bfloat16).astype(jnp.float32)
    middle = (stats - high).astype(jnp.bfloat16).astype(jnp.float32)
    low = stats - high - middle
    pieces = (high + pltpu.roll(middle, 4, 1) + pltpu.roll(low, 8, 1)).astype(jnp.bfloat16)
    for h in range(KVH):
        osend[h, 64:80, :] = pieces[h * GROUP:(h + 1) * GROUP]
    send_o(1)

    slot = lax.broadcasted_iota(jnp.int32, (SHARE, 256), 0)
    for r in range(REQ):
        live = slot < new_s[t * REQ + r] - s * SHARE
        for h in range(KVH):
            got[r, h, pl.ds(pl.multiple_of(s * SHARE, SHARE), SHARE), :] = jnp.where(
                live, kv[r, h, WIDTH:, :], jnp.zeros((), jnp.bfloat16)
            )

    start_first(0, 1, 2)
    for n in range(REQ):
        pair_own(n).start()

    def drain_gather():
        for n in range(REQ):
            pair_own(n).wait()
            for way in range(2):
                first(way, n).wait_send()
                pair_near(way, n).wait()
                if n < 2:
                    second(way, n).wait_send()
                    pair_far(way, n).wait()

    def drain_w():
        for j in range(4):
            w_remote(j).wait_send()

    drains.append(drain_gather)
    drains.append(drain_w)

    wait_o(0)
    wait_o(1)

    tops = []
    for k in range(8):
        piece = orecv[k, 64:80, :].astype(jnp.float32)
        tops.append(piece + pltpu.roll(piece, 124, 1) + pltpu.roll(piece, 120, 1))
    top = functools.reduce(jnp.maximum, tops)
    exps = [jnp.exp(v - top) for v in tops]
    total = functools.reduce(jnp.add, exps)
    shares = [e / total for e in exps]
    for r in range(REQ):
        context = jnp.zeros((GROUP, HD), jnp.float32)
        for k in range(8):
            part = orecv[k, r * GROUP:(r + 1) * GROUP, :].astype(jnp.float32)
            context = context + part * shares[k][:, r:r + 1]
        csend[:, r, :] = context

    def c_copy(core, g):
        return remote(
            csend.at[g], crecv.at[c, t], cs_sem.at[0], cr_sem.at[0], (y * 2 + core, g)
        )

    def send_c(i, _):
        g = tp_peer(i)
        c_copy(c, g).start()
        c_copy(1 - c, g).start()
        return 0

    def drain_c():
        for sent in (csend, csend.at[pl.ds(0, 15)]):
            pltpu.make_async_copy(sent, sent, cs_sem.at[0]).wait()

    drains.append(drain_c)
    others(16, 10, send_c)
    c_copy(1 - c, t).start()
    pltpu.make_async_copy(csend.at[t], crecv.at[c, t], cr_sem.at[0]).start()
    for j in range(4):
        w_local(j).wait()
        w_remote(j).wait_recv()
    pltpu.make_async_copy(crecv, crecv, cr_sem.at[0]).wait()

    flat = jnp.concatenate(
        [
            jnp.concatenate([crecv[core, :, r, :] for r in range(REQ)], axis=0)
            for core in range(2)
        ],
        axis=1,
    ).astype(jnp.bfloat16)

    def r1_copy(way, d, part):
        dst = ((x if way == 0 else z) + d) & 3
        src = (a_send if way == 0 else b_send).at[dst, part]
        to = (a_recv if way == 0 else b_recv).at[d - 1, part]
        return remote(
            src, to, r1s_sem.at[way, d - 1, part], r1r_sem.at[way, d - 1, part],
            (s, x_at(d) if way == 0 else z_at(d)),
        )

    def e1_copy(d):
        return remote(
            e_send.at[(y + d) & 3], e_recv.at[d - 1], e1s_sem.at[d - 1], e1r_sem.at[d - 1], (y_at(d), t)
        )

    def project(j):
        for i in range(4):
            piece = jnp.dot(flat, w_v[j, :, i * 512:(i + 1) * 512], preferred_element_type=jnp.float32)
            a_send[i, j] = piece[:24].astype(jnp.bfloat16)
            middle = piece[24:48].astype(jnp.bfloat16)
            for k in range(4):
                b_send[k, j, :, i * 128:(i + 1) * 128] = middle[:, k * 128:(k + 1) * 128]
            e_send[j, :, i * 512:(i + 1) * 512] = piece[48:].astype(jnp.bfloat16)

    def drain_r1():
        for d in range(1, 4):
            e1_copy(d).wait_send()
            for way in range(2):
                for part in range(4):
                    r1_copy(way, d, part).wait_send()

    drains.append(drain_r1)
    turns = (2, 1, 3, 0)
    for turn in turns:
        part = (y + turn) & 3
        project(part)
        if turn:
            e1_copy(turn).start()
        for d in (2, 1, 3):
            for way in range(2):
                r1_copy(way, d, part).start()

    start_first(3)
    def r2_copy(way, j, k):
        send, recv = ((a2_send, a2_recv), (b2_send, b2_recv), (e2_send, e2_recv))[way]
        if way == 2:
            slot, device = (x, z), (s, j * 4 + k)
        else:
            slot = (y, z if way == 0 else x)
            device = (j * 2 + c, x * 4 + k if way == 0 else k * 4 + z)
        return remote(send.at[j, k], recv.at[slot], r2s_sem.at[way], r2r_sem.at[way], device)

    def send_r2(way, j, k):
        send, recv = ((a2_send, a2_recv), (b2_send, b2_recv), (e2_send, e2_recv))[way]
        mine = ((y, z), (y, x), (x, z))[way]
        away = (j != mine[0]) | (k != mine[1])

        @pl.when(away)
        def _():
            r2_copy(way, j, k).start()

        @pl.when(jnp.logical_not(away))
        def _():
            pltpu.make_async_copy(send.at[j, k], recv.at[j, k], r2r_sem.at[way]).start()

    def drain_r2():
        for way in range(3):
            send = (a2_send, b2_send, e2_send)[way]
            for sent in (send.at[pl.ds(0, 3)], send.at[0, pl.ds(0, 3)]):
                pltpu.make_async_copy(sent, sent, r2s_sem.at[way]).wait()

    def add_e():
        for d in (1, 3, 2):
            e1_copy(d).wait_recv()
        for j in (2, 1, 3, 0):
            cols = slice(j * 512, (j + 1) * 512)
            out = e_send[y, :, cols].astype(jnp.float32)
            for d in range(3):
                out = out + e_recv[d, :, cols].astype(jnp.float32)
            out = out.astype(jnp.bfloat16)
            for k in range(4):
                e2_send[j, k] = out[:, k * 128:(k + 1) * 128]
            for k in range(4):
                send_r2(2, j, k)

    drains.append(drain_r2)
    for turn in turns:
        part = (y + turn) & 3
        for way in range(2):
            for d in (1, 3, 2):
                r1_copy(way, d, part).wait_recv()
            send, recv, nxt = ((a_send, a_recv, a2_send), (b_send, b_recv, b2_send))[way]
            out = send[x if way == 0 else z, part].astype(jnp.float32)
            for d in range(3):
                out = out + recv[d, part].astype(jnp.float32)
            out = out.astype(jnp.bfloat16)
            for k in range(4):
                nxt[part, k] = out[:, k * 128:(k + 1) * 128]
            for k in range(4):
                send_r2(way, part, k)
        if turn == 3:
            add_e()

    start_second(0, 1)

    for load in loads[3:]:
        load.wait()
    rows_v[...] = hid_v[...].astype(jnp.float32)
    stream = jnp.concatenate([rows_v[pl.ds(r, 16, stride=REQ), :] for r in range(REQ)], axis=0)
    start_near(2, 3)
    sums = []
    for way in range(3):
        recv = (a2_recv, b2_recv, e2_recv)[way]
        pltpu.make_async_copy(recv, recv, r2r_sem.at[way]).wait()
        out = recv[0, 0].astype(jnp.float32)
        for i in range(1, 16):
            out = out + recv[i // 4, i % 4].astype(jnp.float32)
        sums.append(out)
    stream = stream + jnp.concatenate(sums, axis=0)

    squares = stream * stream
    n_send[...] = jnp.sum(jnp.concatenate([squares, squares], axis=0).T, axis=0, keepdims=True)

    def send_n(i, _):
        pltpu.make_async_remote_copy(
            src_ref=n_send, dst_ref=n_recv.at[me], send_sem=ns_sem.at[0], recv_sem=nr_sem.at[0],
            device_id=any_peer(i), device_id_type=MESH,
        ).start()
        return 0

    def drain_n():
        sent = n_recv.at[pl.ds(0, 127)]
        pltpu.make_async_copy(sent, sent, ns_sem.at[0]).wait()

    others(128, 85, send_n)
    pltpu.make_async_copy(n_send, n_recv.at[me], nr_sem.at[0]).start()
    for r in range(REQ):
        rows_v[pl.ds(r, 16, stride=REQ), :] = stream[r * 16:(r + 1) * 16]
    res_ref[...] = rows_v[...].astype(jnp.bfloat16)

    start_far()
    scaled = stream * gain_v[...]
    for drain in drains:
        drain()
    pltpu.make_async_copy(n_recv, n_recv, nr_sem.at[0]).wait()
    scale = lax.rsqrt(jnp.sum(n_recv[...], axis=0) / D + 1e-05)
    scale = jnp.broadcast_to(scale, (128, 128)).T[:64]
    normed = scaled * scale
    for r in range(REQ):
        rows_v[pl.ds(r, 16, stride=REQ), :] = normed[r * 16:(r + 1) * 16]
    norm_ref[...] = rows_v[...].astype(jnp.bfloat16)
    drain_n()


def step(queries, cache_kv, new_kv, ctx_len, new_len, wo, hidden_in, norm_gain):
    bf, f32 = jnp.bfloat16, jnp.float32
    dma = pltpu.SemaphoreType.DMA
    anywhere = pl.BlockSpec(memory_space=pl.ANY)
    vmem = pl.BlockSpec(memory_space=pltpu.VMEM)
    V = pltpu.VMEM
    return pl.pallas_call(
        kernel,
        out_shape=(
            V((64, 128), bf),
            V((64, 128), bf),
            V((REQ, KVH, WIDTH, 256), bf),
        ),
        in_specs=[anywhere] * 8,
        out_specs=(vmem, vmem, vmem),
        scratch_shapes=[
            pltpu.SMEM((64,), jnp.int32), pltpu.SMEM((64,), jnp.int32),
            V((REQ, KVH, GROUP, HD), bf),
            V((REQ, KVH, KEYS, 256), bf),
            V((4, 256, 2048), bf),
            V((64, 128), bf),
            V((1, 128), f32),
            V((8, 80, HD), bf), V((8, 80, HD), bf),
            V((16, REQ, HD), f32), V((2, 16, REQ, HD), f32),
            V((4, 4, 24, 512), bf), V((4, 4, 24, 512), bf), V((4, 16, 2048), bf),
            V((3, 4, 24, 512), bf), V((3, 4, 24, 512), bf), V((3, 16, 2048), bf),
            V((4, 4, 24, 128), bf), V((4, 4, 24, 128), bf), V((4, 4, 16, 128), bf),
            V((4, 4, 24, 128), bf), V((4, 4, 24, 128), bf), V((4, 4, 16, 128), bf),
            V((1, 128), f32), V((128, 1, 128), f32),
            V((64, 128), f32),
            dma((5,)), dma((REQ, 2)), dma((4,)), dma((4,)), dma((4,)),
            dma((2,)), dma((2,)), dma((1,)), dma((1,)),
            dma((2, 3, 4)), dma((2, 3, 4)), dma((3,)), dma((3,)), dma((3,)), dma((3,)), dma((1,)), dma((1,)),
            dma((2, 6)), dma((2, 6)), dma((2, 10)), dma((2, 10)),
        ],
        compiler_params=pltpu.CompilerParams(
            collective_id=0, has_side_effects=True, vmem_limit_bytes=40 * 1024 * 1024
        ),
        cost_estimate=pl.CostEstimate(flops=600_000_000, bytes_accessed=14_000_000, transcendentals=1_000_000),
    )(
        *(
            pltpu.with_memory_space_constraint(v, pltpu.HBM)
            for v in (ctx_len, new_len, queries, cache_kv, new_kv, wo, hidden_in, norm_gain.reshape(1, 128))
        )
    )


def store_kernel(
    owner_hbm, res_in, norm_in, deliv_ref, res_hbm, norm_hbm, app_hbm,
    owner_ref, zeros, out_sem, sem,
):
    s = lax.axis_index("seq")
    t = lax.axis_index("tp")

    def blank(r, i):
        return pltpu.make_async_copy(zeros, app_hbm.at[r, pl.ds(i * 2, 2)], out_sem.at[r, i])

    def put(r, i):
        part = pl.ds(i * 2, 2)
        return pltpu.make_async_copy(deliv_ref.at[r, part], app_hbm.at[r, part], out_sem.at[r, i])

    def mine(r):
        return owner_ref[t * REQ + r] == s

    who = pltpu.make_async_copy(owner_hbm, owner_ref, sem.at[2])
    who.start()
    small = (
        pltpu.make_async_copy(res_in, res_hbm, sem.at[0]),
        pltpu.make_async_copy(norm_in, norm_hbm, sem.at[1]),
    )
    for copy in small:
        copy.start()
    zeros[...] = jnp.zeros_like(zeros)
    who.wait()
    for r in range(REQ):
        @pl.when(mine(r))
        def _():
            for i in range(4):
                put(r, i).start()

    for r in range(REQ):
        @pl.when(jnp.logical_not(mine(r)))
        def _():
            for i in range(4):
                blank(r, i).start()

    for copy in small:
        copy.wait()
    for r in range(REQ):
        for i in range(4):
            put(r, i).wait()


def store(owner, residual_out, normed, delivered):
    anywhere = pl.BlockSpec(memory_space=pl.ANY)
    vmem = pl.BlockSpec(memory_space=pltpu.VMEM)
    return pl.pallas_call(
        store_kernel,
        out_shape=tuple(jax.ShapeDtypeStruct(v.shape, v.dtype) for v in (residual_out, normed, delivered)),
        in_specs=[anywhere] + [vmem] * 3,
        out_specs=(anywhere,) * 3,
        scratch_shapes=[
            pltpu.SMEM((64,), jnp.int32),
            pltpu.VMEM((2, WIDTH, 256), jnp.bfloat16),
            pltpu.SemaphoreType.DMA((REQ, 4)),
            pltpu.SemaphoreType.DMA((3,)),
        ],
        compiler_params=pltpu.CompilerParams(vmem_limit_bytes=20 * 1024 * 1024),
        cost_estimate=pl.CostEstimate(flops=0, bytes_accessed=6_000_000, transcendentals=0),
    )(
        owner,
        *(pltpu.with_memory_space_constraint(v, pltpu.VMEM) for v in (residual_out, normed, delivered)),
    )


def per_device(queries, cache_kv, new_kv, ctx_len, new_len, owner, wo, hidden_in, norm_gain):
    residual_out, normed, delivered = step(
        queries, cache_kv, new_kv, ctx_len, new_len, wo, hidden_in, norm_gain
    )
    return store(owner, residual_out, normed, delivered)


def solution(mesh):
    in_specs = (
        P("tp", None, None, None),
        P("tp", None, "seq", None),
        P("tp", None, "seq", None),
        P(),
        P(),
        P(),
        P(("seq", "tp"), None),
        P(None, ("seq", "tp")),
        P(("seq", "tp")),
    )
    out_specs = (P(None, ("seq", "tp")), P(None, ("seq", "tp")), P("tp", None, "seq", None))
    return jax.shard_map(
        per_device, mesh=mesh, in_specs=in_specs, out_specs=out_specs, check_vma=False
    )
```

```python
import functools

import jax
import jax.numpy as jnp
from jax import lax
from jax.experimental import pallas as pl
from jax.experimental.pallas import tpu as pltpu
from jax.sharding import PartitionSpec as P

D = 16384
HD = 128
KVH = 8
GROUP = 16
REQ = 4
WIDTH = 256
SHARE = 32
KEYS = WIDTH + SHARE
NEG = -1e30
LOG2E = 1.4426950408889634
MESH = pl.DeviceIdType.MESH


def remote(src, dst, send, recv, device):
    return pltpu.make_async_remote_copy(
        src_ref=src, dst_ref=dst, send_sem=send, recv_sem=recv, device_id=device, device_id_type=MESH
    )


def kernel(
    ctx_hbm, new_hbm, q_hbm, cache_hbm, newkv_hbm, wo_hbm, hidden_hbm, gain_hbm,
    res_ref, norm_ref, got,
    ctx_s, new_s, q_v, kv, w_v, hid_v, gain_v,
    osend, orecv, csend, crecv,
    a_send, b_send, e_send, a_recv, b_recv, e_recv, a2_send, b2_send, e2_send, a2_recv, b2_recv, e2_recv,
    n_send, n_recv, rows_v,
    loc_sem, kv_sem, wl_sem, ws_sem, wr_sem,
    os_sem, or_sem, cs_sem, cr_sem,
    r1s_sem, r1r_sem, e1s_sem, e1r_sem, r2s_sem, r2r_sem, ns_sem, nr_sem,
    gs_sem, gr_sem, ps_sem, pr_sem,
):
    s = lax.axis_index("seq")
    t = lax.axis_index("tp")
    y, c = s // 2, s % 2
    x, z = t // 4, t % 4
    me = s * 16 + t
    sp = y * 2 + (1 - c)

    def seq_peer(i):
        return (s + 1 + i) & 7

    def tp_peer(i):
        return ((x + 2 - (i & 3)) & 3) * 4 + ((z + 2 - (i >> 2)) & 3)

    def any_peer(i):
        far = (y + 2 - ((i >> 5) & 3)) & 3
        core = c ^ (1 - (i & 1))
        return far * 2 + core, ((x + 2 - ((i >> 1) & 3)) & 3) * 4 + ((z + 2 - ((i >> 3) & 3)) & 3)

    def y_at(d):
        return lax.rem(y + d, 4) * 2 + c

    def x_at(d):
        return lax.rem(x + d, 4) * 4 + z

    def z_at(d):
        return x * 4 + lax.rem(z + d, 4)

    drains = []

    def others(count, own, send):
        lax.fori_loop(0, own, send, 0)
        lax.fori_loop(own + 1, count, send, 0)

    barrier = pltpu.get_barrier_semaphore()

    def greet(device):
        pl.semaphore_signal(barrier, inc=1, device_id=device, device_id_type=MESH)

    def greet_tp(i, _):
        greet((sp, tp_peer(i)))
        greet((s, tp_peer(i)))
        return 0

    def greet_seq(i, _):
        greet((seq_peer(i), t))
        return 0

    others(16, 10, greet_tp)
    lax.fori_loop(0, 7, greet_seq, 0)

    loads = [
        pltpu.make_async_copy(src, dst, loc_sem.at[i])
        for i, (src, dst) in enumerate(
            [(ctx_hbm, ctx_s), (new_hbm, new_s), (q_hbm, q_v), (hidden_hbm, hid_v), (gain_hbm, gain_v)]
        )
    ]

    def kv_copies(r):
        return (
            pltpu.make_async_copy(cache_hbm.at[r], kv.at[r, :, pl.ds(0, WIDTH), :], kv_sem.at[r, 0]),
            pltpu.make_async_copy(newkv_hbm.at[r], kv.at[r, :, pl.ds(WIDTH, SHARE), :], kv_sem.at[r, 1]),
        )

    for load in loads[:3]:
        load.start()
    for r in range(2):
        for copy in kv_copies(r):
            copy.start()

    for r in range(2, REQ):
        for copy in kv_copies(r):
            copy.start()
    for load in loads[3:]:
        load.start()

    def w_local(j):
        return pltpu.make_async_copy(
            wo_hbm.at[:, pl.ds(pl.multiple_of(j * 4096 + c * 2048, 2048), 2048)],
            w_v.at[j, pl.ds(pl.multiple_of(c * 128, 128), 128), :],
            wl_sem.at[j],
        )

    def w_remote(j):
        return remote(
            wo_hbm.at[:, pl.ds(pl.multiple_of(j * 4096 + (1 - c) * 2048, 2048), 2048)],
            w_v.at[j, pl.ds(pl.multiple_of(c * 128, 128), 128), :],
            ws_sem.at[j], wr_sem.at[j], (sp, t),
        )

    for j in range(4):
        w_local(j).start()

    def block(r, who):
        return got.at[r, :, pl.ds(pl.multiple_of(who * SHARE, SHARE), SHARE), :]

    def request(way, n):
        return n if way == 0 else REQ - 1 - n

    def source(way):
        return y_at(3 if way == 0 else 1)

    def ring(way, n, slot, who):
        here = block(request(way, n), who)
        return remote(
            here, here, gs_sem.at[way, slot], gr_sem.at[way, slot], (y_at(1 if way == 0 else 3), t)
        )

    def first(way, n):
        return ring(way, n, n, s)

    def second(way, n):
        return ring(way, n, REQ + n, source(way))

    def pair(way, n, slot, who):
        here = block(request(way, n), who)
        return remote(here, here, ps_sem.at[way, slot], pr_sem.at[way, slot], (sp, t))

    def pair_own(n):
        return pair(0, n, n, s)

    def pair_near(way, n):
        return pair(way, n, REQ + n, source(way))

    def pair_far(way, n):
        return pair(way, n, 2 * REQ + n, y_at(2))

    def start_first(*steps):
        for n in steps:
            for way in range(2):
                first(way, n).start()

    def start_second(*steps):
        for n in steps:
            for way in range(2):
                first(way, n).wait_recv()
                second(way, n).start()
                pair_near(way, n).start()

    def start_near(*steps):
        for n in steps:
            for way in range(2):
                first(way, n).wait_recv()
                pair_near(way, n).start()

    def start_far():
        for n in range(2):
            for way in range(2):
                second(way, n).wait_recv()
                pair_far(way, n).start()

    col = lax.broadcasted_iota(jnp.int32, (1, KEYS), 1)
    lane = lax.broadcasted_iota(jnp.int32, (KVH * GROUP, 128), 1)

    def attend(pair_of, stats):
        scores = []
        for r in pair_of:
            for copy in kv_copies(r):
                copy.wait()
        for r in pair_of:
            live_ctx = jnp.minimum(ctx_s[t * REQ + r] - s * WIDTH, WIDTH)
            live_new = new_s[t * REQ + r] - s * SHARE + WIDTH
            bias = jnp.where((col < live_ctx) | ((col >= WIDTH) & (col < live_new)), 0.0, NEG)
            for h in range(KVH):
                scores.append(
                    lax.dot_general(
                        q_v[r, h], kv[r, h, :, :HD], (((1,), (1,)), ((), ())), preferred_element_type=jnp.float32
                    )
                    + bias
                )
        scores = jnp.concatenate(scores, axis=0)
        top = jnp.maximum(jnp.max(scores, axis=1, keepdims=True), 0.1 * NEG)
        weights = jnp.exp2((scores - top) * (HD ** (-0.5) * LOG2E))
        total = jnp.maximum(jnp.sum(weights, axis=1, keepdims=True), 1e-30)
        weights = weights.astype(jnp.bfloat16)
        out = jnp.concatenate(
            [
                jnp.dot(
                    weights[(i * KVH + h) * GROUP:(i * KVH + h + 1) * GROUP],
                    kv[r, h, :, HD:],
                    preferred_element_type=jnp.float32,
                )
                for i, r in enumerate(pair_of)
                for h in range(KVH)
            ],
            axis=0,
        )
        out = (out * (1.0 / total)).astype(jnp.bfloat16)
        log_total = top * HD ** (-0.5) + jnp.log(total)
        for i, r in enumerate(pair_of):
            for h in range(KVH):
                first_row = (i * KVH + h) * GROUP
                osend[h, r * GROUP:(r + 1) * GROUP, :] = out[first_row:first_row + GROUP]
            stats = jnp.where(lane == r, log_total[i * KVH * GROUP:(i + 1) * KVH * GROUP], stats)
        return stats

    def rows_of(part):
        return pl.ds(0, 32) if part == 0 else pl.ds(32, 48)

    def o_copy(k, part):
        return remote(
            osend.at[k, rows_of(part)], orecv.at[s, rows_of(part)], os_sem.at[part], or_sem.at[part], (k, t)
        )

    def o_own(part):
        return pltpu.make_async_copy(
            osend.at[s, rows_of(part)], orecv.at[s, rows_of(part)], or_sem.at[part]
        )

    def send_o(part):
        o_own(part).start()

        def one(i, _):
            o_copy(seq_peer(i), part).start()
            return 0

        lax.fori_loop(0, 7, one, 0)

    def wait_o(part):
        everything = orecv.at[:, rows_of(part)]
        pltpu.make_async_copy(everything, everything, or_sem.at[part]).wait()

    def drain_o():
        for part in range(2):
            sent = osend.at[pl.ds(0, 7), rows_of(part)]
            pltpu.make_async_copy(sent, sent, os_sem.at[part]).wait()

    for load in loads[:3]:
        load.wait()
    stats = jnp.zeros((KVH * GROUP, 128), jnp.float32)
    stats = attend((0, 1), stats)
    pl.semaphore_wait(barrier, 37)
    drains.append(drain_o)
    send_o(0)
    for j in range(4):
        w_remote(j).start()
    stats = attend((2, 3), stats)
    high = stats.astype(jnp.bfloat16).astype(jnp.float32)
    middle = (stats - high).astype(jnp.bfloat16).astype(jnp.float32)
    low = stats - high - middle
    pieces = (high + pltpu.roll(middle, 4, 1) + pltpu.roll(low, 8, 1)).astype(jnp.bfloat16)
    for h in range(KVH):
        osend[h, 64:80, :] = pieces[h * GROUP:(h + 1) * GROUP]
    send_o(1)

    slot = lax.broadcasted_iota(jnp.int32, (SHARE, 256), 0)
    for r in range(REQ):
        live = slot < new_s[t * REQ + r] - s * SHARE
        for h in range(KVH):
            got[r, h, pl.ds(pl.multiple_of(s * SHARE, SHARE), SHARE), :] = jnp.where(
                live, kv[r, h, WIDTH:, :], jnp.zeros((), jnp.bfloat16)
            )

    start_first(0, 1, 2)
    for n in range(REQ):
        pair_own(n).start()

    def drain_gather():
        for n in range(REQ):
            pair_own(n).wait()
            for way in range(2):
                first(way, n).wait_send()
                pair_near(way, n).wait()
                if n < 2:
                    second(way, n).wait_send()
                    pair_far(way, n).wait()

    def drain_w():
        for j in range(4):
            w_remote(j).wait_send()

    drains.append(drain_gather)
    drains.append(drain_w)

    wait_o(0)
    wait_o(1)

    tops = []
    for k in range(8):
        piece = orecv[k, 64:80, :].astype(jnp.float32)
        tops.append(piece + pltpu.roll(piece, 124, 1) + pltpu.roll(piece, 120, 1))
    top = functools.reduce(jnp.maximum, tops)
    exps = [jnp.exp(v - top) for v in tops]
    total = functools.reduce(jnp.add, exps)
    shares = [e / total for e in exps]
    for r in range(REQ):
        context = jnp.zeros((GROUP, HD), jnp.float32)
        for k in range(8):
            part = orecv[k, r * GROUP:(r + 1) * GROUP, :].astype(jnp.float32)
            context = context + part * shares[k][:, r:r + 1]
        csend[:, r, :] = context

    def c_copy(core, g):
        return remote(
            csend.at[g], crecv.at[c, t], cs_sem.at[0], cr_sem.at[0], (y * 2 + core, g)
        )

    def send_c(i, _):
        g = tp_peer(i)
        c_copy(c, g).start()
        c_copy(1 - c, g).start()
        return 0

    def drain_c():
        for sent in (csend, csend.at[pl.ds(0, 15)]):
            pltpu.make_async_copy(sent, sent, cs_sem.at[0]).wait()

    drains.append(drain_c)
    others(16, 10, send_c)
    c_copy(1 - c, t).start()
    pltpu.make_async_copy(csend.at[t], crecv.at[c, t], cr_sem.at[0]).start()
    for j in range(4):
        w_local(j).wait()
        w_remote(j).wait_recv()
    pltpu.make_async_copy(crecv, crecv, cr_sem.at[0]).wait()

    flat = jnp.concatenate(
        [
            jnp.concatenate([crecv[core, :, r, :] for r in range(REQ)], axis=0)
            for core in range(2)
        ],
        axis=1,
    ).astype(jnp.bfloat16)

    def r1_copy(way, d, part):
        dst = ((x if way == 0 else z) + d) & 3
        src = (a_send if way == 0 else b_send).at[dst, part]
        to = (a_recv if way == 0 else b_recv).at[d - 1, part]
        return remote(
            src, to, r1s_sem.at[way, d - 1, part], r1r_sem.at[way, d - 1, part],
            (s, x_at(d) if way == 0 else z_at(d)),
        )

    def e1_copy(d):
        return remote(
            e_send.at[(y + d) & 3], e_recv.at[d - 1], e1s_sem.at[d - 1], e1r_sem.at[d - 1], (y_at(d), t)
        )

    def project(j):
        for i in range(4):
            piece = jnp.dot(flat, w_v[j, :, i * 512:(i + 1) * 512], preferred_element_type=jnp.float32)
            a_send[i, j] = piece[:24].astype(jnp.bfloat16)
            middle = piece[24:48].astype(jnp.bfloat16)
            for k in range(4):
                b_send[k, j, :, i * 128:(i + 1) * 128] = middle[:, k * 128:(k + 1) * 128]
            e_send[j, :, i * 512:(i + 1) * 512] = piece[48:].astype(jnp.bfloat16)

    def drain_r1():
        for d in range(1, 4):
            e1_copy(d).wait_send()
            for way in range(2):
                for part in range(4):
                    r1_copy(way, d, part).wait_send()

    drains.append(drain_r1)
    turns = (2, 1, 3, 0)
    for turn in turns:
        part = (y + turn) & 3
        project(part)
        if turn:
            e1_copy(turn).start()
        for d in (2, 1, 3):
            for way in range(2):
                r1_copy(way, d, part).start()

    start_first(3)
    def r2_copy(way, j, k):
        send, recv = ((a2_send, a2_recv), (b2_send, b2_recv), (e2_send, e2_recv))[way]
        if way == 2:
            slot, device = (x, z), (s, j * 4 + k)
        else:
            slot = (y, z if way == 0 else x)
            device = (j * 2 + c, x * 4 + k if way == 0 else k * 4 + z)
        return remote(send.at[j, k], recv.at[slot], r2s_sem.at[way], r2r_sem.at[way], device)

    def send_r2(way, j, k):
        send, recv = ((a2_send, a2_recv), (b2_send, b2_recv), (e2_send, e2_recv))[way]
        mine = ((y, z), (y, x), (x, z))[way]
        away = (j != mine[0]) | (k != mine[1])

        @pl.when(away)
        def _():
            r2_copy(way, j, k).start()

        @pl.when(jnp.logical_not(away))
        def _():
            pltpu.make_async_copy(send.at[j, k], recv.at[j, k], r2r_sem.at[way]).start()

    def drain_r2():
        for way in range(3):
            send = (a2_send, b2_send, e2_send)[way]
            for sent in (send.at[pl.ds(0, 3)], send.at[0, pl.ds(0, 3)]):
                pltpu.make_async_copy(sent, sent, r2s_sem.at[way]).wait()

    def add_e():
        for d in (1, 3, 2):
            e1_copy(d).wait_recv()
        for j in (2, 1, 3, 0):
            cols = slice(j * 512, (j + 1) * 512)
            out = e_send[y, :, cols].astype(jnp.float32)
            for d in range(3):
                out = out + e_recv[d, :, cols].astype(jnp.float32)
            out = out.astype(jnp.bfloat16)
            for k in range(4):
                e2_send[j, k] = out[:, k * 128:(k + 1) * 128]
            for k in range(4):
                send_r2(2, j, k)

    drains.append(drain_r2)
    for turn in turns:
        part = (y + turn) & 3
        for way in range(2):
            for d in (1, 3, 2):
                r1_copy(way, d, part).wait_recv()
            send, recv, nxt = ((a_send, a_recv, a2_send), (b_send, b_recv, b2_send))[way]
            out = send[x if way == 0 else z, part].astype(jnp.float32)
            for d in range(3):
                out = out + recv[d, part].astype(jnp.float32)
            out = out.astype(jnp.bfloat16)
            for k in range(4):
                nxt[part, k] = out[:, k * 128:(k + 1) * 128]
            for k in range(4):
                send_r2(way, part, k)
        if turn == 3:
            add_e()

    start_second(0, 1)

    for load in loads[3:]:
        load.wait()
    rows_v[...] = hid_v[...].astype(jnp.float32)
    stream = jnp.concatenate([rows_v[pl.ds(r, 16, stride=REQ), :] for r in range(REQ)], axis=0)
    start_near(2, 3)
    sums = []
    for way in range(3):
        recv = (a2_recv, b2_recv, e2_recv)[way]
        pltpu.make_async_copy(recv, recv, r2r_sem.at[way]).wait()
        out = recv[0, 0].astype(jnp.float32)
        for i in range(1, 16):
            out = out + recv[i // 4, i % 4].astype(jnp.float32)
        sums.append(out)
    stream = stream + jnp.concatenate(sums, axis=0)

    squares = stream * stream
    n_send[...] = jnp.sum(jnp.concatenate([squares, squares], axis=0).T, axis=0, keepdims=True)

    def send_n(i, _):
        pltpu.make_async_remote_copy(
            src_ref=n_send, dst_ref=n_recv.at[me], send_sem=ns_sem.at[0], recv_sem=nr_sem.at[0],
            device_id=any_peer(i), device_id_type=MESH,
        ).start()
        return 0

    def drain_n():
        sent = n_recv.at[pl.ds(0, 127)]
        pltpu.make_async_copy(sent, sent, ns_sem.at[0]).wait()

    others(128, 85, send_n)
    pltpu.make_async_copy(n_send, n_recv.at[me], nr_sem.at[0]).start()
    for r in range(REQ):
        rows_v[pl.ds(r, 16, stride=REQ), :] = stream[r * 16:(r + 1) * 16]
    res_ref[...] = rows_v[...].astype(jnp.bfloat16)

    start_far()
    scaled = stream * gain_v[...]
    for drain in drains:
        drain()
    pltpu.make_async_copy(n_recv, n_recv, nr_sem.at[0]).wait()
    scale = lax.rsqrt(jnp.sum(n_recv[...], axis=0) / D + 1e-05)
    scale = jnp.broadcast_to(scale, (128, 128)).T[:64]
    normed = scaled * scale
    for r in range(REQ):
        rows_v[pl.ds(r, 16, stride=REQ), :] = normed[r * 16:(r + 1) * 16]
    norm_ref[...] = rows_v[...].astype(jnp.bfloat16)
    drain_n()


def step(queries, cache_kv, new_kv, ctx_len, new_len, wo, hidden_in, norm_gain):
    bf, f32 = jnp.bfloat16, jnp.float32
    dma = pltpu.SemaphoreType.DMA
    anywhere = pl.BlockSpec(memory_space=pl.ANY)
    vmem = pl.BlockSpec(memory_space=pltpu.VMEM)
    V = pltpu.VMEM
    return pl.pallas_call(
        kernel,
        out_shape=(
            V((64, 128), bf),
            V((64, 128), bf),
            V((REQ, KVH, WIDTH, 256), bf),
        ),
        in_specs=[anywhere] * 8,
        out_specs=(vmem, vmem, vmem),
        scratch_shapes=[
            pltpu.SMEM((64,), jnp.int32), pltpu.SMEM((64,), jnp.int32),
            V((REQ, KVH, GROUP, HD), bf),
            V((REQ, KVH, KEYS, 256), bf),
            V((4, 256, 2048), bf),
            V((64, 128), bf),
            V((1, 128), f32),
            V((8, 80, HD), bf), V((8, 80, HD), bf),
            V((16, REQ, HD), f32), V((2, 16, REQ, HD), f32),
            V((4, 4, 24, 512), bf), V((4, 4, 24, 512), bf), V((4, 16, 2048), bf),
            V((3, 4, 24, 512), bf), V((3, 4, 24, 512), bf), V((3, 16, 2048), bf),
            V((4, 4, 24, 128), bf), V((4, 4, 24, 128), bf), V((4, 4, 16, 128), bf),
            V((4, 4, 24, 128), bf), V((4, 4, 24, 128), bf), V((4, 4, 16, 128), bf),
            V((1, 128), f32), V((128, 1, 128), f32),
            V((64, 128), f32),
            dma((5,)), dma((REQ, 2)), dma((4,)), dma((4,)), dma((4,)),
            dma((2,)), dma((2,)), dma((1,)), dma((1,)),
            dma((2, 3, 4)), dma((2, 3, 4)), dma((3,)), dma((3,)), dma((3,)), dma((3,)), dma((1,)), dma((1,)),
            dma((2, 6)), dma((2, 6)), dma((2, 10)), dma((2, 10)),
        ],
        compiler_params=pltpu.CompilerParams(
            collective_id=0, has_side_effects=True, vmem_limit_bytes=40 * 1024 * 1024
        ),
        cost_estimate=pl.CostEstimate(flops=600_000_000, bytes_accessed=14_000_000, transcendentals=1_000_000),
    )(
        *(
            pltpu.with_memory_space_constraint(v, pltpu.HBM)
            for v in (ctx_len, new_len, queries, cache_kv, new_kv, wo, hidden_in, norm_gain.reshape(1, 128))
        )
    )


def store_kernel(
    owner_hbm, res_in, norm_in, deliv_ref, res_hbm, norm_hbm, app_hbm,
    owner_ref, zeros, out_sem, sem,
):
    s = lax.axis_index("seq")
    t = lax.axis_index("tp")

    def blank(r, i):
        return pltpu.make_async_copy(zeros, app_hbm.at[r, pl.ds(i * 2, 2)], out_sem.at[r, i])

    def put(r, i):
        part = pl.ds(i * 2, 2)
        return pltpu.make_async_copy(deliv_ref.at[r, part], app_hbm.at[r, part], out_sem.at[r, i])

    def mine(r):
        return owner_ref[t * REQ + r] == s

    who = pltpu.make_async_copy(owner_hbm, owner_ref, sem.at[2])
    who.start()
    small = (
        pltpu.make_async_copy(res_in, res_hbm, sem.at[0]),
        pltpu.make_async_copy(norm_in, norm_hbm, sem.at[1]),
    )
    for copy in small:
        copy.start()
    zeros[...] = jnp.zeros_like(zeros)
    who.wait()
    for r in range(REQ):
        @pl.when(mine(r))
        def _():
            for i in range(4):
                put(r, i).start()

    for r in range(REQ):
        @pl.when(jnp.logical_not(mine(r)))
        def _():
            for i in range(4):
                blank(r, i).start()

    for copy in small:
        copy.wait()
    for r in range(REQ):
        for i in range(4):
            put(r, i).wait()


def store(owner, residual_out, normed, delivered):
    anywhere = pl.BlockSpec(memory_space=pl.ANY)
    vmem = pl.BlockSpec(memory_space=pltpu.VMEM)
    return pl.pallas_call(
        store_kernel,
        out_shape=tuple(jax.ShapeDtypeStruct(v.shape, v.dtype) for v in (residual_out, normed, delivered)),
        in_specs=[anywhere] + [vmem] * 3,
        out_specs=(anywhere,) * 3,
        scratch_shapes=[
            pltpu.SMEM((64,), jnp.int32),
            pltpu.VMEM((2, WIDTH, 256), jnp.bfloat16),
            pltpu.SemaphoreType.DMA((REQ, 4)),
            pltpu.SemaphoreType.DMA((3,)),
        ],
        compiler_params=pltpu.CompilerParams(vmem_limit_bytes=20 * 1024 * 1024),
        cost_estimate=pl.CostEstimate(flops=0, bytes_accessed=6_000_000, transcendentals=0),
    )(
        owner,
        *(pltpu.with_memory_space_constraint(v, pltpu.VMEM) for v in (residual_out, normed, delivered)),
    )


def per_device(queries, cache_kv, new_kv, ctx_len, new_len, owner, wo, hidden_in, norm_gain):
    residual_out, normed, delivered = step(
        queries, cache_kv, new_kv, ctx_len, new_len, wo, hidden_in, norm_gain
    )
    return store(owner, residual_out, normed, delivered)


def solution(mesh):
    in_specs = (
        P("tp", None, None, None),
        P("tp", None, "seq", None),
        P("tp", None, "seq", None),
        P(),
        P(),
        P(),
        P(("seq", "tp"), None),
        P(None, ("seq", "tp")),
        P(("seq", "tp")),
    )
    out_specs = (P(None, ("seq", "tp")), P(None, ("seq", "tp")), P("tp", None, "seq", None))
    return jax.shard_map(
        per_device, mesh=mesh, in_specs=in_specs, out_specs=out_specs, check_vma=False
    )
```

```python
import functools

import jax
import jax.numpy as jnp
from jax import lax
from jax.experimental import pallas as pl
from jax.experimental.pallas import tpu as pltpu
from jax.sharding import PartitionSpec as P

D = 16384
HD = 128
KVH = 8
GROUP = 16
REQ = 4
WIDTH = 256
SHARE = 32
KEYS = WIDTH + SHARE
NEG = -1e30
LOG2E = 1.4426950408889634
MESH = pl.DeviceIdType.MESH


def remote(src, dst, send, recv, device):
    return pltpu.make_async_remote_copy(
        src_ref=src, dst_ref=dst, send_sem=send, recv_sem=recv, device_id=device, device_id_type=MESH
    )


def kernel(
    owner_hbm, ctx_hbm, new_hbm, q_hbm, cache_hbm, newkv_hbm, wo_hbm, hidden_hbm, gain_hbm,
    res_ref, norm_ref, got, owner_out,
    ctx_s, new_s, q_v, kv, w_v, hid_v, gain_v,
    osend, orecv, csend, crecv,
    a_send, b_send, e_send, a_recv, b_recv, e_recv, a2_send, b2_send, e2_send, a2_recv, b2_recv, e2_recv,
    n_send, n_recv, rows_v,
    loc_sem, kv_sem, wl_sem, ws_sem, wr_sem,
    os_sem, or_sem, cs_sem, cr_sem,
    r1s_sem, r1r_sem, e1s_sem, e1r_sem, r2s_sem, r2r_sem, ns_sem, nr_sem,
    gs_sem, gr_sem, ps_sem, pr_sem,
):
    s = lax.axis_index("seq")
    t = lax.axis_index("tp")
    y, c = s // 2, s % 2
    x, z = t // 4, t % 4
    me = s * 16 + t
    sp = y * 2 + (1 - c)

    def seq_peer(i):
        return (s + 1 + i) & 7

    def tp_peer(i):
        return ((x + 2 - (i & 3)) & 3) * 4 + ((z + 2 - (i >> 2)) & 3)

    def any_peer(i):
        far = (y + 2 - ((i >> 5) & 3)) & 3
        core = c ^ (1 - (i & 1))
        return far * 2 + core, ((x + 2 - ((i >> 1) & 3)) & 3) * 4 + ((z + 2 - ((i >> 3) & 3)) & 3)

    def y_at(d):
        return lax.rem(y + d, 4) * 2 + c

    def x_at(d):
        return lax.rem(x + d, 4) * 4 + z

    def z_at(d):
        return x * 4 + lax.rem(z + d, 4)

    drains = []

    def others(count, own, send):
        lax.fori_loop(0, own, send, 0)
        lax.fori_loop(own + 1, count, send, 0)

    barrier = pltpu.get_barrier_semaphore()

    def greet(device):
        pl.semaphore_signal(barrier, inc=1, device_id=device, device_id_type=MESH)

    def greet_tp(i, _):
        greet((sp, tp_peer(i)))
        greet((s, tp_peer(i)))
        return 0

    def greet_seq(i, _):
        greet((seq_peer(i), t))
        return 0

    others(16, 10, greet_tp)
    lax.fori_loop(0, 7, greet_seq, 0)

    loads = [
        pltpu.make_async_copy(src, dst, loc_sem.at[i])
        for i, (src, dst) in enumerate(
            [(ctx_hbm, ctx_s), (new_hbm, new_s), (q_hbm, q_v), (hidden_hbm, hid_v), (gain_hbm, gain_v),
             (owner_hbm, owner_out)]
        )
    ]

    def kv_copies(r):
        return (
            pltpu.make_async_copy(cache_hbm.at[r], kv.at[r, :, pl.ds(0, WIDTH), :], kv_sem.at[r, 0]),
            pltpu.make_async_copy(newkv_hbm.at[r], kv.at[r, :, pl.ds(WIDTH, SHARE), :], kv_sem.at[r, 1]),
        )

    for load in loads[:3]:
        load.start()
    for r in range(2):
        for copy in kv_copies(r):
            copy.start()

    for r in range(2, REQ):
        for copy in kv_copies(r):
            copy.start()
    for load in loads[3:]:
        load.start()

    def w_local(j):
        return pltpu.make_async_copy(
            wo_hbm.at[:, pl.ds(pl.multiple_of(j * 4096 + c * 2048, 2048), 2048)],
            w_v.at[j, pl.ds(pl.multiple_of(c * 128, 128), 128), :],
            wl_sem.at[j],
        )

    def w_remote(j):
        return remote(
            wo_hbm.at[:, pl.ds(pl.multiple_of(j * 4096 + (1 - c) * 2048, 2048), 2048)],
            w_v.at[j, pl.ds(pl.multiple_of(c * 128, 128), 128), :],
            ws_sem.at[j], wr_sem.at[j], (sp, t),
        )

    for j in range(4):
        w_local(j).start()

    def block(r, who):
        return got.at[r, :, pl.ds(pl.multiple_of(who * SHARE, SHARE), SHARE), :]

    def request(way, n):
        return n if way == 0 else REQ - 1 - n

    def source(way):
        return y_at(3 if way == 0 else 1)

    def ring(way, n, slot, who):
        here = block(request(way, n), who)
        return remote(
            here, here, gs_sem.at[way, slot], gr_sem.at[way, slot], (y_at(1 if way == 0 else 3), t)
        )

    def first(way, n):
        return ring(way, n, n, s)

    def second(way, n):
        return ring(way, n, REQ + n, source(way))

    def pair(way, n, slot, who):
        here = block(request(way, n), who)
        return remote(here, here, ps_sem.at[way, slot], pr_sem.at[way, slot], (sp, t))

    def pair_own(n):
        return pair(0, n, n, s)

    def pair_near(way, n):
        return pair(way, n, REQ + n, source(way))

    def pair_far(way, n):
        return pair(way, n, 2 * REQ + n, y_at(2))

    def start_first(*steps):
        for n in steps:
            for way in range(2):
                first(way, n).start()

    def start_second(*steps):
        for n in steps:
            for way in range(2):
                first(way, n).wait_recv()
                second(way, n).start()
                pair_near(way, n).start()

    def start_near(*steps):
        for n in steps:
            for way in range(2):
                first(way, n).wait_recv()
                pair_near(way, n).start()

    def start_far():
        for n in range(2):
            for way in range(2):
                second(way, n).wait_recv()
                pair_far(way, n).start()

    col = lax.broadcasted_iota(jnp.int32, (1, KEYS), 1)
    lane = lax.broadcasted_iota(jnp.int32, (KVH * GROUP, 128), 1)

    def attend(pair_of, stats):
        scores = []
        for r in pair_of:
            kv_copies(r)[0].wait()
        for r in pair_of:
            live_ctx = jnp.minimum(ctx_s[t * REQ + r] - s * WIDTH, WIDTH)
            live_new = new_s[t * REQ + r] - s * SHARE + WIDTH
            bias = jnp.where((col < live_ctx) | ((col >= WIDTH) & (col < live_new)), 0.0, NEG)
            for h in range(KVH):
                scores.append(
                    lax.dot_general(
                        q_v[r, h], kv[r, h, :, :HD], (((1,), (1,)), ((), ())), preferred_element_type=jnp.float32
                    )
                    + bias
                )
        scores = jnp.concatenate(scores, axis=0)
        top = jnp.maximum(jnp.max(scores, axis=1, keepdims=True), 0.1 * NEG)
        weights = jnp.exp2((scores - top) * (HD ** (-0.5) * LOG2E))
        total = jnp.maximum(jnp.sum(weights, axis=1, keepdims=True), 1e-30)
        weights = weights.astype(jnp.bfloat16)
        out = jnp.concatenate(
            [
                jnp.dot(
                    weights[(i * KVH + h) * GROUP:(i * KVH + h + 1) * GROUP],
                    kv[r, h, :, HD:],
                    preferred_element_type=jnp.float32,
                )
                for i, r in enumerate(pair_of)
                for h in range(KVH)
            ],
            axis=0,
        )
        out = (out * (1.0 / total)).astype(jnp.bfloat16)
        log_total = top * HD ** (-0.5) + jnp.log(total)
        for i, r in enumerate(pair_of):
            for h in range(KVH):
                first_row = (i * KVH + h) * GROUP
                osend[h, r * GROUP:(r + 1) * GROUP, :] = out[first_row:first_row + GROUP]
            stats = jnp.where(lane == r, log_total[i * KVH * GROUP:(i + 1) * KVH * GROUP], stats)
        return stats

    def rows_of(part):
        return pl.ds(0, 32) if part == 0 else pl.ds(32, 48)

    def o_copy(k, part):
        return remote(
            osend.at[k, rows_of(part)], orecv.at[s, rows_of(part)], os_sem.at[part], or_sem.at[part], (k, t)
        )

    def o_own(part):
        return pltpu.make_async_copy(
            osend.at[s, rows_of(part)], orecv.at[s, rows_of(part)], or_sem.at[part]
        )

    def send_o(part):
        o_own(part).start()

        def one(i, _):
            o_copy(seq_peer(i), part).start()
            return 0

        lax.fori_loop(0, 7, one, 0)

    def wait_o(part):
        everything = orecv.at[:, rows_of(part)]
        pltpu.make_async_copy(everything, everything, or_sem.at[part]).wait()

    def drain_o():
        for part in range(2):
            sent = osend.at[pl.ds(0, 7), rows_of(part)]
            pltpu.make_async_copy(sent, sent, os_sem.at[part]).wait()

    for load in loads[:3]:
        load.wait()
    stats = jnp.zeros((KVH * GROUP, 128), jnp.float32)
    for r in range(2):
        kv_copies(r)[1].wait()
    stats = attend((0, 1), stats)
    slot = lax.broadcasted_iota(jnp.int32, (SHARE, 256), 0)
    for r in range(2, REQ):
        kv_copies(r)[1].wait()
    for r in range(REQ):
        live = slot < new_s[t * REQ + r] - s * SHARE
        for h in range(KVH):
            got[r, h, pl.ds(pl.multiple_of(s * SHARE, SHARE), SHARE), :] = jnp.where(
                live, kv[r, h, WIDTH:, :], jnp.zeros((), jnp.bfloat16)
            )

    pl.semaphore_wait(barrier, 37)
    drains.append(drain_o)
    send_o(0)
    for j in range(4):
        w_remote(j).start()
    stats = attend((2, 3), stats)
    high = stats.astype(jnp.bfloat16).astype(jnp.float32)
    middle = (stats - high).astype(jnp.bfloat16).astype(jnp.float32)
    low = stats - high - middle
    pieces = (high + pltpu.roll(middle, 4, 1) + pltpu.roll(low, 8, 1)).astype(jnp.bfloat16)
    for h in range(KVH):
        osend[h, 64:80, :] = pieces[h * GROUP:(h + 1) * GROUP]
    send_o(1)

    start_first(0, 1, 2)
    for n in range(REQ):
        pair_own(n).start()

    def drain_gather():
        for n in range(REQ):
            pair_own(n).wait()
            for way in range(2):
                first(way, n).wait_send()
                pair_near(way, n).wait()
                if n < 2:
                    second(way, n).wait_send()
                    pair_far(way, n).wait()

    def drain_w():
        for j in range(4):
            w_remote(j).wait_send()

    drains.append(drain_gather)
    drains.append(drain_w)

    wait_o(0)
    wait_o(1)

    tops = []
    for k in range(8):
        piece = orecv[k, 64:80, :].astype(jnp.float32)
        tops.append(piece + pltpu.roll(piece, 124, 1) + pltpu.roll(piece, 120, 1))
    top = functools.reduce(jnp.maximum, tops)
    exps = [jnp.exp(v - top) for v in tops]
    total = functools.reduce(jnp.add, exps)
    shares = [e / total for e in exps]
    for r in range(REQ):
        context = jnp.zeros((GROUP, HD), jnp.float32)
        for k in range(8):
            part = orecv[k, r * GROUP:(r + 1) * GROUP, :].astype(jnp.float32)
            context = context + part * shares[k][:, r:r + 1]
        csend[:, r, :] = context

    def c_copy(core, g):
        return remote(
            csend.at[g], crecv.at[c, t], cs_sem.at[0], cr_sem.at[0], (y * 2 + core, g)
        )

    def send_c(i, _):
        g = tp_peer(i)
        c_copy(c, g).start()
        c_copy(1 - c, g).start()
        return 0

    def drain_c():
        for sent in (csend, csend.at[pl.ds(0, 15)]):
            pltpu.make_async_copy(sent, sent, cs_sem.at[0]).wait()

    drains.append(drain_c)
    others(16, 10, send_c)
    c_copy(1 - c, t).start()
    pltpu.make_async_copy(csend.at[t], crecv.at[c, t], cr_sem.at[0]).start()
    for j in range(4):
        w_local(j).wait()
        w_remote(j).wait_recv()
    pltpu.make_async_copy(crecv, crecv, cr_sem.at[0]).wait()

    flat = jnp.concatenate(
        [
            jnp.concatenate([crecv[core, :, r, :] for r in range(REQ)], axis=0)
            for core in range(2)
        ],
        axis=1,
    ).astype(jnp.bfloat16)

    def r1_copy(way, d, part):
        dst = ((x if way == 0 else z) + d) & 3
        src = (a_send if way == 0 else b_send).at[dst, part]
        to = (a_recv if way == 0 else b_recv).at[d - 1, part]
        return remote(
            src, to, r1s_sem.at[way, d - 1, part], r1r_sem.at[way, d - 1, part],
            (s, x_at(d) if way == 0 else z_at(d)),
        )

    def e1_copy(d):
        return remote(
            e_send.at[(y + d) & 3], e_recv.at[d - 1], e1s_sem.at[d - 1], e1r_sem.at[d - 1], (y_at(d), t)
        )

    def project(j):
        for i in range(4):
            piece = jnp.dot(flat, w_v[j, :, i * 512:(i + 1) * 512], preferred_element_type=jnp.float32)
            a_send[i, j] = piece[:24].astype(jnp.bfloat16)
            middle = piece[24:48].astype(jnp.bfloat16)
            for k in range(4):
                b_send[k, j, :, i * 128:(i + 1) * 128] = middle[:, k * 128:(k + 1) * 128]
            e_send[j, :, i * 512:(i + 1) * 512] = piece[48:].astype(jnp.bfloat16)

    def drain_r1():
        for d in range(1, 4):
            e1_copy(d).wait_send()
            for way in range(2):
                for part in range(4):
                    r1_copy(way, d, part).wait_send()

    drains.append(drain_r1)
    turns = (2, 1, 3, 0)
    for turn in turns:
        part = (y + turn) & 3
        project(part)
        if turn:
            e1_copy(turn).start()
        for d in (2, 1, 3):
            for way in range(2):
                r1_copy(way, d, part).start()

    start_first(3)
    def r2_copy(way, j, k):
        send, recv = ((a2_send, a2_recv), (b2_send, b2_recv), (e2_send, e2_recv))[way]
        if way == 2:
            slot, device = (x, z), (s, j * 4 + k)
        else:
            slot = (y, z if way == 0 else x)
            device = (j * 2 + c, x * 4 + k if way == 0 else k * 4 + z)
        return remote(send.at[j, k], recv.at[slot], r2s_sem.at[way], r2r_sem.at[way], device)

    def send_r2(way, j, k):
        send, recv = ((a2_send, a2_recv), (b2_send, b2_recv), (e2_send, e2_recv))[way]
        mine = ((y, z), (y, x), (x, z))[way]
        away = (j != mine[0]) | (k != mine[1])

        @pl.when(away)
        def _():
            r2_copy(way, j, k).start()

        @pl.when(jnp.logical_not(away))
        def _():
            pltpu.make_async_copy(send.at[j, k], recv.at[j, k], r2r_sem.at[way]).start()

    def drain_r2():
        for way in range(3):
            send = (a2_send, b2_send, e2_send)[way]
            for sent in (send.at[pl.ds(0, 3)], send.at[0, pl.ds(0, 3)]):
                pltpu.make_async_copy(sent, sent, r2s_sem.at[way]).wait()

    def add_e():
        for d in (1, 3, 2):
            e1_copy(d).wait_recv()
        for j in (2, 1, 3, 0):
            cols = slice(j * 512, (j + 1) * 512)
            out = e_send[y, :, cols].astype(jnp.float32)
            for d in range(3):
                out = out + e_recv[d, :, cols].astype(jnp.float32)
            out = out.astype(jnp.bfloat16)
            for k in range(4):
                e2_send[j, k] = out[:, k * 128:(k + 1) * 128]
            for k in range(4):
                send_r2(2, j, k)

    drains.append(drain_r2)
    for turn in turns:
        part = (y + turn) & 3
        for way in range(2):
            for d in (1, 3, 2):
                r1_copy(way, d, part).wait_recv()
            send, recv, nxt = ((a_send, a_recv, a2_send), (b_send, b_recv, b2_send))[way]
            out = send[x if way == 0 else z, part].astype(jnp.float32)
            for d in range(3):
                out = out + recv[d, part].astype(jnp.float32)
            out = out.astype(jnp.bfloat16)
            for k in range(4):
                nxt[part, k] = out[:, k * 128:(k + 1) * 128]
            for k in range(4):
                send_r2(way, part, k)
        if turn == 3:
            add_e()
            start_second(0, 1)


    for load in loads[3:]:
        load.wait()
    rows_v[...] = hid_v[...].astype(jnp.float32)
    stream = jnp.concatenate([rows_v[pl.ds(r, 16, stride=REQ), :] for r in range(REQ)], axis=0)
    start_near(2, 3)
    sums = []
    for way in range(3):
        recv = (a2_recv, b2_recv, e2_recv)[way]
        pltpu.make_async_copy(recv, recv, r2r_sem.at[way]).wait()
        out = recv[0, 0].astype(jnp.float32)
        for i in range(1, 16):
            out = out + recv[i // 4, i % 4].astype(jnp.float32)
        sums.append(out)
    stream = stream + jnp.concatenate(sums, axis=0)

    squares = stream * stream
    n_send[...] = jnp.sum(jnp.concatenate([squares, squares], axis=0).T, axis=0, keepdims=True)

    def send_n(i, _):
        pltpu.make_async_remote_copy(
            src_ref=n_send, dst_ref=n_recv.at[me], send_sem=ns_sem.at[0], recv_sem=nr_sem.at[0],
            device_id=any_peer(i), device_id_type=MESH,
        ).start()
        return 0

    def drain_n():
        sent = n_recv.at[pl.ds(0, 127)]
        pltpu.make_async_copy(sent, sent, ns_sem.at[0]).wait()

    others(128, 85, send_n)
    pltpu.make_async_copy(n_send, n_recv.at[me], nr_sem.at[0]).start()
    for r in range(REQ):
        rows_v[pl.ds(r, 16, stride=REQ), :] = stream[r * 16:(r + 1) * 16]
    res_ref[...] = rows_v[...].astype(jnp.bfloat16)

    start_far()
    scaled = stream * gain_v[...]
    for drain in drains:
        drain()
    pltpu.make_async_copy(n_recv, n_recv, nr_sem.at[0]).wait()
    scale = lax.rsqrt(jnp.sum(n_recv[...], axis=0) / D + 1e-05)
    scale = jnp.broadcast_to(scale, (128, 128)).T[:64]
    normed = scaled * scale
    for r in range(REQ):
        rows_v[pl.ds(r, 16, stride=REQ), :] = normed[r * 16:(r + 1) * 16]
    norm_ref[...] = rows_v[...].astype(jnp.bfloat16)
    drain_n()


def step(queries, cache_kv, new_kv, ctx_len, new_len, owner, wo, hidden_in, norm_gain):
    bf, f32 = jnp.bfloat16, jnp.float32
    dma = pltpu.SemaphoreType.DMA
    anywhere = pl.BlockSpec(memory_space=pl.ANY)
    vmem = pl.BlockSpec(memory_space=pltpu.VMEM)
    V = pltpu.VMEM
    return pl.pallas_call(
        kernel,
        out_shape=(
            V((64, 128), bf),
            V((64, 128), bf),
            V((REQ, KVH, WIDTH, 256), bf),
            pltpu.SMEM((64,), jnp.int32),
        ),
        in_specs=[anywhere] * 9,
        out_specs=(vmem, vmem, vmem, pl.BlockSpec(memory_space=pltpu.SMEM)),
        scratch_shapes=[
            pltpu.SMEM((64,), jnp.int32), pltpu.SMEM((64,), jnp.int32),
            V((REQ, KVH, GROUP, HD), bf),
            V((REQ, KVH, KEYS, 256), bf),
            V((4, 256, 2048), bf),
            V((64, 128), bf),
            V((1, 128), f32),
            V((8, 80, HD), bf), V((8, 80, HD), bf),
            V((16, REQ, HD), f32), V((2, 16, REQ, HD), f32),
            V((4, 4, 24, 512), bf), V((4, 4, 24, 512), bf), V((4, 16, 2048), bf),
            V((3, 4, 24, 512), bf), V((3, 4, 24, 512), bf), V((3, 16, 2048), bf),
            V((4, 4, 24, 128), bf), V((4, 4, 24, 128), bf), V((4, 4, 16, 128), bf),
            V((4, 4, 24, 128), bf), V((4, 4, 24, 128), bf), V((4, 4, 16, 128), bf),
            V((1, 128), f32), V((128, 1, 128), f32),
            V((64, 128), f32),
            dma((6,)), dma((REQ, 2)), dma((4,)), dma((4,)), dma((4,)),
            dma((2,)), dma((2,)), dma((1,)), dma((1,)),
            dma((2, 3, 4)), dma((2, 3, 4)), dma((3,)), dma((3,)), dma((3,)), dma((3,)), dma((1,)), dma((1,)),
            dma((2, 6)), dma((2, 6)), dma((2, 10)), dma((2, 10)),
        ],
        compiler_params=pltpu.CompilerParams(
            collective_id=0, has_side_effects=True, vmem_limit_bytes=40 * 1024 * 1024
        ),
        cost_estimate=pl.CostEstimate(flops=600_000_000, bytes_accessed=14_000_000, transcendentals=1_000_000),
    )(
        *(
            pltpu.with_memory_space_constraint(v, pltpu.HBM)
            for v in (owner, ctx_len, new_len, queries, cache_kv, new_kv, wo, hidden_in, norm_gain.reshape(1, 128))
        )
    )


def store_kernel(
    owner_ref, res_in, norm_in, deliv_ref, res_hbm, norm_hbm, app_hbm,
    zeros, out_sem, sem,
):
    s = lax.axis_index("seq")
    t = lax.axis_index("tp")

    def blank(r, i):
        return pltpu.make_async_copy(zeros, app_hbm.at[r, pl.ds(i * 2, 2)], out_sem.at[r, i])

    def put(r, i):
        part = pl.ds(i * 2, 2)
        return pltpu.make_async_copy(deliv_ref.at[r, part], app_hbm.at[r, part], out_sem.at[r, i])

    def mine(r):
        return owner_ref[t * REQ + r] == s

    small = (
        pltpu.make_async_copy(res_in, res_hbm, sem.at[0]),
        pltpu.make_async_copy(norm_in, norm_hbm, sem.at[1]),
    )
    for copy in small:
        copy.start()
    zeros[...] = jnp.zeros_like(zeros)
    for r in range(REQ):
        @pl.when(mine(r))
        def _():
            for i in range(4):
                put(r, i).start()

    for r in range(REQ):
        @pl.when(jnp.logical_not(mine(r)))
        def _():
            for i in range(4):
                blank(r, i).start()

    for copy in small:
        copy.wait()
    for r in range(REQ):
        for i in range(4):
            put(r, i).wait()


def store(owner, residual_out, normed, delivered):
    anywhere = pl.BlockSpec(memory_space=pl.ANY)
    vmem = pl.BlockSpec(memory_space=pltpu.VMEM)
    return pl.pallas_call(
        store_kernel,
        out_shape=tuple(jax.ShapeDtypeStruct(v.shape, v.dtype) for v in (residual_out, normed, delivered)),
        in_specs=[pl.BlockSpec(memory_space=pltpu.SMEM)] + [vmem] * 3,
        out_specs=(anywhere,) * 3,
        scratch_shapes=[
            pltpu.VMEM((2, WIDTH, 256), jnp.bfloat16),
            pltpu.SemaphoreType.DMA((REQ, 4)),
            pltpu.SemaphoreType.DMA((2,)),
        ],
        compiler_params=pltpu.CompilerParams(vmem_limit_bytes=20 * 1024 * 1024),
        cost_estimate=pl.CostEstimate(flops=0, bytes_accessed=6_000_000, transcendentals=0),
    )(
        pltpu.with_memory_space_constraint(owner, pltpu.SMEM),
        *(pltpu.with_memory_space_constraint(v, pltpu.VMEM) for v in (residual_out, normed, delivered)),
    )


def per_device(queries, cache_kv, new_kv, ctx_len, new_len, owner, wo, hidden_in, norm_gain):
    residual_out, normed, delivered, owner = step(
        queries, cache_kv, new_kv, ctx_len, new_len, owner, wo, hidden_in, norm_gain
    )
    return store(owner, residual_out, normed, delivered)


def solution(mesh):
    in_specs = (
        P("tp", None, None, None),
        P("tp", None, "seq", None),
        P("tp", None, "seq", None),
        P(),
        P(),
        P(),
        P(("seq", "tp"), None),
        P(None, ("seq", "tp")),
        P(("seq", "tp")),
    )
    out_specs = (P(None, ("seq", "tp")), P(None, ("seq", "tp")), P("tp", None, "seq", None))
    return jax.shard_map(
        per_device, mesh=mesh, in_specs=in_specs, out_specs=out_specs, check_vma=False
    )
```

```python
import functools

import jax
import jax.numpy as jnp
from jax import lax
from jax.experimental import pallas as pl
from jax.experimental.pallas import tpu as pltpu
from jax.sharding import PartitionSpec as P

D = 16384
HD = 128
KVH = 8
GROUP = 16
REQ = 4
WIDTH = 256
SHARE = 32
KEYS = WIDTH + SHARE
NEG = -1e30
LOG2E = 1.4426950408889634
MESH = pl.DeviceIdType.MESH


def remote(src, dst, send, recv, device):
    return pltpu.make_async_remote_copy(
        src_ref=src, dst_ref=dst, send_sem=send, recv_sem=recv, device_id=device, device_id_type=MESH
    )


def kernel(
    after_hbm, owner_hbm, ctx_hbm, new_hbm, q_hbm, cache_hbm, newkv_hbm, wo_hbm, hidden_hbm, gain_hbm,
    res_ref, norm_ref, got, owner_out,
    ctx_s, new_s, q_v, kv, w_v, hid_v, gain_v,
    osend, orecv, csend, crecv,
    a_send, b_send, e_send, a_recv, b_recv, e_recv, a2_send, b2_send, e2_send, a2_recv, b2_recv, e2_recv,
    n_send, n_recv, rows_v,
    loc_sem, kv_sem, wl_sem, ws_sem, wr_sem,
    os_sem, or_sem, cs_sem, cr_sem,
    r1s_sem, r1r_sem, e1s_sem, e1r_sem, r2s_sem, r2r_sem, ns_sem, nr_sem,
    gs_sem, gr_sem, ps_sem, pr_sem,
):
    s = lax.axis_index("seq")
    t = lax.axis_index("tp")
    y, c = s // 2, s % 2
    x, z = t // 4, t % 4
    me = s * 16 + t
    sp = y * 2 + (1 - c)

    def seq_peer(i):
        return (s + 1 + i) & 7

    def tp_peer(i):
        return ((x + 2 - (i & 3)) & 3) * 4 + ((z + 2 - (i >> 2)) & 3)

    def any_peer(i):
        far = (y + 2 - ((i >> 5) & 3)) & 3
        core = c ^ (1 - (i & 1))
        return far * 2 + core, ((x + 2 - ((i >> 1) & 3)) & 3) * 4 + ((z + 2 - ((i >> 3) & 3)) & 3)

    def y_at(d):
        return lax.rem(y + d, 4) * 2 + c

    def x_at(d):
        return lax.rem(x + d, 4) * 4 + z

    def z_at(d):
        return x * 4 + lax.rem(z + d, 4)

    drains = []

    def others(count, own, send):
        lax.fori_loop(0, own, send, 0)
        lax.fori_loop(own + 1, count, send, 0)

    barrier = pltpu.get_barrier_semaphore()

    def greet(device):
        pl.semaphore_signal(barrier, inc=1, device_id=device, device_id_type=MESH)

    def greet_tp(i, _):
        greet((sp, tp_peer(i)))
        greet((s, tp_peer(i)))
        return 0

    def greet_seq(i, _):
        greet((seq_peer(i), t))
        return 0

    others(16, 10, greet_tp)
    lax.fori_loop(0, 7, greet_seq, 0)

    loads = [
        pltpu.make_async_copy(src, dst, loc_sem.at[i])
        for i, (src, dst) in enumerate(
            [(ctx_hbm, ctx_s), (new_hbm, new_s), (q_hbm, q_v), (hidden_hbm, hid_v), (gain_hbm, gain_v),
             (owner_hbm, owner_out)]
        )
    ]

    def kv_copies(r):
        return (
            pltpu.make_async_copy(cache_hbm.at[r], kv.at[r, :, pl.ds(0, WIDTH), :], kv_sem.at[r, 0]),
            pltpu.make_async_copy(newkv_hbm.at[r], kv.at[r, :, pl.ds(WIDTH, SHARE), :], kv_sem.at[r, 1]),
        )

    for load in loads[:3]:
        load.start()
    for r in range(2):
        for copy in kv_copies(r):
            copy.start()

    for r in range(2, REQ):
        for copy in kv_copies(r):
            copy.start()
    for load in loads[3:]:
        load.start()

    def w_local(j):
        return pltpu.make_async_copy(
            wo_hbm.at[:, pl.ds(pl.multiple_of(j * 4096 + c * 2048, 2048), 2048)],
            w_v.at[j, pl.ds(pl.multiple_of(c * 128, 128), 128), :],
            wl_sem.at[j],
        )

    def w_remote(j):
        return remote(
            wo_hbm.at[:, pl.ds(pl.multiple_of(j * 4096 + (1 - c) * 2048, 2048), 2048)],
            w_v.at[j, pl.ds(pl.multiple_of(c * 128, 128), 128), :],
            ws_sem.at[j], wr_sem.at[j], (sp, t),
        )

    for j in range(4):
        w_local(j).start()

    def block(r, who):
        return got.at[r, :, pl.ds(pl.multiple_of(who * SHARE, SHARE), SHARE), :]

    def request(way, n):
        return n if way == 0 else REQ - 1 - n

    def source(way):
        return y_at(3 if way == 0 else 1)

    def ring(way, n, slot, who):
        here = block(request(way, n), who)
        return remote(
            here, here, gs_sem.at[way, slot], gr_sem.at[way, slot], (y_at(1 if way == 0 else 3), t)
        )

    def first(way, n):
        return ring(way, n, n, s)

    def second(way, n):
        return ring(way, n, REQ + n, source(way))

    def pair(way, n, slot, who):
        here = block(request(way, n), who)
        return remote(here, here, ps_sem.at[way, slot], pr_sem.at[way, slot], (sp, t))

    def pair_own(n):
        return pair(0, n, n, s)

    def pair_near(way, n):
        return pair(way, n, REQ + n, source(way))

    def pair_far(way, n):
        return pair(way, n, 2 * REQ + n, y_at(2))

    def start_first(*steps):
        for n in steps:
            for way in range(2):
                first(way, n).start()

    def start_second(*steps):
        for n in steps:
            for way in range(2):
                first(way, n).wait_recv()
                second(way, n).start()
                pair_near(way, n).start()

    def start_near(*steps):
        for n in steps:
            for way in range(2):
                first(way, n).wait_recv()
                pair_near(way, n).start()

    def start_far():
        for n in range(2):
            for way in range(2):
                second(way, n).wait_recv()
                pair_far(way, n).start()

    col = lax.broadcasted_iota(jnp.int32, (1, KEYS), 1)
    lane = lax.broadcasted_iota(jnp.int32, (KVH * GROUP, 128), 1)

    def attend(pair_of, stats):
        scores = []
        for r in pair_of:
            kv_copies(r)[0].wait()
        for r in pair_of:
            live_ctx = jnp.minimum(ctx_s[t * REQ + r] - s * WIDTH, WIDTH)
            live_new = new_s[t * REQ + r] - s * SHARE + WIDTH
            bias = jnp.where((col < live_ctx) | ((col >= WIDTH) & (col < live_new)), 0.0, NEG)
            for h in range(KVH):
                scores.append(
                    lax.dot_general(
                        q_v[r, h], kv[r, h, :, :HD], (((1,), (1,)), ((), ())), preferred_element_type=jnp.float32
                    )
                    + bias
                )
        scores = jnp.concatenate(scores, axis=0)
        top = jnp.maximum(jnp.max(scores, axis=1, keepdims=True), 0.1 * NEG)
        weights = jnp.exp2((scores - top) * (HD ** (-0.5) * LOG2E))
        total = jnp.maximum(jnp.sum(weights, axis=1, keepdims=True), 1e-30)
        weights = weights.astype(jnp.bfloat16)
        out = jnp.concatenate(
            [
                jnp.dot(
                    weights[(i * KVH + h) * GROUP:(i * KVH + h + 1) * GROUP],
                    kv[r, h, :, HD:],
                    preferred_element_type=jnp.float32,
                )
                for i, r in enumerate(pair_of)
                for h in range(KVH)
            ],
            axis=0,
        )
        out = (out * (1.0 / total)).astype(jnp.bfloat16)
        log_total = top * HD ** (-0.5) + jnp.log(total)
        for i, r in enumerate(pair_of):
            for h in range(KVH):
                first_row = (i * KVH + h) * GROUP
                osend[h, r * GROUP:(r + 1) * GROUP, :] = out[first_row:first_row + GROUP]
            stats = jnp.where(lane == r, log_total[i * KVH * GROUP:(i + 1) * KVH * GROUP], stats)
        return stats

    def rows_of(part):
        return pl.ds(0, 32) if part == 0 else pl.ds(32, 48)

    def o_copy(k, part):
        return remote(
            osend.at[k, rows_of(part)], orecv.at[s, rows_of(part)], os_sem.at[part], or_sem.at[part], (k, t)
        )

    def o_own(part):
        return pltpu.make_async_copy(
            osend.at[s, rows_of(part)], orecv.at[s, rows_of(part)], or_sem.at[part]
        )

    def send_o(part):
        o_own(part).start()

        def one(i, _):
            o_copy(seq_peer(i), part).start()
            return 0

        lax.fori_loop(0, 7, one, 0)

    def wait_o(part):
        everything = orecv.at[:, rows_of(part)]
        pltpu.make_async_copy(everything, everything, or_sem.at[part]).wait()

    def drain_o():
        for part in range(2):
            sent = osend.at[pl.ds(0, 7), rows_of(part)]
            pltpu.make_async_copy(sent, sent, os_sem.at[part]).wait()

    for load in loads[:3]:
        load.wait()
    stats = jnp.zeros((KVH * GROUP, 128), jnp.float32)
    for r in range(2):
        kv_copies(r)[1].wait()
    stats = attend((0, 1), stats)
    slot = lax.broadcasted_iota(jnp.int32, (SHARE, 256), 0)
    for r in range(2, REQ):
        kv_copies(r)[1].wait()
    for r in range(REQ):
        live = slot < new_s[t * REQ + r] - s * SHARE
        for h in range(KVH):
            got[r, h, pl.ds(pl.multiple_of(s * SHARE, SHARE), SHARE), :] = jnp.where(
                live, kv[r, h, WIDTH:, :], jnp.zeros((), jnp.bfloat16)
            )

    pl.semaphore_wait(barrier, 37)
    drains.append(drain_o)
    send_o(0)
    for j in range(4):
        w_remote(j).start()
    stats = attend((2, 3), stats)
    high = stats.astype(jnp.bfloat16).astype(jnp.float32)
    middle = (stats - high).astype(jnp.bfloat16).astype(jnp.float32)
    low = stats - high - middle
    pieces = (high + pltpu.roll(middle, 4, 1) + pltpu.roll(low, 8, 1)).astype(jnp.bfloat16)
    for h in range(KVH):
        osend[h, 64:80, :] = pieces[h * GROUP:(h + 1) * GROUP]
    send_o(1)

    start_first(0, 1, 2)
    for n in range(REQ):
        pair_own(n).start()

    def drain_gather():
        for n in range(REQ):
            pair_own(n).wait()
            for way in range(2):
                first(way, n).wait_send()
                pair_near(way, n).wait()
                if n < 2:
                    second(way, n).wait_send()
                    pair_far(way, n).wait()

    def drain_w():
        for j in range(4):
            w_remote(j).wait_send()

    drains.append(drain_gather)
    drains.append(drain_w)

    wait_o(0)
    wait_o(1)

    tops = []
    for k in range(8):
        piece = orecv[k, 64:80, :].astype(jnp.float32)
        tops.append(piece + pltpu.roll(piece, 124, 1) + pltpu.roll(piece, 120, 1))
    top = functools.reduce(jnp.maximum, tops)
    exps = [jnp.exp(v - top) for v in tops]
    total = functools.reduce(jnp.add, exps)
    shares = [e / total for e in exps]
    for r in range(REQ):
        context = jnp.zeros((GROUP, HD), jnp.float32)
        for k in range(8):
            part = orecv[k, r * GROUP:(r + 1) * GROUP, :].astype(jnp.float32)
            context = context + part * shares[k][:, r:r + 1]
        csend[:, r, :] = context

    def c_copy(core, g):
        return remote(
            csend.at[g], crecv.at[c, t], cs_sem.at[0], cr_sem.at[0], (y * 2 + core, g)
        )

    def send_c(i, _):
        g = tp_peer(i)
        c_copy(c, g).start()
        c_copy(1 - c, g).start()
        return 0

    def drain_c():
        for sent in (csend, csend.at[pl.ds(0, 15)]):
            pltpu.make_async_copy(sent, sent, cs_sem.at[0]).wait()

    drains.append(drain_c)
    others(16, 10, send_c)
    c_copy(1 - c, t).start()
    pltpu.make_async_copy(csend.at[t], crecv.at[c, t], cr_sem.at[0]).start()
    for j in range(4):
        w_local(j).wait()
        w_remote(j).wait_recv()
    pltpu.make_async_copy(crecv, crecv, cr_sem.at[0]).wait()

    flat = jnp.concatenate(
        [
            jnp.concatenate([crecv[core, :, r, :] for r in range(REQ)], axis=0)
            for core in range(2)
        ],
        axis=1,
    ).astype(jnp.bfloat16)

    def r1_copy(way, d, part):
        dst = ((x if way == 0 else z) + d) & 3
        src = (a_send if way == 0 else b_send).at[dst, part]
        to = (a_recv if way == 0 else b_recv).at[d - 1, part]
        return remote(
            src, to, r1s_sem.at[way, d - 1, part], r1r_sem.at[way, d - 1, part],
            (s, x_at(d) if way == 0 else z_at(d)),
        )

    def e1_copy(d):
        return remote(
            e_send.at[(y + d) & 3], e_recv.at[d - 1], e1s_sem.at[d - 1], e1r_sem.at[d - 1], (y_at(d), t)
        )

    def project(j):
        for i in range(4):
            piece = jnp.dot(flat, w_v[j, :, i * 512:(i + 1) * 512], preferred_element_type=jnp.float32)
            a_send[i, j] = piece[:24].astype(jnp.bfloat16)
            middle = piece[24:48].astype(jnp.bfloat16)
            for k in range(4):
                b_send[k, j, :, i * 128:(i + 1) * 128] = middle[:, k * 128:(k + 1) * 128]
            e_send[j, :, i * 512:(i + 1) * 512] = piece[48:].astype(jnp.bfloat16)

    def drain_r1():
        for d in range(1, 4):
            e1_copy(d).wait_send()
            for way in range(2):
                for part in range(4):
                    r1_copy(way, d, part).wait_send()

    drains.append(drain_r1)
    turns = (2, 1, 3, 0)
    for turn in turns:
        part = (y + turn) & 3
        project(part)
        if turn:
            e1_copy(turn).start()
        for d in (2, 1, 3):
            for way in range(2):
                r1_copy(way, d, part).start()

    start_first(3)
    def r2_copy(way, j, k):
        send, recv = ((a2_send, a2_recv), (b2_send, b2_recv), (e2_send, e2_recv))[way]
        if way == 2:
            slot, device = (x, z), (s, j * 4 + k)
        else:
            slot = (y, z if way == 0 else x)
            device = (j * 2 + c, x * 4 + k if way == 0 else k * 4 + z)
        return remote(send.at[j, k], recv.at[slot], r2s_sem.at[way], r2r_sem.at[way], device)

    def send_r2(way, dj, dk):
        send, recv = ((a2_send, a2_recv), (b2_send, b2_recv), (e2_send, e2_recv))[way]
        mine = ((y, z), (y, x), (x, z))[way]
        j, k = (mine[0] + dj) & 3, (mine[1] + dk) & 3
        if dj or dk:
            r2_copy(way, j, k).start()
        else:
            pltpu.make_async_copy(send.at[j, k], recv.at[j, k], r2r_sem.at[way]).start()

    def drain_r2():
        for way in range(3):
            send = (a2_send, b2_send, e2_send)[way]
            for sent in (send.at[pl.ds(0, 3)], send.at[0, pl.ds(0, 3)]):
                pltpu.make_async_copy(sent, sent, r2s_sem.at[way]).wait()

    def add_e():
        for d in (1, 3, 2):
            e1_copy(d).wait_recv()
        for j in (2, 1, 3, 0):
            cols = slice(j * 512, (j + 1) * 512)
            out = e_send[y, :, cols].astype(jnp.float32)
            for d in range(3):
                out = out + e_recv[d, :, cols].astype(jnp.float32)
            out = out.astype(jnp.bfloat16)
            for k in range(4):
                e2_send[j, k] = out[:, k * 128:(k + 1) * 128]
        for dj in (2, 1, 3, 0):
            for dk in (2, 1, 3, 0):
                send_r2(2, dj, dk)

    drains.append(drain_r2)
    for turn in turns:
        part = (y + turn) & 3
        for way in range(2):
            for d in (1, 3, 2):
                r1_copy(way, d, part).wait_recv()
            send, recv, nxt = ((a_send, a_recv, a2_send), (b_send, b_recv, b2_send))[way]
            out = send[x if way == 0 else z, part].astype(jnp.float32)
            for d in range(3):
                out = out + recv[d, part].astype(jnp.float32)
            out = out.astype(jnp.bfloat16)
            for k in range(4):
                nxt[part, k] = out[:, k * 128:(k + 1) * 128]
            for dk in (2, 1, 3, 0):
                send_r2(way, turn, dk)
        if turn == 3:
            add_e()
            start_second(0, 1)


    for load in loads[3:]:
        load.wait()
    rows_v[...] = hid_v[...].astype(jnp.float32)
    stream = jnp.concatenate([rows_v[pl.ds(r, 16, stride=REQ), :] for r in range(REQ)], axis=0)
    start_near(2, 3)
    sums = []
    for way in range(3):
        recv = (a2_recv, b2_recv, e2_recv)[way]
        pltpu.make_async_copy(recv, recv, r2r_sem.at[way]).wait()
        out = recv[0, 0].astype(jnp.float32)
        for i in range(1, 16):
            out = out + recv[i // 4, i % 4].astype(jnp.float32)
        sums.append(out)
    stream = stream + jnp.concatenate(sums, axis=0)

    squares = stream * stream
    n_send[...] = jnp.sum(jnp.concatenate([squares, squares], axis=0).T, axis=0, keepdims=True)

    def send_n(i, _):
        pltpu.make_async_remote_copy(
            src_ref=n_send, dst_ref=n_recv.at[me], send_sem=ns_sem.at[0], recv_sem=nr_sem.at[0],
            device_id=any_peer(i), device_id_type=MESH,
        ).start()
        return 0

    def drain_n():
        sent = n_recv.at[pl.ds(0, 127)]
        pltpu.make_async_copy(sent, sent, ns_sem.at[0]).wait()

    others(128, 85, send_n)
    pltpu.make_async_copy(n_send, n_recv.at[me], nr_sem.at[0]).start()
    for r in range(REQ):
        rows_v[pl.ds(r, 16, stride=REQ), :] = stream[r * 16:(r + 1) * 16]
    res_ref[...] = rows_v[...].astype(jnp.bfloat16)

    start_far()
    scaled = stream * gain_v[...]
    for drain in drains:
        drain()
    pltpu.make_async_copy(n_recv, n_recv, nr_sem.at[0]).wait()
    scale = lax.rsqrt(jnp.sum(n_recv[...], axis=0) / D + 1e-05)
    scale = jnp.broadcast_to(scale, (128, 128)).T[:64]
    normed = scaled * scale
    for r in range(REQ):
        rows_v[pl.ds(r, 16, stride=REQ), :] = normed[r * 16:(r + 1) * 16]
    norm_ref[...] = rows_v[...].astype(jnp.bfloat16)
    drain_n()


def step(after, queries, cache_kv, new_kv, ctx_len, new_len, owner, wo, hidden_in, norm_gain):
    bf, f32 = jnp.bfloat16, jnp.float32
    dma = pltpu.SemaphoreType.DMA
    anywhere = pl.BlockSpec(memory_space=pl.ANY)
    vmem = pl.BlockSpec(memory_space=pltpu.VMEM)
    V = pltpu.VMEM
    return pl.pallas_call(
        kernel,
        out_shape=(
            V((64, 128), bf),
            V((64, 128), bf),
            V((REQ, KVH, WIDTH, 256), bf),
            pltpu.SMEM((64,), jnp.int32),
        ),
        in_specs=[anywhere] * 10,
        out_specs=(vmem, vmem, vmem, pl.BlockSpec(memory_space=pltpu.SMEM)),
        scratch_shapes=[
            pltpu.SMEM((64,), jnp.int32), pltpu.SMEM((64,), jnp.int32),
            V((REQ, KVH, GROUP, HD), bf),
            V((REQ, KVH, KEYS, 256), bf),
            V((4, 256, 2048), bf),
            V((64, 128), bf),
            V((1, 128), f32),
            V((8, 80, HD), bf), V((8, 80, HD), bf),
            V((16, REQ, HD), f32), V((2, 16, REQ, HD), f32),
            V((4, 4, 24, 512), bf), V((4, 4, 24, 512), bf), V((4, 16, 2048), bf),
            V((3, 4, 24, 512), bf), V((3, 4, 24, 512), bf), V((3, 16, 2048), bf),
            V((4, 4, 24, 128), bf), V((4, 4, 24, 128), bf), V((4, 4, 16, 128), bf),
            V((4, 4, 24, 128), bf), V((4, 4, 24, 128), bf), V((4, 4, 16, 128), bf),
            V((1, 128), f32), V((128, 1, 128), f32),
            V((64, 128), f32),
            dma((6,)), dma((REQ, 2)), dma((4,)), dma((4,)), dma((4,)),
            dma((2,)), dma((2,)), dma((1,)), dma((1,)),
            dma((2, 3, 4)), dma((2, 3, 4)), dma((3,)), dma((3,)), dma((3,)), dma((3,)), dma((1,)), dma((1,)),
            dma((2, 6)), dma((2, 6)), dma((2, 10)), dma((2, 10)),
        ],
        compiler_params=pltpu.CompilerParams(
            collective_id=0, has_side_effects=True, vmem_limit_bytes=40 * 1024 * 1024
        ),
        cost_estimate=pl.CostEstimate(flops=600_000_000, bytes_accessed=14_000_000, transcendentals=1_000_000),
    )(
        *(
            pltpu.with_memory_space_constraint(v, pltpu.HBM)
            for v in (after, owner, ctx_len, new_len, queries, cache_kv, new_kv, wo, hidden_in, norm_gain.reshape(1, 128))
        )
    )


def starts_early():
    return (lax.axis_index("tp") & 3) == 0


def blank_kernel(app_hbm, zeros, sem):
    def blank(r, i):
        return pltpu.make_async_copy(zeros, app_hbm.at[r, pl.ds(i * 2, 2)], sem.at[r, i])

    @pl.when(starts_early())
    def _():
        zeros[...] = jnp.zeros_like(zeros)
        for r in range(REQ):
            for i in range(4):
                blank(r, i).start()
        for r in range(REQ):
            for i in range(4):
                blank(r, i).wait()


def blanks():
    return pl.pallas_call(
        blank_kernel,
        out_shape=pltpu.HBM((REQ, KVH, WIDTH, 256), jnp.bfloat16),
        out_specs=pl.BlockSpec(memory_space=pl.ANY),
        scratch_shapes=[pltpu.VMEM((2, WIDTH, 256), jnp.bfloat16), pltpu.SemaphoreType.DMA((REQ, 4))],
        compiler_params=pltpu.CompilerParams(vmem_limit_bytes=20 * 1024 * 1024),
        cost_estimate=pl.CostEstimate(flops=0, bytes_accessed=4_000_000, transcendentals=0),
    )()


def store_kernel(
    owner_ref, res_in, norm_in, deliv_ref, app_in, res_hbm, norm_hbm, app_hbm,
    zeros, out_sem, sem,
):
    s = lax.axis_index("seq")
    t = lax.axis_index("tp")

    def blank(r, i):
        return pltpu.make_async_copy(zeros, app_hbm.at[r, pl.ds(i * 2, 2)], out_sem.at[r, i])

    def put(r, i):
        part = pl.ds(i * 2, 2)
        return pltpu.make_async_copy(deliv_ref.at[r, part], app_hbm.at[r, part], out_sem.at[r, i])

    def mine(r):
        return owner_ref[t * REQ + r] == s

    small = (
        pltpu.make_async_copy(res_in, res_hbm, sem.at[0]),
        pltpu.make_async_copy(norm_in, norm_hbm, sem.at[1]),
    )
    for copy in small:
        copy.start()
    @pl.when(jnp.logical_not(starts_early()))
    def _():
        zeros[...] = jnp.zeros_like(zeros)

    for r in range(REQ):
        @pl.when(mine(r))
        def _():
            for i in range(4):
                put(r, i).start()

    for r in range(REQ):
        @pl.when(jnp.logical_not(mine(r) | starts_early()))
        def _():
            for i in range(4):
                blank(r, i).start()

    for copy in small:
        copy.wait()
    for r in range(REQ):
        @pl.when(mine(r) | jnp.logical_not(starts_early()))
        def _():
            for i in range(4):
                put(r, i).wait()


def store(owner, residual_out, normed, delivered, appended):
    anywhere = pl.BlockSpec(memory_space=pl.ANY)
    vmem = pl.BlockSpec(memory_space=pltpu.VMEM)
    return pl.pallas_call(
        store_kernel,
        out_shape=tuple(jax.ShapeDtypeStruct(v.shape, v.dtype) for v in (residual_out, normed, delivered)),
        in_specs=[pl.BlockSpec(memory_space=pltpu.SMEM)] + [vmem] * 3 + [anywhere],
        out_specs=(anywhere,) * 3,
        scratch_shapes=[
            pltpu.VMEM((2, WIDTH, 256), jnp.bfloat16),
            pltpu.SemaphoreType.DMA((REQ, 4)),
            pltpu.SemaphoreType.DMA((2,)),
        ],
        input_output_aliases={4: 2},
        compiler_params=pltpu.CompilerParams(vmem_limit_bytes=20 * 1024 * 1024),
        cost_estimate=pl.CostEstimate(flops=0, bytes_accessed=6_000_000, transcendentals=0),
    )(
        pltpu.with_memory_space_constraint(owner, pltpu.SMEM),
        *(pltpu.with_memory_space_constraint(v, pltpu.VMEM) for v in (residual_out, normed, delivered)),
        appended,
    )


def per_device(queries, cache_kv, new_kv, ctx_len, new_len, owner, wo, hidden_in, norm_gain):
    appended = blanks()
    residual_out, normed, delivered, owner = step(
        appended, queries, cache_kv, new_kv, ctx_len, new_len, owner, wo, hidden_in, norm_gain
    )
    return store(owner, residual_out, normed, delivered, appended)


def solution(mesh):
    in_specs = (
        P("tp", None, None, None),
        P("tp", None, "seq", None),
        P("tp", None, "seq", None),
        P(),
        P(),
        P(),
        P(("seq", "tp"), None),
        P(None, ("seq", "tp")),
        P(("seq", "tp")),
    )
    out_specs = (P(None, ("seq", "tp")), P(None, ("seq", "tp")), P("tp", None, "seq", None))
    return jax.shard_map(
        per_device, mesh=mesh, in_specs=in_specs, out_specs=out_specs, check_vma=False
    )
```

```python
import functools

import jax
import jax.numpy as jnp
from jax import lax
from jax.experimental import pallas as pl
from jax.experimental.pallas import tpu as pltpu
from jax.sharding import PartitionSpec as P

D = 16384
HD = 128
KVH = 8
GROUP = 16
REQ = 4
WIDTH = 256
SHARE = 32
KEYS = WIDTH + SHARE
NEG = -1e30
LOG2E = 1.4426950408889634
MESH = pl.DeviceIdType.MESH


def remote(src, dst, send, recv, device):
    return pltpu.make_async_remote_copy(
        src_ref=src, dst_ref=dst, send_sem=send, recv_sem=recv, device_id=device, device_id_type=MESH
    )


def kernel(
    after_hbm, owner_hbm, ctx_hbm, new_hbm, q_hbm, cache_hbm, newkv_hbm, wo_hbm, hidden_hbm, gain_hbm,
    res_ref, norm_ref, got, owner_out,
    ctx_s, new_s, q_v, kv, w_v, hid_v, gain_v,
    osend, orecv, csend, crecv,
    a_send, b_send, e_send, a_recv, b_recv, e_recv, a2_send, b2_send, e2_send, a2_recv, b2_recv, e2_recv,
    n_send, n_recv, rows_v,
    loc_sem, kv_sem, wl_sem, ws_sem, wr_sem,
    os_sem, or_sem, cs_sem, cr_sem,
    r1s_sem, r1r_sem, e1s_sem, e1r_sem, r2s_sem, r2r_sem, ns_sem, nr_sem,
    gs_sem, gr_sem, ps_sem, pr_sem,
):
    s = lax.axis_index("seq")
    t = lax.axis_index("tp")
    y, c = s // 2, s % 2
    x, z = t // 4, t % 4
    me = s * 16 + t
    sp = y * 2 + (1 - c)

    def seq_peer(i):
        return (s + 1 + i) & 7

    def tp_peer(i):
        return ((x + 2 - (i & 3)) & 3) * 4 + ((z + 2 - (i >> 2)) & 3)

    def any_peer(i):
        far = (y + 2 - ((i >> 5) & 3)) & 3
        core = c ^ (1 - (i & 1))
        return far * 2 + core, ((x + 2 - ((i >> 1) & 3)) & 3) * 4 + ((z + 2 - ((i >> 3) & 3)) & 3)

    def y_at(d):
        return lax.rem(y + d, 4) * 2 + c

    def x_at(d):
        return lax.rem(x + d, 4) * 4 + z

    def z_at(d):
        return x * 4 + lax.rem(z + d, 4)

    drains = []

    def others(count, own, send):
        lax.fori_loop(0, own, send, 0)
        lax.fori_loop(own + 1, count, send, 0)

    barrier = pltpu.get_barrier_semaphore()

    def greet(device):
        pl.semaphore_signal(barrier, inc=1, device_id=device, device_id_type=MESH)

    def greet_tp(i, _):
        greet((sp, tp_peer(i)))
        greet((s, tp_peer(i)))
        return 0

    def greet_seq(i, _):
        greet((seq_peer(i), t))
        return 0

    others(16, 10, greet_tp)
    lax.fori_loop(0, 7, greet_seq, 0)

    loads = [
        pltpu.make_async_copy(src, dst, loc_sem.at[i])
        for i, (src, dst) in enumerate(
            [(ctx_hbm, ctx_s), (new_hbm, new_s), (q_hbm, q_v), (hidden_hbm, hid_v), (gain_hbm, gain_v),
             (owner_hbm, owner_out)]
        )
    ]

    def kv_copies(r):
        return (
            pltpu.make_async_copy(cache_hbm.at[r], kv.at[r, :, pl.ds(0, WIDTH), :], kv_sem.at[r, 0]),
            pltpu.make_async_copy(newkv_hbm.at[r], kv.at[r, :, pl.ds(WIDTH, SHARE), :], kv_sem.at[r, 1]),
        )

    for load in loads[:3]:
        load.start()
    for r in range(2):
        for copy in kv_copies(r):
            copy.start()

    for r in range(2, REQ):
        for copy in kv_copies(r):
            copy.start()
    for load in loads[3:]:
        load.start()

    def w_local(j):
        return pltpu.make_async_copy(
            wo_hbm.at[:, pl.ds(pl.multiple_of(j * 4096 + c * 2048, 2048), 2048)],
            w_v.at[j, pl.ds(pl.multiple_of(c * 128, 128), 128), :],
            wl_sem.at[j],
        )

    def w_remote(j):
        return remote(
            wo_hbm.at[:, pl.ds(pl.multiple_of(j * 4096 + (1 - c) * 2048, 2048), 2048)],
            w_v.at[j, pl.ds(pl.multiple_of(c * 128, 128), 128), :],
            ws_sem.at[j], wr_sem.at[j], (sp, t),
        )

    for j in range(4):
        w_local(j).start()

    def block(r, who):
        return got.at[r, :, pl.ds(pl.multiple_of(who * SHARE, SHARE), SHARE), :]

    def request(way, n):
        return n if way == 0 else REQ - 1 - n

    def source(way):
        return y_at(3 if way == 0 else 1)

    def ring(way, n, slot, who):
        here = block(request(way, n), who)
        return remote(
            here, here, gs_sem.at[way, slot], gr_sem.at[way, slot], (y_at(1 if way == 0 else 3), t)
        )

    def first(way, n):
        return ring(way, n, n, s)

    def second(way, n):
        return ring(way, n, REQ + n, source(way))

    def pair(way, n, slot, who):
        here = block(request(way, n), who)
        return remote(here, here, ps_sem.at[way, slot], pr_sem.at[way, slot], (sp, t))

    def pair_own(n):
        return pair(0, n, n, s)

    def pair_near(way, n):
        return pair(way, n, REQ + n, source(way))

    def pair_far(way, n):
        return pair(way, n, 2 * REQ + n, y_at(2))

    def start_first(*steps):
        for n in steps:
            for way in range(2):
                first(way, n).start()

    def start_second(*steps):
        for n in steps:
            for way in range(2):
                first(way, n).wait_recv()
                second(way, n).start()
                pair_near(way, n).start()

    def start_near(*steps):
        for n in steps:
            for way in range(2):
                first(way, n).wait_recv()
                pair_near(way, n).start()

    def start_far():
        for n in range(2):
            for way in range(2):
                second(way, n).wait_recv()
                pair_far(way, n).start()

    col = lax.broadcasted_iota(jnp.int32, (1, KEYS), 1)
    lane = lax.broadcasted_iota(jnp.int32, (KVH * GROUP, 128), 1)

    def attend(pair_of, stats):
        scores = []
        for r in pair_of:
            kv_copies(r)[0].wait()
        for r in pair_of:
            live_ctx = jnp.minimum(ctx_s[t * REQ + r] - s * WIDTH, WIDTH)
            live_new = new_s[t * REQ + r] - s * SHARE + WIDTH
            bias = jnp.where((col < live_ctx) | ((col >= WIDTH) & (col < live_new)), 0.0, NEG)
            for h in range(KVH):
                scores.append(
                    lax.dot_general(
                        q_v[r, h], kv[r, h, :, :HD], (((1,), (1,)), ((), ())), preferred_element_type=jnp.float32
                    )
                    + bias
                )
        scores = jnp.concatenate(scores, axis=0)
        top = jnp.maximum(jnp.max(scores, axis=1, keepdims=True), 0.1 * NEG)
        weights = jnp.exp2((scores - top) * (HD ** (-0.5) * LOG2E))
        total = jnp.maximum(jnp.sum(weights, axis=1, keepdims=True), 1e-30)
        weights = weights.astype(jnp.bfloat16)
        out = jnp.concatenate(
            [
                jnp.dot(
                    weights[(i * KVH + h) * GROUP:(i * KVH + h + 1) * GROUP],
                    kv[r, h, :, HD:],
                    preferred_element_type=jnp.float32,
                )
                for i, r in enumerate(pair_of)
                for h in range(KVH)
            ],
            axis=0,
        )
        out = (out * (1.0 / total)).astype(jnp.bfloat16)
        log_total = top * HD ** (-0.5) + jnp.log(total)
        for i, r in enumerate(pair_of):
            for h in range(KVH):
                first_row = (i * KVH + h) * GROUP
                osend[h, r * GROUP:(r + 1) * GROUP, :] = out[first_row:first_row + GROUP]
            stats = jnp.where(lane == r, log_total[i * KVH * GROUP:(i + 1) * KVH * GROUP], stats)
        return stats

    def rows_of(part):
        return pl.ds(0, 32) if part == 0 else pl.ds(32, 48)

    def o_copy(k, part):
        return remote(
            osend.at[k, rows_of(part)], orecv.at[s, rows_of(part)], os_sem.at[part], or_sem.at[part], (k, t)
        )

    def o_own(part):
        return pltpu.make_async_copy(
            osend.at[s, rows_of(part)], orecv.at[s, rows_of(part)], or_sem.at[part]
        )

    def send_o(part):
        o_own(part).start()

        def one(i, _):
            o_copy(seq_peer(i), part).start()
            return 0

        for i in range(7):
            one(i, 0)

    def wait_o(part):
        everything = orecv.at[:, rows_of(part)]
        pltpu.make_async_copy(everything, everything, or_sem.at[part]).wait()

    def drain_o():
        for part in range(2):
            sent = osend.at[pl.ds(0, 7), rows_of(part)]
            pltpu.make_async_copy(sent, sent, os_sem.at[part]).wait()

    for load in loads[:3]:
        load.wait()
    stats = jnp.zeros((KVH * GROUP, 128), jnp.float32)
    for r in range(2):
        kv_copies(r)[1].wait()
    stats = attend((0, 1), stats)
    slot = lax.broadcasted_iota(jnp.int32, (SHARE, 256), 0)
    for r in range(2, REQ):
        kv_copies(r)[1].wait()
    for r in range(REQ):
        live = slot < new_s[t * REQ + r] - s * SHARE
        for h in range(KVH):
            got[r, h, pl.ds(pl.multiple_of(s * SHARE, SHARE), SHARE), :] = jnp.where(
                live, kv[r, h, WIDTH:, :], jnp.zeros((), jnp.bfloat16)
            )

    pl.semaphore_wait(barrier, 37)
    drains.append(drain_o)
    send_o(0)
    for j in range(4):
        w_remote(j).start()
    stats = attend((2, 3), stats)
    high = stats.astype(jnp.bfloat16).astype(jnp.float32)
    middle = (stats - high).astype(jnp.bfloat16).astype(jnp.float32)
    low = stats - high - middle
    pieces = (high + pltpu.roll(middle, 4, 1) + pltpu.roll(low, 8, 1)).astype(jnp.bfloat16)
    for h in range(KVH):
        osend[h, 64:80, :] = pieces[h * GROUP:(h + 1) * GROUP]
    send_o(1)

    start_first(0, 1, 2)
    for n in range(REQ):
        pair_own(n).start()

    def drain_gather():
        for n in range(REQ):
            pair_own(n).wait()
            for way in range(2):
                first(way, n).wait_send()
                pair_near(way, n).wait()
                if n < 2:
                    second(way, n).wait_send()
                    pair_far(way, n).wait()

    def drain_w():
        for j in range(4):
            w_remote(j).wait_send()

    drains.append(drain_gather)
    drains.append(drain_w)

    wait_o(0)
    wait_o(1)

    tops = []
    for k in range(8):
        piece = orecv[k, 64:80, :].astype(jnp.float32)
        tops.append(piece + pltpu.roll(piece, 124, 1) + pltpu.roll(piece, 120, 1))
    top = functools.reduce(jnp.maximum, tops)
    exps = [jnp.exp(v - top) for v in tops]
    total = functools.reduce(jnp.add, exps)
    shares = [e / total for e in exps]
    for r in range(REQ):
        context = jnp.zeros((GROUP, HD), jnp.float32)
        for k in range(8):
            part = orecv[k, r * GROUP:(r + 1) * GROUP, :].astype(jnp.float32)
            context = context + part * shares[k][:, r:r + 1]
        csend[:, r, :] = context

    def c_copy(core, g):
        return remote(
            csend.at[g], crecv.at[c, t], cs_sem.at[0], cr_sem.at[0], (y * 2 + core, g)
        )

    def send_c(i, _):
        g = tp_peer(i)
        c_copy(c, g).start()
        c_copy(1 - c, g).start()
        return 0

    def drain_c():
        for sent in (csend, csend.at[pl.ds(0, 15)]):
            pltpu.make_async_copy(sent, sent, cs_sem.at[0]).wait()

    drains.append(drain_c)
    for i in range(16):
        if i != 10:
            send_c(i, 0)
    c_copy(1 - c, t).start()
    pltpu.make_async_copy(csend.at[t], crecv.at[c, t], cr_sem.at[0]).start()
    for j in range(4):
        w_local(j).wait()
        w_remote(j).wait_recv()
    pltpu.make_async_copy(crecv, crecv, cr_sem.at[0]).wait()

    flat = jnp.concatenate(
        [
            jnp.concatenate([crecv[core, :, r, :] for r in range(REQ)], axis=0)
            for core in range(2)
        ],
        axis=1,
    ).astype(jnp.bfloat16)

    def r1_copy(way, d, part):
        dst = ((x if way == 0 else z) + d) & 3
        src = (a_send if way == 0 else b_send).at[dst, part]
        to = (a_recv if way == 0 else b_recv).at[d - 1, part]
        return remote(
            src, to, r1s_sem.at[way, d - 1, part], r1r_sem.at[way, d - 1, part],
            (s, x_at(d) if way == 0 else z_at(d)),
        )

    def e1_copy(d):
        return remote(
            e_send.at[(y + d) & 3], e_recv.at[d - 1], e1s_sem.at[d - 1], e1r_sem.at[d - 1], (y_at(d), t)
        )

    def project(j):
        for i in range(4):
            piece = jnp.dot(flat, w_v[j, :, i * 512:(i + 1) * 512], preferred_element_type=jnp.float32)
            a_send[i, j] = piece[:24].astype(jnp.bfloat16)
            middle = piece[24:48].astype(jnp.bfloat16)
            for k in range(4):
                b_send[k, j, :, i * 128:(i + 1) * 128] = middle[:, k * 128:(k + 1) * 128]
            e_send[j, :, i * 512:(i + 1) * 512] = piece[48:].astype(jnp.bfloat16)

    def drain_r1():
        for d in range(1, 4):
            e1_copy(d).wait_send()
            for way in range(2):
                for part in range(4):
                    r1_copy(way, d, part).wait_send()

    drains.append(drain_r1)
    turns = (2, 1, 3, 0)
    for turn in turns:
        part = (y + turn) & 3
        project(part)
        if turn:
            e1_copy(turn).start()
        for d in (2, 1, 3):
            for way in range(2):
                r1_copy(way, d, part).start()

    start_first(3)
    def r2_copy(way, j, k):
        send, recv = ((a2_send, a2_recv), (b2_send, b2_recv), (e2_send, e2_recv))[way]
        if way == 2:
            slot, device = (x, z), (s, j * 4 + k)
        else:
            slot = (y, z if way == 0 else x)
            device = (j * 2 + c, x * 4 + k if way == 0 else k * 4 + z)
        return remote(send.at[j, k], recv.at[slot], r2s_sem.at[way], r2r_sem.at[way], device)

    def send_r2(way, dj, dk):
        send, recv = ((a2_send, a2_recv), (b2_send, b2_recv), (e2_send, e2_recv))[way]
        mine = ((y, z), (y, x), (x, z))[way]
        j, k = (mine[0] + dj) & 3, (mine[1] + dk) & 3
        if dj or dk:
            r2_copy(way, j, k).start()
        else:
            pltpu.make_async_copy(send.at[j, k], recv.at[j, k], r2r_sem.at[way]).start()

    def drain_r2():
        for way in range(3):
            send = (a2_send, b2_send, e2_send)[way]
            for sent in (send.at[pl.ds(0, 3)], send.at[0, pl.ds(0, 3)]):
                pltpu.make_async_copy(sent, sent, r2s_sem.at[way]).wait()

    def add_e():
        for d in (1, 3, 2):
            e1_copy(d).wait_recv()
        for j in (2, 1, 3, 0):
            cols = slice(j * 512, (j + 1) * 512)
            out = e_send[y, :, cols].astype(jnp.float32)
            for d in range(3):
                out = out + e_recv[d, :, cols].astype(jnp.float32)
            out = out.astype(jnp.bfloat16)
            for k in range(4):
                e2_send[j, k] = out[:, k * 128:(k + 1) * 128]
        for dj in (2, 1, 3, 0):
            for dk in (2, 1, 3, 0):
                send_r2(2, dj, dk)

    drains.append(drain_r2)
    for turn in turns:
        part = (y + turn) & 3
        for way in range(2):
            for d in (1, 3, 2):
                r1_copy(way, d, part).wait_recv()
            send, recv, nxt = ((a_send, a_recv, a2_send), (b_send, b_recv, b2_send))[way]
            out = send[x if way == 0 else z, part].astype(jnp.float32)
            for d in range(3):
                out = out + recv[d, part].astype(jnp.float32)
            out = out.astype(jnp.bfloat16)
            for k in range(4):
                nxt[part, k] = out[:, k * 128:(k + 1) * 128]
            for dk in (2, 1, 3, 0):
                send_r2(way, turn, dk)
        if turn == 3:
            add_e()
            start_second(0, 1)


    for load in loads[3:]:
        load.wait()
    rows_v[...] = hid_v[...].astype(jnp.float32)
    stream = jnp.concatenate([rows_v[pl.ds(r, 16, stride=REQ), :] for r in range(REQ)], axis=0)
    start_near(2, 3)
    sums = []
    for way in range(3):
        recv = (a2_recv, b2_recv, e2_recv)[way]
        pltpu.make_async_copy(recv, recv, r2r_sem.at[way]).wait()
        out = recv[0, 0].astype(jnp.float32)
        for i in range(1, 16):
            out = out + recv[i // 4, i % 4].astype(jnp.float32)
        sums.append(out)
    stream = stream + jnp.concatenate(sums, axis=0)

    squares = stream * stream
    n_send[...] = jnp.sum(jnp.concatenate([squares, squares], axis=0).T, axis=0, keepdims=True)

    def send_n(i, _):
        pltpu.make_async_remote_copy(
            src_ref=n_send, dst_ref=n_recv.at[me], send_sem=ns_sem.at[0], recv_sem=nr_sem.at[0],
            device_id=any_peer(i), device_id_type=MESH,
        ).start()
        return 0

    def drain_n():
        sent = n_recv.at[pl.ds(0, 127)]
        pltpu.make_async_copy(sent, sent, ns_sem.at[0]).wait()

    others(128, 85, send_n)
    pltpu.make_async_copy(n_send, n_recv.at[me], nr_sem.at[0]).start()
    for r in range(REQ):
        rows_v[pl.ds(r, 16, stride=REQ), :] = stream[r * 16:(r + 1) * 16]
    res_ref[...] = rows_v[...].astype(jnp.bfloat16)

    start_far()
    scaled = stream * gain_v[...]
    for drain in drains:
        drain()
    pltpu.make_async_copy(n_recv, n_recv, nr_sem.at[0]).wait()
    scale = lax.rsqrt(jnp.sum(n_recv[...], axis=0) / D + 1e-05)
    scale = jnp.broadcast_to(scale, (128, 128)).T[:64]
    normed = scaled * scale
    for r in range(REQ):
        rows_v[pl.ds(r, 16, stride=REQ), :] = normed[r * 16:(r + 1) * 16]
    norm_ref[...] = rows_v[...].astype(jnp.bfloat16)
    drain_n()


def step(after, queries, cache_kv, new_kv, ctx_len, new_len, owner, wo, hidden_in, norm_gain):
    bf, f32 = jnp.bfloat16, jnp.float32
    dma = pltpu.SemaphoreType.DMA
    anywhere = pl.BlockSpec(memory_space=pl.ANY)
    vmem = pl.BlockSpec(memory_space=pltpu.VMEM)
    V = pltpu.VMEM
    return pl.pallas_call(
        kernel,
        out_shape=(
            V((64, 128), bf),
            V((64, 128), bf),
            V((REQ, KVH, WIDTH, 256), bf),
            pltpu.SMEM((64,), jnp.int32),
        ),
        in_specs=[anywhere] * 10,
        out_specs=(vmem, vmem, vmem, pl.BlockSpec(memory_space=pltpu.SMEM)),
        scratch_shapes=[
            pltpu.SMEM((64,), jnp.int32), pltpu.SMEM((64,), jnp.int32),
            V((REQ, KVH, GROUP, HD), bf),
            V((REQ, KVH, KEYS, 256), bf),
            V((4, 256, 2048), bf),
            V((64, 128), bf),
            V((1, 128), f32),
            V((8, 80, HD), bf), V((8, 80, HD), bf),
            V((16, REQ, HD), f32), V((2, 16, REQ, HD), f32),
            V((4, 4, 24, 512), bf), V((4, 4, 24, 512), bf), V((4, 16, 2048), bf),
            V((3, 4, 24, 512), bf), V((3, 4, 24, 512), bf), V((3, 16, 2048), bf),
            V((4, 4, 24, 128), bf), V((4, 4, 24, 128), bf), V((4, 4, 16, 128), bf),
            V((4, 4, 24, 128), bf), V((4, 4, 24, 128), bf), V((4, 4, 16, 128), bf),
            V((1, 128), f32), V((128, 1, 128), f32),
            V((64, 128), f32),
            dma((6,)), dma((REQ, 2)), dma((4,)), dma((4,)), dma((4,)),
            dma((2,)), dma((2,)), dma((1,)), dma((1,)),
            dma((2, 3, 4)), dma((2, 3, 4)), dma((3,)), dma((3,)), dma((3,)), dma((3,)), dma((1,)), dma((1,)),
            dma((2, 6)), dma((2, 6)), dma((2, 10)), dma((2, 10)),
        ],
        compiler_params=pltpu.CompilerParams(
            collective_id=0, has_side_effects=True, vmem_limit_bytes=40 * 1024 * 1024
        ),
        cost_estimate=pl.CostEstimate(flops=600_000_000, bytes_accessed=14_000_000, transcendentals=1_000_000),
    )(
        *(
            pltpu.with_memory_space_constraint(v, pltpu.HBM)
            for v in (after, owner, ctx_len, new_len, queries, cache_kv, new_kv, wo, hidden_in, norm_gain.reshape(1, 128))
        )
    )


def starts_early():
    return (lax.axis_index("tp") & 3) == 0


def blank_kernel(app_hbm, zeros, sem):
    def blank(r, i):
        return pltpu.make_async_copy(zeros, app_hbm.at[r, pl.ds(i * 2, 2)], sem.at[r, i])

    @pl.when(starts_early())
    def _():
        zeros[...] = jnp.zeros_like(zeros)
        for r in range(REQ):
            for i in range(4):
                blank(r, i).start()
        for r in range(REQ):
            for i in range(4):
                blank(r, i).wait()


def blanks():
    return pl.pallas_call(
        blank_kernel,
        out_shape=pltpu.HBM((REQ, KVH, WIDTH, 256), jnp.bfloat16),
        out_specs=pl.BlockSpec(memory_space=pl.ANY),
        scratch_shapes=[pltpu.VMEM((2, WIDTH, 256), jnp.bfloat16), pltpu.SemaphoreType.DMA((REQ, 4))],
        compiler_params=pltpu.CompilerParams(vmem_limit_bytes=20 * 1024 * 1024),
        cost_estimate=pl.CostEstimate(flops=0, bytes_accessed=4_000_000, transcendentals=0),
    )()


def store_kernel(
    owner_ref, res_in, norm_in, deliv_ref, app_in, res_hbm, norm_hbm, app_hbm,
    zeros, out_sem, sem,
):
    s = lax.axis_index("seq")
    t = lax.axis_index("tp")

    def blank(r, i):
        return pltpu.make_async_copy(zeros, app_hbm.at[r, pl.ds(i * 2, 2)], out_sem.at[r, i])

    def put(r, i):
        part = pl.ds(i * 2, 2)
        return pltpu.make_async_copy(deliv_ref.at[r, part], app_hbm.at[r, part], out_sem.at[r, i])

    def mine(r):
        return owner_ref[t * REQ + r] == s

    small = (
        pltpu.make_async_copy(res_in, res_hbm, sem.at[0]),
        pltpu.make_async_copy(norm_in, norm_hbm, sem.at[1]),
    )
    for copy in small:
        copy.start()
    @pl.when(jnp.logical_not(starts_early()))
    def _():
        zeros[...] = jnp.zeros_like(zeros)

    for r in range(REQ):
        @pl.when(mine(r))
        def _():
            for i in range(4):
                put(r, i).start()

    for r in range(REQ):
        @pl.when(jnp.logical_not(mine(r) | starts_early()))
        def _():
            for i in range(4):
                blank(r, i).start()

    for copy in small:
        copy.wait()
    for r in range(REQ):
        @pl.when(mine(r) | jnp.logical_not(starts_early()))
        def _():
            for i in range(4):
                put(r, i).wait()


def store(owner, residual_out, normed, delivered, appended):
    anywhere = pl.BlockSpec(memory_space=pl.ANY)
    vmem = pl.BlockSpec(memory_space=pltpu.VMEM)
    return pl.pallas_call(
        store_kernel,
        out_shape=tuple(jax.ShapeDtypeStruct(v.shape, v.dtype) for v in (residual_out, normed, delivered)),
        in_specs=[pl.BlockSpec(memory_space=pltpu.SMEM)] + [vmem] * 3 + [anywhere],
        out_specs=(anywhere,) * 3,
        scratch_shapes=[
            pltpu.VMEM((2, WIDTH, 256), jnp.bfloat16),
            pltpu.SemaphoreType.DMA((REQ, 4)),
            pltpu.SemaphoreType.DMA((2,)),
        ],
        input_output_aliases={4: 2},
        compiler_params=pltpu.CompilerParams(vmem_limit_bytes=20 * 1024 * 1024),
        cost_estimate=pl.CostEstimate(flops=0, bytes_accessed=6_000_000, transcendentals=0),
    )(
        pltpu.with_memory_space_constraint(owner, pltpu.SMEM),
        *(pltpu.with_memory_space_constraint(v, pltpu.VMEM) for v in (residual_out, normed, delivered)),
        appended,
    )


def per_device(queries, cache_kv, new_kv, ctx_len, new_len, owner, wo, hidden_in, norm_gain):
    appended = blanks()
    residual_out, normed, delivered, owner = step(
        appended, queries, cache_kv, new_kv, ctx_len, new_len, owner, wo, hidden_in, norm_gain
    )
    return store(owner, residual_out, normed, delivered, appended)


def solution(mesh):
    in_specs = (
        P("tp", None, None, None),
        P("tp", None, "seq", None),
        P("tp", None, "seq", None),
        P(),
        P(),
        P(),
        P(("seq", "tp"), None),
        P(None, ("seq", "tp")),
        P(("seq", "tp")),
    )
    out_specs = (P(None, ("seq", "tp")), P(None, ("seq", "tp")), P("tp", None, "seq", None))
    return jax.shard_map(
        per_device, mesh=mesh, in_specs=in_specs, out_specs=out_specs, check_vma=False
    )
```
